32 devices in a mesh: ch: 8 (over z, y), grp: 4 (over x, core).
Axes of the slice: x: 2, y: 2, z: 4, core: 2. Of those that a mesh axis runs over, the one named last changes fastest.
Arguments:
- raw: bfloat16 [4, 1024, 128], P('grp', 'ch'), may hold values from -400 to 400
- order: int32 [8, 16], P('ch'), may hold values from 0 to 15, each once within a row
- pair_blocks: int32 [8, 3], P('ch'), may hold values from -1 to 0, as said below
Outputs:
- corr: bfloat16 [128, 3, 128, 256], P(('ch', 'grp'))
The draws below stay inside these ranges and needn't reach their ends.
Inputs may be any that keep to these rules, and one draw needn't show every extreme that they name: `pair_blocks`: row i names distinct blocks among i * 16 // 128 - 1, i * 16 // 128, i * 16 // 128 + 1 that lie in 0 .. 0; slot 0 is always i * 16 // 128; live slots come first and empty ones hold -1.
All inputs are finite; a program needn't handle non-finite values.
Results may differ from the reference program's by a relative error of at most 0.013.
Values may be sent and summed in bfloat16 or wider, within the bound.
No kernel may reach another device: no remote copies, remote signals or barrier semaphores. Data moves between devices by JAX's collectives and lax.ppermute only.
A program may use at most 128 MiB of HBM per device.

```python
import math
import jax
import jax.numpy as jnp
from jax import lax

CH_DEV = 16
SRC = 128
SEG = 256
LAGS = 256
SMOOTH = 8
MAXP = 3
NSEG = 4
WINDOWS = 4
CHANNELS = 128
NBLK = 1


def draw_raw(key, part):
    key_noise, key_chan, key_seg = jax.random.split(key, 3)
    full_shape = (WINDOWS, NSEG, SEG, CHANNELS)
    noise = jax.random.truncated_normal(key_noise, -6.0, 6.0, full_shape, jnp.float32)
    chan_scale = jnp.exp(jax.random.uniform(key_chan, (1, 1, 1, CHANNELS), jnp.float32, 0.0, math.log(10.0)))
    seg_scale = jnp.exp(jax.random.uniform(key_seg, (WINDOWS, NSEG, 1, 1), jnp.float32, 0.0, math.log(3.0)))
    values = noise * chan_scale * seg_scale
    return values.reshape(WINDOWS, NSEG * SEG, CHANNELS).astype(jnp.bfloat16)


def draw_pair_blocks(key, part):
    block_rows = CHANNELS // CH_DEV
    key_extra, key_swap = jax.random.split(key, 2)
    rows = jnp.arange(block_rows, dtype=jnp.int32)
    own_block = rows * CH_DEV // SRC
    extra = jax.random.randint(key_extra, (block_rows,), 0, 4, dtype=jnp.int32)
    swapped = jax.random.randint(key_swap, (block_rows,), 0, 2, dtype=jnp.int32)
    left_block = own_block - 1
    right_block = own_block + 1
    has_left = (extra % 2 == 1) & (left_block >= 0)
    has_right = (extra // 2 == 1) & (right_block < NBLK)
    left_first = has_left & (~has_right | (swapped == 0))
    second_slot = jnp.where(left_first, left_block, jnp.where(has_right, right_block, -1))
    third_slot = jnp.where(has_left & has_right, jnp.where(swapped == 0, right_block, left_block), -1)
    return jnp.stack([own_block, second_slot, third_slot], axis=1).astype(jnp.int32)


def setup_inputs(seed: int = 0) -> dict:
    seeds = jax.random.split(jax.random.key(seed), 4)
    raw = draw_raw(jax.random.fold_in(seeds[3], 71), 0)
    order = jax.vmap(lambda own: jax.random.permutation(own, CH_DEV))(jax.random.split(seeds[1], (CHANNELS // CH_DEV))).reshape((CHANNELS // CH_DEV, CH_DEV)).astype(jnp.int32)
    pair_blocks = draw_pair_blocks(jax.random.fold_in(seeds[3], 71), 0)
    return dict(raw=raw, order=order, pair_blocks=pair_blocks)


lag_scale = 1.0 / 16.0

def transform_tables(half_len, lag_count, smooth_half):
    samples = jnp.arange(half_len, dtype=jnp.int32)
    column = jnp.arange(2 * half_len, dtype=jnp.int32)
    freq = column % half_len + 1
    phase_fwd = samples[:, None] * freq[None, :] % (2 * half_len)
    angle_fwd = phase_fwd.astype(jnp.float32) * (math.pi / half_len)
    forward = jnp.where(column[None, :] < half_len, jnp.cos(angle_fwd), -jnp.sin(angle_fwd)).astype(jnp.bfloat16)
    lag_steps = jnp.arange(lag_count, dtype=jnp.int32) - lag_count // 2
    phase_inv = freq[:, None] * lag_steps[None, :] % (2 * half_len)
    angle_inv = phase_inv.astype(jnp.float32) * (math.pi / half_len)
    inverse = (jnp.where(column[:, None] < half_len, jnp.cos(angle_inv), -jnp.sin(angle_inv)) * lag_scale).astype(jnp.bfloat16)
    bins = jnp.arange(half_len, dtype=jnp.int32)
    smoothing = (jnp.abs(bins[:, None] - bins[None, :]) <= smooth_half).astype(jnp.float32) / (2 * smooth_half + 1)
    return (forward, inverse, smoothing)

def whiten(segments, forward, smoothing):
    half_len = segments.shape[-1]
    flat_rows = segments.reshape(-1, half_len)
    spectrum = jnp.dot(flat_rows, forward, preferred_element_type=jnp.float32)
    real_part = spectrum[:, :half_len]
    imag_part = spectrum[:, half_len:]
    power_bins = real_part * real_part + imag_part * imag_part
    smoothed = jnp.dot(power_bins, smoothing, precision=lax.Precision.HIGHEST)
    water_level = lax.optimization_barrier(jnp.mean(power_bins, axis=1, keepdims=True))
    divisor = jnp.sqrt(smoothed + 0.1 * water_level + 1e-06)
    whitened = spectrum / jnp.concatenate([divisor, divisor], axis=1)
    return whitened.astype(jnp.bfloat16).reshape(segments.shape[:-1] + (2 * half_len,))

def correlate(receivers, sources, inverse):
    half_len = receivers.shape[-1] // 2
    seg_count = receivers.shape[1]
    recv_re = receivers[..., :half_len].astype(jnp.float32)
    recv_im = receivers[..., half_len:].astype(jnp.float32)
    left_first = jnp.concatenate([recv_re, recv_im], axis=1)
    left_second = jnp.concatenate([recv_im, -recv_re], axis=1)
    right_both = jnp.concatenate([sources[..., :half_len], sources[..., half_len:]], axis=1).astype(jnp.float32)
    cross_re = jnp.einsum('rnk,snk->rsk', left_first, right_both)
    cross_im = jnp.einsum('rnk,snk->rsk', left_second, right_both)
    cross_spec = (jnp.concatenate([cross_re, cross_im], axis=2) * (1.0 / seg_count)).astype(jnp.bfloat16)
    recv_count = receivers.shape[0]
    src_count = sources.shape[0]
    lag_values = jnp.dot(cross_spec.reshape(-1, 2 * half_len), inverse, preferred_element_type=jnp.float32)
    return lag_values.reshape(recv_count, src_count, inverse.shape[1])

def reference(raw, order, pair_blocks):
    forward, inverse, smoothing = transform_tables(SEG, LAGS, SMOOTH)
    block_count = CHANNELS // CH_DEV
    destination = (jnp.arange(block_count, dtype=jnp.int32)[:, None] * CH_DEV + order).reshape(-1).astype(jnp.int32)
    series = jnp.zeros(raw.shape, raw.dtype).at[:, :, destination].set(raw)
    series = jnp.transpose(series, (0, 2, 1)).reshape(WINDOWS, CHANNELS, NSEG, SEG)
    whitened = whiten(series, forward, smoothing)

    def one_device(device_index):
        receivers = lax.dynamic_slice_in_dim(whitened, (device_index * CH_DEV).astype(jnp.int32), CH_DEV, 1)
        slot_results = []
        for slot_index in range(MAXP):
            block_id = pair_blocks[device_index, slot_index]
            is_live = (block_id >= 0).astype(jnp.float32)
            source_start = (jnp.maximum(block_id, 0) * SRC).astype(jnp.int32)
            sources = lax.dynamic_slice_in_dim(whitened, source_start, SRC, 1)
            total = jnp.zeros((CH_DEV, SRC, LAGS), jnp.float32)
            for window_index in range(WINDOWS):
                lag_values = correlate(receivers[window_index], sources[window_index], inverse)
                total = total + (lag_values * is_live).astype(jnp.bfloat16).astype(jnp.float32)
            slot_results.append(total)
        stacked = jnp.stack(slot_results, axis=1)
        return (stacked / WINDOWS).astype(jnp.bfloat16)
    result = lax.map(one_device, jnp.arange(block_count, dtype=jnp.int32))
    return result.reshape(CHANNELS, MAXP, SRC, LAGS)
```

```python
import functools
import math

import jax
import jax.numpy as jnp
import numpy as np
from jax import lax
from jax.experimental import pallas as pl
from jax.experimental.pallas import tpu as pltpu
from jax.sharding import PartitionSpec as P

SRC = 128
SEG = 256
LAGS = 256
SMOOTH = 8
MAXP = 3
REACH = 15


lag_scale = 1.0 / 16.0


def from_behind(value, axis, steps):
    count = lax.axis_size(axis)
    initial, last = (max(0, -steps), min(count, count - steps))
    return lax.ppermute(value, axis, [(source, source + steps) for source in range(initial, last)])


def transform_tables(half_len, lag_count, smooth_half):
    samples = np.arange(half_len)
    column = np.arange(2 * half_len)
    freq = column % half_len + 1
    angle_fwd = (samples[:, None] * freq[None, :] % (2 * half_len)) * (math.pi / half_len)
    forward = np.where(column[None, :] < half_len, np.cos(angle_fwd), -np.sin(angle_fwd))
    lag_steps = np.arange(lag_count) - lag_count // 2
    angle_inv = (freq[:, None] * lag_steps[None, :] % (2 * half_len)) * (math.pi / half_len)
    inverse = np.where(column[:, None] < half_len, np.cos(angle_inv), -np.sin(angle_inv)) * lag_scale
    bins = np.arange(half_len)
    band = np.abs(bins[:, None] - bins[None, :]) <= smooth_half
    return (
        jnp.asarray(forward.astype(np.float32), jnp.bfloat16),
        jnp.asarray(inverse.astype(np.float32), jnp.bfloat16),
        jnp.asarray(band.astype(np.float32)),
    )


def whiten(segments, forward, band):
    half_len = segments.shape[-1]
    flat_rows = segments.reshape(-1, half_len)
    spectrum = jnp.dot(flat_rows, forward, preferred_element_type=jnp.float32)
    real_part = spectrum[:, :half_len]
    imag_part = spectrum[:, half_len:]
    power_bins = real_part * real_part + imag_part * imag_part
    smoothed = jnp.dot(power_bins, band, precision=lax.Precision.HIGHEST) / (2 * SMOOTH + 1)
    water_level = jnp.mean(power_bins, axis=1, keepdims=True)
    divisor = jnp.sqrt(smoothed + 0.1 * water_level + 1e-06)
    whitened = spectrum / jnp.concatenate([divisor, divisor], axis=1)
    return whitened.astype(jnp.bfloat16).reshape(segments.shape[:-1] + (2 * half_len,))


def correlate(receivers, sources, inverse):
    half_len = receivers.shape[-1] // 2
    seg_count = receivers.shape[1]
    recv_re = receivers[..., :half_len]
    recv_im = receivers[..., half_len:]
    left_first = jnp.concatenate([recv_re, recv_im], axis=1)
    left_second = jnp.concatenate([recv_im, -recv_re], axis=1)
    right_both = jnp.concatenate([sources[..., :half_len], sources[..., half_len:]], axis=1)
    cross_re = jnp.einsum(
        "rnk,snk->rsk", left_first, right_both, preferred_element_type=jnp.float32
    )
    cross_im = jnp.einsum(
        "rnk,snk->rsk", left_second, right_both, preferred_element_type=jnp.float32
    )
    cross_spec = (jnp.concatenate([cross_re, cross_im], axis=2) * (1.0 / seg_count)).astype(
        jnp.bfloat16
    )
    recv_count = receivers.shape[0]
    src_count = sources.shape[0]
    lag_values = jnp.dot(
        cross_spec.reshape(-1, 2 * half_len), inverse, preferred_element_type=jnp.float32
    )
    return lag_values.reshape(recv_count, src_count, inverse.shape[1])


def many_blocks(raw, order, pair_blocks):
    recorded = lax.all_to_all(raw, "ch", split_axis=2, concat_axis=1, tiled=True)
    local_channels = recorded.shape[2]
    onehot = (order[0][:, None] == jnp.arange(local_channels, dtype=jnp.int32)[None, :]).astype(
        jnp.bfloat16
    )
    series = jnp.einsum(
        "ck,tc->kt", onehot, recorded[0], preferred_element_type=jnp.float32
    ).astype(jnp.bfloat16)
    segments = series.reshape(1, local_channels, -1, SEG)
    forward, inverse, band = transform_tables(SEG, LAGS, SMOOTH)
    own_white = whiten(segments, forward, band)
    before_list = []
    for distance in range(REACH, 0, -1):
        before_list.append(from_behind(own_white, "ch", distance))
    after_list = []
    for distance in range(1, REACH + 1):
        after_list.append(from_behind(own_white, "ch", -distance))
    window = jnp.concatenate(before_list + [own_white] + after_list, axis=1)
    window_base = (lax.axis_index("ch") - REACH) * local_channels
    groups = lax.axis_size("grp")
    receivers = own_white[0]
    slot_results = []
    for slot_index in range(MAXP):
        block_id = pair_blocks[0, slot_index]
        source_start = jnp.maximum(block_id, 0) * SRC - window_base
        sources = lax.dynamic_slice_in_dim(window[0], source_start, SRC, 0)
        is_live = (block_id >= 0).astype(jnp.float32)
        lag_values = correlate(receivers, sources, inverse) * is_live
        slot_results.append(lag_values)
    stacked = lax.psum_scatter(
        jnp.stack(slot_results, axis=1).astype(jnp.bfloat16), "grp", scatter_dimension=0, tiled=True
    ).astype(jnp.float32)
    return (stacked / groups).astype(jnp.bfloat16)


RECV = 4
NTILE = SRC // 8


def correlate_kernel(
    info, own, rest, own_sib, rest_sib, forward, band, inverse, out, fwd, white, recv, cross
):
    half = forward.shape[0] // 2
    bins = band.shape[0]
    zb = own.shape[0]
    base = info[0]
    mine = info[1]
    live = info[2]

    fwd[0:half, :] = forward[pl.ds(pl.multiple_of(mine * half, half), half), :]
    fwd[half:, :] = forward[pl.ds(pl.multiple_of((1 - mine) * half, half), half), :]
    out[:, 1:] = jnp.zeros((RECV, MAXP - 1, SRC, LAGS), out.dtype)

    dest = own[0, half : half + 8, :]
    for j in range(1, zb):
        dest = jnp.maximum(dest, own[j, half : half + 8, :])
    for j in range(zb, 2 * zb):
        dest = jnp.maximum(dest, rest[j, half : half + 8, :])
    dest = dest.astype(jnp.float32)[0:1, :]
    rows = lax.broadcasted_iota(jnp.int32, (SRC, SRC), 0).astype(jnp.float32)
    perm = (rows == dest).astype(jnp.bfloat16)

    def whiten_one(near, far, slot):
        samples = jnp.concatenate([near, far], axis=0)
        series = lax.dot_general(
            perm, samples, (((1,), (1,)), ((), ())), preferred_element_type=jnp.float32
        ).astype(jnp.bfloat16)
        spectrum = jnp.dot(series, fwd[...], preferred_element_type=jnp.float32)
        re = spectrum[:, :bins]
        im = spectrum[:, bins:]
        power = re * re + im * im
        smoothed = jnp.dot(
            power.astype(jnp.bfloat16), band[...], preferred_element_type=jnp.float32
        )
        level = jnp.mean(power, axis=1, keepdims=True)
        scale = lax.rsqrt(smoothed * (1.0 / (2 * SMOOTH + 1)) + (0.1 * level + 1e-06))
        wre = (re * scale).astype(jnp.bfloat16).astype(jnp.float32)
        wim = (im * scale).astype(jnp.bfloat16).astype(jnp.float32)
        white[slot, :, :, 0:bins] = wre.reshape(NTILE, 8, bins)
        white[slot, :, :, bins:] = wim.reshape(NTILE, 8, bins)

    for core, (a, b) in enumerate(((own, rest), (own_sib, rest_sib))):

        @pl.loop(0, zb)
        def _(z):
            whiten_one(a[z, 0:half, :], b[zb + z, 0:half, :], core * 2 * zb + z)
            whiten_one(b[z, 0:half, :], b[2 * zb + z, 0:half, :], core * 2 * zb + zb + z)

    count = 4 * zb

    @pl.loop(0, count)
    def _(j):
        for q in range(RECV):
            row = base + q
            line = white[j, row // 8, pl.ds(row % 8, 1), :]
            a = line[:, 0:bins]
            b = line[:, bins:]
            recv[j, 3 * q] = jnp.broadcast_to(a, (8, bins))
            recv[j, 3 * q + 1] = jnp.broadcast_to(b, (8, bins))
            recv[j, 3 * q + 2] = jnp.broadcast_to(a + b, (8, bins))

    @pl.loop(0, NTILE // 2)
    def _(t):
        for k in range(0, bins, 128):
            sums = [jnp.zeros((2, 8, 128), jnp.float32) for _ in range(3 * RECV)]
            for j in range(count):
                c = white[j, pl.ds(2 * t, 2), :, k : k + 128]
                d = white[j, pl.ds(2 * t, 2), :, bins + k : bins + k + 128]
                e = c - d
                for q in range(RECV):
                    sums[3 * q] += recv[j, 3 * q, :, k : k + 128] * c
                    sums[3 * q + 1] += recv[j, 3 * q + 1, :, k : k + 128] * d
                    sums[3 * q + 2] += recv[j, 3 * q + 2, :, k : k + 128] * e
            for q in range(RECV):
                p1, p2, p3 = sums[3 * q : 3 * q + 3]
                re = ((p1 + p2) * (1.0 / count)).reshape(16, 128).astype(jnp.bfloat16)
                im = ((p3 - p1 + p2) * (1.0 / count)).reshape(16, 128).astype(jnp.bfloat16)
                at = pl.ds(pl.multiple_of(16 * t, 16), 16)
                cross[q, at, k : k + 128] = re
                cross[q, at, bins + k : bins + k + 128] = im

    keep = jnp.where(live >= 0, 1.0, 0.0)
    for q in range(RECV):
        lags = jnp.dot(cross[q], inverse[...], preferred_element_type=jnp.float32)
        out[q, 0] = (lags * keep).astype(out.dtype)


def one_block(raw, order, pair_blocks):
    ch = lax.axis_index("ch")
    grp = lax.axis_index("grp")
    groups = lax.axis_size("grp")
    total = lax.axis_size("ch") * groups
    samples, channels = raw.shape[1:]
    held = order.shape[1]

    lanes = jnp.arange(channels, dtype=jnp.int32)
    dest = jnp.where(lanes // held == ch, jnp.tile(order[0], channels // held) + held * ch, 0)
    tail = jnp.broadcast_to(dest.astype(raw.dtype)[None, None, :], (1, 8, channels))
    block = jnp.concatenate([raw, tail], axis=1)

    def swap(value, ch_bits, grp_bits):
        flip = ch_bits * groups + grp_bits
        return lax.ppermute(value, ("ch", "grp"), [(d, d ^ flip) for d in range(total)])

    own = jnp.concatenate([block, swap(block, 4, 0)], axis=0)
    own = jnp.concatenate([own, swap(own, 2, 0)], axis=0)
    own_sib = swap(own, 0, 1)
    rest = jnp.concatenate([swap(own, 0, 2), swap(own, 1, 0), swap(own, 1, 2)], axis=0)
    rest_sib = swap(rest, 0, 1)

    forward, inverse, band = transform_tables(SEG, LAGS, SMOOTH)
    info = jnp.stack([ch * held + grp * RECV, ch % 2, pair_blocks[0, 0]]).astype(jnp.int32)
    count = 4 * own.shape[0]
    vmem = pl.BlockSpec(memory_space=pltpu.VMEM)
    return pl.pallas_call(
        correlate_kernel,
        out_shape=jax.ShapeDtypeStruct((RECV, MAXP, SRC, LAGS), jnp.bfloat16),
        in_specs=[pl.BlockSpec(memory_space=pltpu.SMEM)] + [vmem] * 7,
        out_specs=vmem,
        scratch_shapes=[
            pltpu.VMEM((SEG, 2 * SEG), jnp.bfloat16),
            pltpu.VMEM((count, NTILE, 8, 2 * SEG), jnp.float32),
            pltpu.VMEM((count, 3 * RECV, 8, SEG), jnp.float32),
            pltpu.VMEM((RECV, SRC, 2 * SEG), jnp.bfloat16),
        ],
        compiler_params=pltpu.CompilerParams(vmem_limit_bytes=40 * 1024 * 1024),
    )(info, own, rest, own_sib, rest_sib, forward, band.astype(jnp.bfloat16), inverse)


def local(raw, order, pair_blocks):
    held = order.shape[1]
    gathered = (
        raw.shape[2] == SRC
        and lax.axis_size("ch") == 8
        and lax.axis_size("grp") == 4
        and raw.shape[0] == 1
        and 2 * raw.shape[1] == SEG
        and held == 4 * RECV
    )
    if gathered:
        return one_block(raw, order, pair_blocks)
    return many_blocks(raw, order, pair_blocks)


def solution(mesh):
    placed = (P("grp", "ch", None), P("ch", None), P("ch", None))
    return jax.shard_map(
        local,
        mesh=mesh,
        in_specs=placed,
        out_specs=P(("ch", "grp"), None, None, None),
        check_vma=False,
    )
```

```python
import functools
import math

import jax
import jax.numpy as jnp
import numpy as np
from jax import lax
from jax.experimental import pallas as pl
from jax.experimental.pallas import tpu as pltpu
from jax.sharding import PartitionSpec as P

SRC = 128
SEG = 256
LAGS = 256
SMOOTH = 8
MAXP = 3
REACH = 15


lag_scale = 1.0 / 16.0


def from_behind(value, axis, steps):
    count = lax.axis_size(axis)
    initial, last = (max(0, -steps), min(count, count - steps))
    return lax.ppermute(value, axis, [(source, source + steps) for source in range(initial, last)])


def transform_tables(half_len, lag_count, smooth_half):
    samples = np.arange(half_len)
    column = np.arange(2 * half_len)
    freq = column % half_len + 1
    angle_fwd = (samples[:, None] * freq[None, :] % (2 * half_len)) * (math.pi / half_len)
    forward = np.where(column[None, :] < half_len, np.cos(angle_fwd), -np.sin(angle_fwd))
    lag_steps = np.arange(lag_count) - lag_count // 2
    angle_inv = (freq[:, None] * lag_steps[None, :] % (2 * half_len)) * (math.pi / half_len)
    inverse = np.where(column[:, None] < half_len, np.cos(angle_inv), -np.sin(angle_inv)) * lag_scale
    bins = np.arange(half_len)
    band = np.abs(bins[:, None] - bins[None, :]) <= smooth_half
    return (forward.astype(np.float32), inverse.astype(np.float32), band.astype(np.float32))


def whiten(segments, forward, band):
    half_len = segments.shape[-1]
    flat_rows = segments.reshape(-1, half_len)
    spectrum = jnp.dot(flat_rows, forward, preferred_element_type=jnp.float32)
    real_part = spectrum[:, :half_len]
    imag_part = spectrum[:, half_len:]
    power_bins = real_part * real_part + imag_part * imag_part
    smoothed = jnp.dot(power_bins, band, precision=lax.Precision.HIGHEST) / (2 * SMOOTH + 1)
    water_level = jnp.mean(power_bins, axis=1, keepdims=True)
    divisor = jnp.sqrt(smoothed + 0.1 * water_level + 1e-06)
    whitened = spectrum / jnp.concatenate([divisor, divisor], axis=1)
    return whitened.astype(jnp.bfloat16).reshape(segments.shape[:-1] + (2 * half_len,))


def correlate(receivers, sources, inverse):
    half_len = receivers.shape[-1] // 2
    seg_count = receivers.shape[1]
    recv_re = receivers[..., :half_len]
    recv_im = receivers[..., half_len:]
    left_first = jnp.concatenate([recv_re, recv_im], axis=1)
    left_second = jnp.concatenate([recv_im, -recv_re], axis=1)
    right_both = jnp.concatenate([sources[..., :half_len], sources[..., half_len:]], axis=1)
    cross_re = jnp.einsum(
        "rnk,snk->rsk", left_first, right_both, preferred_element_type=jnp.float32
    )
    cross_im = jnp.einsum(
        "rnk,snk->rsk", left_second, right_both, preferred_element_type=jnp.float32
    )
    cross_spec = (jnp.concatenate([cross_re, cross_im], axis=2) * (1.0 / seg_count)).astype(
        jnp.bfloat16
    )
    recv_count = receivers.shape[0]
    src_count = sources.shape[0]
    lag_values = jnp.dot(
        cross_spec.reshape(-1, 2 * half_len), inverse, preferred_element_type=jnp.float32
    )
    return lag_values.reshape(recv_count, src_count, inverse.shape[1])


def many_blocks(raw, order, pair_blocks):
    recorded = lax.all_to_all(raw, "ch", split_axis=2, concat_axis=1, tiled=True)
    local_channels = recorded.shape[2]
    onehot = (order[0][:, None] == jnp.arange(local_channels, dtype=jnp.int32)[None, :]).astype(
        jnp.bfloat16
    )
    series = jnp.einsum(
        "ck,tc->kt", onehot, recorded[0], preferred_element_type=jnp.float32
    ).astype(jnp.bfloat16)
    segments = series.reshape(1, local_channels, -1, SEG)
    forward, inverse, band = transform_tables(SEG, LAGS, SMOOTH)
    forward = jnp.asarray(forward, jnp.bfloat16)
    inverse = jnp.asarray(inverse, jnp.bfloat16)
    own_white = whiten(segments, forward, band)
    before_list = []
    for distance in range(REACH, 0, -1):
        before_list.append(from_behind(own_white, "ch", distance))
    after_list = []
    for distance in range(1, REACH + 1):
        after_list.append(from_behind(own_white, "ch", -distance))
    window = jnp.concatenate(before_list + [own_white] + after_list, axis=1)
    window_base = (lax.axis_index("ch") - REACH) * local_channels
    groups = lax.axis_size("grp")
    receivers = own_white[0]
    slot_results = []
    for slot_index in range(MAXP):
        block_id = pair_blocks[0, slot_index]
        source_start = jnp.maximum(block_id, 0) * SRC - window_base
        sources = lax.dynamic_slice_in_dim(window[0], source_start, SRC, 0)
        is_live = (block_id >= 0).astype(jnp.float32)
        lag_values = correlate(receivers, sources, inverse) * is_live
        slot_results.append(lag_values)
    stacked = lax.psum_scatter(
        jnp.stack(slot_results, axis=1).astype(jnp.bfloat16), "grp", scatter_dimension=0, tiled=True
    ).astype(jnp.float32)
    return (stacked / groups).astype(jnp.bfloat16)


RECV = 4
KB = 8
WIDTH = 2 * SMOOTH + 1


def label_kernel(order, pairs, raw, out, keep):
    held = order.shape[1]
    half, channels = raw.shape[1:]
    me = lax.axis_index("ch")
    lanes = lax.broadcasted_iota(jnp.int32, (8, channels), 1)
    row = jnp.zeros((8, channels), jnp.int32)
    for c in range(held):
        row = jnp.where(lanes % held == c, order[0, c], row)
    row = jnp.where(lanes // held == me, row + held * me, 0)
    keep[...] = jnp.broadcast_to(jnp.where(pairs[0, 0] >= 0, 1.0, 0.0), keep.shape)
    out[0, 0:half, :] = raw[0]
    out[0, half : half + 8, :] = row.astype(jnp.float32).astype(out.dtype)


def whiten_group(items, fwd, band, spec, pows, white):
    bins = band.shape[0]
    levels = []
    for i, (first, second, first_next, second_next) in enumerate(items):
        samples = jnp.concatenate(
            [
                jnp.concatenate([first, first_next], axis=1),
                jnp.concatenate([second, second_next], axis=1),
            ],
            axis=0,
        )
        re = jnp.dot(fwd[0:bins, :], samples, preferred_element_type=jnp.float32)
        im = jnp.dot(fwd[bins:, :], samples, preferred_element_type=jnp.float32)
        power = re * re + im * im
        spec[i, 0] = re
        spec[i, 1] = im
        pows[i] = power.astype(jnp.bfloat16)
        levels.append(jnp.sum(power.reshape(bins // 8, 8, 2 * SRC), axis=0))
    for i in range(len(items)):
        level = jnp.sum(levels[i], axis=0, keepdims=True) * (0.1 * WIDTH / bins) + 1e-6 * WIDTH
        smoothed = jnp.dot(band[...], pows[i], preferred_element_type=jnp.float32)
        scale = lax.rsqrt(smoothed + level)
        for part in range(2):
            value = spec[i, part] * scale
            left = value[:, 0:SRC].reshape(bins // KB, KB, SRC)
            right = value[:, SRC:].reshape(bins // KB, KB, SRC)
            both = jnp.concatenate([left, right], axis=1).astype(jnp.bfloat16)
            white[:, part, 2 * KB * i : 2 * KB * (i + 1), :] = both


def own_kernel(own, near, other, diag, forward, band, white, fwd, perm, select, spec, pows):
    half = forward.shape[1] // 2
    zb = own.shape[0]
    ch = lax.axis_index("ch")
    base = (ch * lax.axis_size("grp") + lax.axis_index("grp")) * RECV
    mine = ch % 2
    fwd[:, 0:half] = forward[:, pl.ds(pl.multiple_of(mine * half, half), half)]
    fwd[:, half:] = forward[:, pl.ds(pl.multiple_of((1 - mine) * half, half), half)]

    dest = own[0, half : half + 8, :]
    for z in range(1, zb):
        dest = jnp.maximum(dest, own[z, half : half + 8, :])
    for z in range(zb):
        dest = jnp.maximum(dest, near[z, half : half + 8, :])
    dest = dest.astype(jnp.float32)[0:1, :]
    rows = lax.broadcasted_iota(jnp.int32, (SRC, SRC), 0)
    perm[...] = (rows.astype(jnp.float32) == dest).astype(jnp.bfloat16)
    wanted = (lax.broadcasted_iota(jnp.int32, (KB * RECV, SRC), 0) // KB + base).astype(jnp.float32)
    select[...] = (wanted == dest).astype(jnp.bfloat16)

    items = [(own[z, 0:half], near[z, 0:half], other[z], diag[z]) for z in range(zb)]
    whiten_group(items, fwd, band, spec, pows, white)


def cross_kernel(
    keep, sib, own_white, fwd, perm, select, band, inverse, out,
    white, pick, cross, lags, blank, spec, pows, sems,
):
    bins = band.shape[0]
    zb = sib.shape[0] // 4
    count = 4 * zb
    blocks = bins // KB
    deep = 2 * count * KB

    blank[...] = jnp.zeros(blank.shape, blank.dtype)
    copies = [
        pltpu.make_async_copy(blank, out.at[q, pl.ds(1, MAXP - 1)], sems.at[q]) for q in range(RECV)
    ]
    for copy in copies:
        copy.start()

    items = [(sib[z], sib[2 * zb + z], sib[zb + z], sib[3 * zb + z]) for z in range(zb)]
    whiten_group(items, fwd, band, spec, pows, white)

    def both(kb):
        return jnp.concatenate(
            [own_white[kb, 0], white[kb, 0], own_white[kb, 1], white[kb, 1]], axis=0
        )

    lane = lax.broadcasted_iota(jnp.int32, (KB * RECV, deep), 1) % KB
    sub = lax.broadcasted_iota(jnp.int32, (KB * RECV, deep), 0) % KB
    same = (lane == sub).astype(jnp.float32)
    for kb in range(blocks):
        v = lax.dot_general(
            select[...], both(kb), (((1,), (1,)), ((), ())), preferred_element_type=jnp.float32
        )
        v = v * same
        pick[kb, 0 : KB * RECV, :] = v.astype(jnp.bfloat16)
        turned = jnp.concatenate([v[:, deep // 2 :], -v[:, 0 : deep // 2]], axis=1)
        pick[kb, KB * RECV :, :] = turned.astype(jnp.bfloat16)

    sums = [jnp.dot(pick[kb], both(kb), preferred_element_type=jnp.float32) for kb in range(blocks)]
    for part in range(2):
        for q in range(RECV):
            at = (part * RECV + q) * KB
            column = jnp.concatenate([s[at : at + KB] for s in sums], axis=0) * (WIDTH / count)
            lanes = slice((q % 2) * SRC, (q % 2 + 1) * SRC)
            cross[q // 2, part * bins : (part + 1) * bins, lanes] = column.astype(jnp.bfloat16)

    for p in range(RECV // 2):
        turned = jnp.dot(inverse[...], cross[p], preferred_element_type=jnp.float32) * keep[0:1, :]
        turned = turned.astype(jnp.bfloat16)
        for u in range(2):
            q = 2 * p + u
            lags[q] = lax.dot_general(
                perm[...],
                turned[:, u * SRC : (u + 1) * SRC],
                (((1,), (1,)), ((), ())),
                preferred_element_type=jnp.float32,
            ).astype(jnp.bfloat16)
            copy = pltpu.make_async_copy(lags.at[q], out.at[q, 0], sems.at[RECV + q])
            copy.start()
            copies.append(copy)
    for copy in copies:
        copy.wait()


def one_block(raw, order, pair_blocks):
    groups = lax.axis_size("grp")
    total = lax.axis_size("ch") * groups
    half, channels = raw.shape[1:]
    vmem = pl.BlockSpec(memory_space=pltpu.VMEM)
    smem = pl.BlockSpec(memory_space=pltpu.SMEM)
    params = pltpu.CompilerParams(vmem_limit_bytes=24 * 1024 * 1024)
    dtype = raw.dtype

    block, keep = pl.pallas_call(
        label_kernel,
        out_shape=[pltpu.VMEM((1, half + 8, channels), dtype), pltpu.VMEM((8, 2 * SRC), jnp.float32)],
        in_specs=[smem, smem, vmem],
        out_specs=[vmem, vmem],
    )(order, pair_blocks, raw)

    def swap(value, ch_bits, grp_bits):
        flip = ch_bits * groups + grp_bits
        return lax.ppermute(value, ("ch", "grp"), [(d, d ^ flip) for d in range(total)])

    parts = [block, swap(block, 4, 0), swap(block, 2, 0), swap(block, 6, 0)]
    own = jnp.concatenate(parts, axis=0)
    bare = jnp.concatenate([p[:, 0:half] for p in parts], axis=0)
    diag = swap(bare, 1, 2)
    near = swap(own, 1, 0)
    other = swap(bare, 0, 2)
    sib = swap(jnp.concatenate([bare, other, near[:, 0:half], diag], axis=0), 0, 1)

    forward, inverse, band = transform_tables(SEG, LAGS, SMOOTH)
    forward, band, inverse = [
        jnp.asarray(np.ascontiguousarray(t), jnp.bfloat16) for t in (forward.T, band, inverse.T)
    ]
    zb = own.shape[0]
    blocks = SEG // KB
    white = pltpu.VMEM((blocks, 2, 2 * zb * KB, SRC), jnp.bfloat16)
    work = [
        pltpu.VMEM((zb, 2, SEG, 2 * SRC), jnp.float32),
        pltpu.VMEM((zb, SEG, 2 * SRC), jnp.bfloat16),
    ]
    own_white, fwd, perm, select = pl.pallas_call(
        own_kernel,
        out_shape=[
            white,
            pltpu.VMEM((2 * SEG, SEG), jnp.bfloat16),
            pltpu.VMEM((SRC, SRC), jnp.bfloat16),
            pltpu.VMEM((KB * RECV, SRC), jnp.bfloat16),
        ],
        in_specs=[vmem] * 6,
        out_specs=[vmem] * 4,
        scratch_shapes=work,
        compiler_params=params,
    )(own, near, other, diag, forward, band)
    return pl.pallas_call(
        cross_kernel,
        out_shape=jax.ShapeDtypeStruct((RECV, MAXP, SRC, LAGS), jnp.bfloat16),
        in_specs=[vmem] * 8,
        out_specs=pl.BlockSpec(memory_space=pl.ANY),
        scratch_shapes=[
            white,
            pltpu.VMEM((blocks, 2 * RECV * KB, 8 * zb * KB), jnp.bfloat16),
            pltpu.VMEM((RECV // 2, 2 * SEG, 2 * SRC), jnp.bfloat16),
            pltpu.VMEM((RECV, SRC, LAGS), jnp.bfloat16),
            pltpu.VMEM((MAXP - 1, SRC, LAGS), jnp.bfloat16),
            *work,
            pltpu.SemaphoreType.DMA((2 * RECV,)),
        ],
        compiler_params=params,
    )(keep, sib, own_white, fwd, perm, select, band, inverse)


def local(raw, order, pair_blocks):
    held = order.shape[1]
    gathered = (
        raw.shape[2] == SRC
        and lax.axis_size("ch") == 8
        and lax.axis_size("grp") == 4
        and raw.shape[0] == 1
        and 2 * raw.shape[1] == SEG
        and held == 4 * RECV
    )
    if gathered:
        return one_block(raw, order, pair_blocks)
    return many_blocks(raw, order, pair_blocks)


def solution(mesh):
    placed = (P("grp", "ch", None), P("ch", None), P("ch", None))
    return jax.shard_map(
        local,
        mesh=mesh,
        in_specs=placed,
        out_specs=P(("ch", "grp"), None, None, None),
        check_vma=False,
    )
```

```python
import functools
import math

import jax
import jax.numpy as jnp
import numpy as np
from jax import lax
from jax.experimental import pallas as pl
from jax.experimental.pallas import tpu as pltpu
from jax.sharding import PartitionSpec as P

SRC = 128
SEG = 256
LAGS = 256
SMOOTH = 8
MAXP = 3
REACH = 15


lag_scale = 1.0 / 16.0


def from_behind(value, axis, steps):
    count = lax.axis_size(axis)
    initial, last = (max(0, -steps), min(count, count - steps))
    return lax.ppermute(value, axis, [(source, source + steps) for source in range(initial, last)])


def transform_tables(half_len, lag_count, smooth_half):
    samples = np.arange(half_len)
    column = np.arange(2 * half_len)
    freq = column % half_len + 1
    angle_fwd = (samples[:, None] * freq[None, :] % (2 * half_len)) * (math.pi / half_len)
    forward = np.where(column[None, :] < half_len, np.cos(angle_fwd), -np.sin(angle_fwd))
    lag_steps = np.arange(lag_count) - lag_count // 2
    angle_inv = (freq[:, None] * lag_steps[None, :] % (2 * half_len)) * (math.pi / half_len)
    inverse = np.where(column[:, None] < half_len, np.cos(angle_inv), -np.sin(angle_inv)) * lag_scale
    bins = np.arange(half_len)
    band = np.abs(bins[:, None] - bins[None, :]) <= smooth_half
    return (forward.astype(np.float32), inverse.astype(np.float32), band.astype(np.float32))


def whiten(segments, forward, band):
    half_len = segments.shape[-1]
    flat_rows = segments.reshape(-1, half_len)
    spectrum = jnp.dot(flat_rows, forward, preferred_element_type=jnp.float32)
    real_part = spectrum[:, :half_len]
    imag_part = spectrum[:, half_len:]
    power_bins = real_part * real_part + imag_part * imag_part
    smoothed = jnp.dot(power_bins, band, precision=lax.Precision.HIGHEST) / (2 * SMOOTH + 1)
    water_level = jnp.mean(power_bins, axis=1, keepdims=True)
    divisor = jnp.sqrt(smoothed + 0.1 * water_level + 1e-06)
    whitened = spectrum / jnp.concatenate([divisor, divisor], axis=1)
    return whitened.astype(jnp.bfloat16).reshape(segments.shape[:-1] + (2 * half_len,))


def correlate(receivers, sources, inverse):
    half_len = receivers.shape[-1] // 2
    seg_count = receivers.shape[1]
    recv_re = receivers[..., :half_len]
    recv_im = receivers[..., half_len:]
    left_first = jnp.concatenate([recv_re, recv_im], axis=1)
    left_second = jnp.concatenate([recv_im, -recv_re], axis=1)
    right_both = jnp.concatenate([sources[..., :half_len], sources[..., half_len:]], axis=1)
    cross_re = jnp.einsum(
        "rnk,snk->rsk", left_first, right_both, preferred_element_type=jnp.float32
    )
    cross_im = jnp.einsum(
        "rnk,snk->rsk", left_second, right_both, preferred_element_type=jnp.float32
    )
    cross_spec = (jnp.concatenate([cross_re, cross_im], axis=2) * (1.0 / seg_count)).astype(
        jnp.bfloat16
    )
    recv_count = receivers.shape[0]
    src_count = sources.shape[0]
    lag_values = jnp.dot(
        cross_spec.reshape(-1, 2 * half_len), inverse, preferred_element_type=jnp.float32
    )
    return lag_values.reshape(recv_count, src_count, inverse.shape[1])


def many_blocks(raw, order, pair_blocks):
    recorded = lax.all_to_all(raw, "ch", split_axis=2, concat_axis=1, tiled=True)
    local_channels = recorded.shape[2]
    onehot = (order[0][:, None] == jnp.arange(local_channels, dtype=jnp.int32)[None, :]).astype(
        jnp.bfloat16
    )
    series = jnp.einsum(
        "ck,tc->kt", onehot, recorded[0], preferred_element_type=jnp.float32
    ).astype(jnp.bfloat16)
    segments = series.reshape(1, local_channels, -1, SEG)
    forward, inverse, band = transform_tables(SEG, LAGS, SMOOTH)
    forward = jnp.asarray(forward, jnp.bfloat16)
    inverse = jnp.asarray(inverse, jnp.bfloat16)
    own_white = whiten(segments, forward, band)
    before_list = []
    for distance in range(REACH, 0, -1):
        before_list.append(from_behind(own_white, "ch", distance))
    after_list = []
    for distance in range(1, REACH + 1):
        after_list.append(from_behind(own_white, "ch", -distance))
    window = jnp.concatenate(before_list + [own_white] + after_list, axis=1)
    window_base = (lax.axis_index("ch") - REACH) * local_channels
    groups = lax.axis_size("grp")
    receivers = own_white[0]
    slot_results = []
    for slot_index in range(MAXP):
        block_id = pair_blocks[0, slot_index]
        source_start = jnp.maximum(block_id, 0) * SRC - window_base
        sources = lax.dynamic_slice_in_dim(window[0], source_start, SRC, 0)
        is_live = (block_id >= 0).astype(jnp.float32)
        lag_values = correlate(receivers, sources, inverse) * is_live
        slot_results.append(lag_values)
    stacked = lax.psum_scatter(
        jnp.stack(slot_results, axis=1).astype(jnp.bfloat16), "grp", scatter_dimension=0, tiled=True
    ).astype(jnp.float32)
    return (stacked / groups).astype(jnp.bfloat16)


RECV = 4
WIDTH = 2 * SMOOTH + 1
DEEP = 128


def label_kernel(order, pairs, raw, out, keep):
    held = order.shape[1]
    half, channels = raw.shape[1:]
    me = lax.axis_index("ch")
    lanes = lax.broadcasted_iota(jnp.int32, (8, channels), 1)
    row = jnp.zeros((8, channels), jnp.int32)
    for c in range(held):
        row = jnp.where(lanes % held == c, order[0, c], row)
    row = jnp.where(lanes // held == me, row + held * me, 0)
    keep[...] = jnp.broadcast_to(jnp.where(pairs[0, 0] >= 0, 1.0, 0.0), keep.shape)
    out[0, 0:half, :] = raw[0]
    out[0, half : half + 8, :] = row.astype(jnp.float32).astype(out.dtype)


def whiten_group(items, fwd, band, spec, pows, white):
    bins = band.shape[0]
    levels = []
    for i, (first, second, first_next, second_next) in enumerate(items):
        samples = jnp.concatenate(
            [
                jnp.concatenate([first, first_next], axis=1),
                jnp.concatenate([second, second_next], axis=1),
            ],
            axis=0,
        )
        re = jnp.dot(fwd[0:bins, :], samples, preferred_element_type=jnp.float32)
        im = jnp.dot(fwd[bins:, :], samples, preferred_element_type=jnp.float32)
        power = re * re + im * im
        spec[i, 0] = re
        spec[i, 1] = im
        pows[i] = power.astype(jnp.bfloat16)
        levels.append(jnp.sum(power.reshape(bins // 8, 8, 2 * SRC), axis=0))
    blocks, _, rows, _ = white.shape
    kb = bins // blocks
    for i in range(len(items)):
        level = jnp.sum(levels[i], axis=0, keepdims=True) * (0.1 * WIDTH / bins) + 1e-6 * WIDTH
        smoothed = jnp.dot(band[...], pows[i], preferred_element_type=jnp.float32)
        scale = lax.rsqrt(smoothed + level)
        for part in range(2):
            value = spec[i, part] * scale
            left = value[:, 0:SRC].reshape(blocks, kb, SRC)
            right = value[:, SRC:].reshape(blocks, kb, SRC)
            both = jnp.concatenate([left, right], axis=1).astype(jnp.bfloat16)
            white[:, part, 2 * kb * i : 2 * kb * (i + 1), :] = both


def receiver_products(white, select, pick):
    blocks, parts, rows, _ = white.shape
    kb = SEG // blocks
    deep = parts * rows
    lane = lax.broadcasted_iota(jnp.int32, (kb * RECV, deep), 1)
    sub = lax.broadcasted_iota(jnp.int32, (kb * RECV, deep), 0)
    same = (lane % kb == sub % kb).astype(jnp.float32)
    sign = jnp.where(lane < rows, 1.0, -1.0)
    for g in range(0, blocks, 2):
        sources = white[g : g + 2].reshape(2 * deep, SRC)
        both = lax.dot_general(
            select, sources, (((1,), (1,)), ((), ())), preferred_element_type=jnp.float32
        )
        for u in range(2):
            v = both[:, u * deep : (u + 1) * deep] * same
            turned = pltpu.roll(v, rows, 1) * sign
            pick[g + u, 0 : kb * RECV, :] = v.astype(jnp.bfloat16)
            pick[g + u, kb * RECV :, :] = turned.astype(jnp.bfloat16)
    sums = [
        jnp.dot(pick[g], white[g].reshape(deep, SRC), preferred_element_type=jnp.float32)
        for g in range(blocks)
    ]
    return [
        jnp.concatenate([s[at * kb : (at + 1) * kb] for s in sums], axis=0)
        for at in range(2 * RECV)
    ]


def pair_items(first, second, half):
    return [
        (first[z, 0:half], second[z, 0:half], first[z + 1, 0:half], second[z + 1, 0:half])
        for z in range(0, first.shape[0], 2)
    ]


def window_kernel(
    own, near, forward, band, partial, fwd, perm, chosen, white, pick, spec, pows
):
    half = forward.shape[1] // 2
    zb = own.shape[0]
    ch = lax.axis_index("ch")
    base = (ch * lax.axis_size("grp") + lax.axis_index("grp")) * RECV
    mine = ch % 2
    fwd[:, 0:half] = forward[:, pl.ds(pl.multiple_of(mine * half, half), half)]
    fwd[:, half:] = forward[:, pl.ds(pl.multiple_of((1 - mine) * half, half), half)]

    dest = own[0, half : half + 8, :]
    for z in range(1, zb):
        dest = jnp.maximum(dest, own[z, half : half + 8, :])
    for z in range(zb):
        dest = jnp.maximum(dest, near[z, half : half + 8, :])
    dest = dest.astype(jnp.float32)[0:1, :]
    rows = lax.broadcasted_iota(jnp.int32, (SRC, SRC), 0)
    perm[...] = (rows.astype(jnp.float32) == dest).astype(jnp.bfloat16)
    wanted = lax.broadcasted_iota(jnp.int32, chosen.shape, 0) * RECV // chosen.shape[0] + base
    chosen[...] = (wanted.astype(jnp.float32) == dest).astype(jnp.bfloat16)

    whiten_group(pair_items(own, near, half), fwd, band, spec, pows, white)
    for at, value in enumerate(receiver_products(white, chosen[...], pick)):
        partial[at] = value


def middle_kernel(sib, other, diag, fwd, band, chosen, before, partial, white, pick, spec, pows):
    zb, half = other.shape[0:2]
    items = pair_items(sib.at[0:zb], sib.at[zb : 2 * zb], half) + pair_items(other, diag, half)
    whiten_group(items, fwd, band, spec, pows, white)
    each = RECV * SEG // white.shape[0]
    step = chosen.shape[0] // RECV
    select = jnp.concatenate(
        [chosen[q * step : q * step + each // RECV, :] for q in range(RECV)], axis=0
    )
    for at, value in enumerate(receiver_products(white, select, pick)):
        partial[at] = before[at] + value


def cross_kernel(
    keep, sib, before, fwd, perm, chosen, band, inverse, out,
    white, pick, cross, lags, blank, spec, pows, sems,
):
    bins = band.shape[0]
    zb, half = sib.shape[0] // 2, sib.shape[1]

    blank[...] = jnp.zeros(blank.shape, blank.dtype)
    copies = [
        pltpu.make_async_copy(blank, out.at[q, pl.ds(1, MAXP - 1)], sems.at[q]) for q in range(RECV)
    ]
    for copy in copies:
        copy.start()

    whiten_group(
        pair_items(sib.at[0:zb], sib.at[zb : 2 * zb], half), fwd, band, spec, pows, white
    )
    for at, value in enumerate(receiver_products(white, chosen[...], pick)):
        total = (before[at] + value) * (WIDTH / (4 * zb))
        part, q = at // RECV, at % RECV
        lanes = slice((q % 2) * SRC, (q % 2 + 1) * SRC)
        cross[q // 2, part * bins : (part + 1) * bins, lanes] = total.astype(jnp.bfloat16)

    for p in range(RECV // 2):
        turned = jnp.dot(inverse[...], cross[p], preferred_element_type=jnp.float32) * keep[0:1, :]
        turned = turned.astype(jnp.bfloat16)
        for u in range(2):
            q = 2 * p + u
            lags[q] = lax.dot_general(
                perm[...],
                turned[:, u * SRC : (u + 1) * SRC],
                (((1,), (1,)), ((), ())),
                preferred_element_type=jnp.float32,
            ).astype(jnp.bfloat16)
            copy = pltpu.make_async_copy(lags.at[q], out.at[q, 0], sems.at[RECV + q])
            copy.start()
            copies.append(copy)
    for copy in copies:
        copy.wait()


def one_block(raw, order, pair_blocks):
    groups = lax.axis_size("grp")
    total = lax.axis_size("ch") * groups
    half, channels = raw.shape[1:]
    vmem = pl.BlockSpec(memory_space=pltpu.VMEM)
    smem = pl.BlockSpec(memory_space=pltpu.SMEM)
    params = pltpu.CompilerParams(vmem_limit_bytes=24 * 1024 * 1024)
    dtype = raw.dtype

    block, keep = pl.pallas_call(
        label_kernel,
        out_shape=[pltpu.VMEM((1, half + 8, channels), dtype), pltpu.VMEM((8, 2 * SRC), jnp.float32)],
        in_specs=[smem, smem, vmem],
        out_specs=[vmem, vmem],
    )(order, pair_blocks, raw)

    def swap(value, ch_bits, grp_bits):
        flip = ch_bits * groups + grp_bits
        return lax.ppermute(value, ("ch", "grp"), [(d, d ^ flip) for d in range(total)])

    parts = [block, swap(block, 4, 0), swap(block, 2, 0), swap(block, 6, 0)]
    own = jnp.concatenate(parts, axis=0)
    bare = jnp.concatenate([p[:, 0:half] for p in parts], axis=0)
    near = swap(own, 1, 0)
    diag = swap(bare, 1, 2)
    other = swap(bare, 0, 2)
    first_sib = swap(jnp.concatenate([bare, near[:, 0:half]], axis=0), 0, 1)

    forward, inverse, band = transform_tables(SEG, LAGS, SMOOTH)
    forward, band, inverse = [
        jnp.asarray(np.ascontiguousarray(t), jnp.bfloat16) for t in (forward.T, band, inverse.T)
    ]
    zb = own.shape[0]

    def scratch(segments):
        kb = DEEP // (2 * segments)
        return [
            pltpu.VMEM((SEG // kb, 2, DEEP // 2, SRC), jnp.bfloat16),
            pltpu.VMEM((SEG // kb, 2 * RECV * kb, DEEP), jnp.bfloat16),
        ], [
            pltpu.VMEM((segments // 2, 2, SEG, 2 * SRC), jnp.float32),
            pltpu.VMEM((segments // 2, SEG, 2 * SRC), jnp.bfloat16),
        ]

    partial = pltpu.VMEM((2 * RECV, SEG, SRC), jnp.float32)
    spectra, work = scratch(zb)
    before, fwd, perm, chosen = pl.pallas_call(
        window_kernel,
        out_shape=[
            partial,
            pltpu.VMEM((2 * SEG, SEG), jnp.bfloat16),
            pltpu.VMEM((SRC, SRC), jnp.bfloat16),
            pltpu.VMEM((RECV * DEEP // (2 * zb), SRC), jnp.bfloat16),
        ],
        in_specs=[vmem] * 4,
        out_specs=[vmem] * 4,
        scratch_shapes=[*spectra, *work],
        compiler_params=params,
    )(own, near, forward, band)
    other, diag, chosen = lax.optimization_barrier((other, diag, chosen))
    second_sib = swap(jnp.concatenate([other, diag], axis=0), 0, 1)
    many_spectra, many_work = scratch(2 * zb)
    before = pl.pallas_call(
        middle_kernel,
        out_shape=partial,
        in_specs=[vmem] * 7,
        out_specs=vmem,
        scratch_shapes=[*many_spectra, *many_work],
        compiler_params=params,
    )(first_sib, other, diag, fwd, band, chosen, before)
    return pl.pallas_call(
        cross_kernel,
        out_shape=jax.ShapeDtypeStruct((RECV, MAXP, SRC, LAGS), jnp.bfloat16),
        in_specs=[vmem] * 8,
        out_specs=pl.BlockSpec(memory_space=pl.ANY),
        scratch_shapes=[
            *spectra,
            pltpu.VMEM((RECV // 2, 2 * SEG, 2 * SRC), jnp.bfloat16),
            pltpu.VMEM((RECV, SRC, LAGS), jnp.bfloat16),
            pltpu.VMEM((MAXP - 1, SRC, LAGS), jnp.bfloat16),
            *work,
            pltpu.SemaphoreType.DMA((2 * RECV,)),
        ],
        compiler_params=params,
    )(keep, second_sib, before, fwd, perm, chosen, band, inverse)


def local(raw, order, pair_blocks):
    held = order.shape[1]
    gathered = (
        raw.shape[2] == SRC
        and lax.axis_size("ch") == 8
        and lax.axis_size("grp") == 4
        and raw.shape[0] == 1
        and 2 * raw.shape[1] == SEG
        and held == 4 * RECV
    )
    if gathered:
        return one_block(raw, order, pair_blocks)
    return many_blocks(raw, order, pair_blocks)


def solution(mesh):
    placed = (P("grp", "ch", None), P("ch", None), P("ch", None))
    return jax.shard_map(
        local,
        mesh=mesh,
        in_specs=placed,
        out_specs=P(("ch", "grp"), None, None, None),
        check_vma=False,
    )
```

```python
import functools
import math

import jax
import jax.numpy as jnp
import numpy as np
from jax import lax
from jax.experimental import pallas as pl
from jax.experimental.pallas import tpu as pltpu
from jax.sharding import PartitionSpec as P

SRC = 128
SEG = 256
LAGS = 256
SMOOTH = 8
MAXP = 3
REACH = 15


lag_scale = 1.0 / 16.0


def from_behind(value, axis, steps):
    count = lax.axis_size(axis)
    initial, last = (max(0, -steps), min(count, count - steps))
    return lax.ppermute(value, axis, [(source, source + steps) for source in range(initial, last)])


def transform_tables(half_len, lag_count, smooth_half):
    samples = np.arange(half_len)
    column = np.arange(2 * half_len)
    freq = column % half_len + 1
    angle_fwd = (samples[:, None] * freq[None, :] % (2 * half_len)) * (math.pi / half_len)
    forward = np.where(column[None, :] < half_len, np.cos(angle_fwd), -np.sin(angle_fwd))
    lag_steps = np.arange(lag_count) - lag_count // 2
    angle_inv = (freq[:, None] * lag_steps[None, :] % (2 * half_len)) * (math.pi / half_len)
    inverse = np.where(column[:, None] < half_len, np.cos(angle_inv), -np.sin(angle_inv)) * lag_scale
    bins = np.arange(half_len)
    band = np.abs(bins[:, None] - bins[None, :]) <= smooth_half
    return (forward.astype(np.float32), inverse.astype(np.float32), band.astype(np.float32))


def whiten(segments, forward, band):
    half_len = segments.shape[-1]
    flat_rows = segments.reshape(-1, half_len)
    spectrum = jnp.dot(flat_rows, forward, preferred_element_type=jnp.float32)
    real_part = spectrum[:, :half_len]
    imag_part = spectrum[:, half_len:]
    power_bins = real_part * real_part + imag_part * imag_part
    smoothed = jnp.dot(power_bins, band, precision=lax.Precision.HIGHEST) / (2 * SMOOTH + 1)
    water_level = jnp.mean(power_bins, axis=1, keepdims=True)
    divisor = jnp.sqrt(smoothed + 0.1 * water_level + 1e-06)
    whitened = spectrum / jnp.concatenate([divisor, divisor], axis=1)
    return whitened.astype(jnp.bfloat16).reshape(segments.shape[:-1] + (2 * half_len,))


def correlate(receivers, sources, inverse):
    half_len = receivers.shape[-1] // 2
    seg_count = receivers.shape[1]
    recv_re = receivers[..., :half_len]
    recv_im = receivers[..., half_len:]
    left_first = jnp.concatenate([recv_re, recv_im], axis=1)
    left_second = jnp.concatenate([recv_im, -recv_re], axis=1)
    right_both = jnp.concatenate([sources[..., :half_len], sources[..., half_len:]], axis=1)
    cross_re = jnp.einsum(
        "rnk,snk->rsk", left_first, right_both, preferred_element_type=jnp.float32
    )
    cross_im = jnp.einsum(
        "rnk,snk->rsk", left_second, right_both, preferred_element_type=jnp.float32
    )
    cross_spec = (jnp.concatenate([cross_re, cross_im], axis=2) * (1.0 / seg_count)).astype(
        jnp.bfloat16
    )
    recv_count = receivers.shape[0]
    src_count = sources.shape[0]
    lag_values = jnp.dot(
        cross_spec.reshape(-1, 2 * half_len), inverse, preferred_element_type=jnp.float32
    )
    return lag_values.reshape(recv_count, src_count, inverse.shape[1])


def many_blocks(raw, order, pair_blocks):
    recorded = lax.all_to_all(raw, "ch", split_axis=2, concat_axis=1, tiled=True)
    local_channels = recorded.shape[2]
    onehot = (order[0][:, None] == jnp.arange(local_channels, dtype=jnp.int32)[None, :]).astype(
        jnp.bfloat16
    )
    series = jnp.einsum(
        "ck,tc->kt", onehot, recorded[0], preferred_element_type=jnp.float32
    ).astype(jnp.bfloat16)
    segments = series.reshape(1, local_channels, -1, SEG)
    forward, inverse, band = transform_tables(SEG, LAGS, SMOOTH)
    forward = jnp.asarray(forward, jnp.bfloat16)
    inverse = jnp.asarray(inverse, jnp.bfloat16)
    own_white = whiten(segments, forward, band)
    before_list = []
    for distance in range(REACH, 0, -1):
        before_list.append(from_behind(own_white, "ch", distance))
    after_list = []
    for distance in range(1, REACH + 1):
        after_list.append(from_behind(own_white, "ch", -distance))
    window = jnp.concatenate(before_list + [own_white] + after_list, axis=1)
    window_base = (lax.axis_index("ch") - REACH) * local_channels
    groups = lax.axis_size("grp")
    receivers = own_white[0]
    slot_results = []
    for slot_index in range(MAXP):
        block_id = pair_blocks[0, slot_index]
        source_start = jnp.maximum(block_id, 0) * SRC - window_base
        sources = lax.dynamic_slice_in_dim(window[0], source_start, SRC, 0)
        is_live = (block_id >= 0).astype(jnp.float32)
        lag_values = correlate(receivers, sources, inverse) * is_live
        slot_results.append(lag_values)
    stacked = lax.psum_scatter(
        jnp.stack(slot_results, axis=1).astype(jnp.bfloat16), "grp", scatter_dimension=0, tiled=True
    ).astype(jnp.float32)
    return (stacked / groups).astype(jnp.bfloat16)


RECV = 4
WIDTH = 2 * SMOOTH + 1
DEEP = 128


def label_kernel(order, pairs, raw, out, keep):
    held = order.shape[1]
    half, channels = raw.shape[1:]
    me = lax.axis_index("ch")
    lanes = lax.broadcasted_iota(jnp.int32, (8, channels), 1)
    row = jnp.zeros((8, channels), jnp.int32)
    for c in range(held):
        row = jnp.where(lanes % held == c, order[0, c], row)
    row = jnp.where(lanes // held == me, row + held * me, 0)
    keep[...] = jnp.broadcast_to(jnp.where(pairs[0, 0] >= 0, 1.0, 0.0), keep.shape)
    out[0, 0:half, :] = raw[0]
    out[0, half : half + 8, :] = row.astype(jnp.float32).astype(out.dtype)


def tables_kernel(forward, band_from, inverse_from, fwd, band, inverse, sems):
    half = forward.shape[1] // 2
    mine = lax.axis_index("ch") % 2
    near = forward.at[:, pl.ds(pl.multiple_of(mine * half, half), half)]
    far = forward.at[:, pl.ds(pl.multiple_of((1 - mine) * half, half), half)]
    copies = [
        pltpu.make_async_copy(near, fwd.at[:, 0:half], sems.at[0]),
        pltpu.make_async_copy(far, fwd.at[:, half : 2 * half], sems.at[1]),
        pltpu.make_async_copy(band_from, band, sems.at[2]),
        pltpu.make_async_copy(inverse_from, inverse, sems.at[3]),
    ]
    for copy in copies:
        copy.start()
    for copy in copies:
        copy.wait()


def whiten_group(items, fwd, band, spec, pows, white):
    bins = band.shape[0]
    levels = []
    for i, (first, second, first_next, second_next) in enumerate(items):
        samples = jnp.concatenate(
            [
                jnp.concatenate([first, first_next], axis=1),
                jnp.concatenate([second, second_next], axis=1),
            ],
            axis=0,
        )
        re = jnp.dot(fwd[0:bins, :], samples, preferred_element_type=jnp.float32)
        im = jnp.dot(fwd[bins:, :], samples, preferred_element_type=jnp.float32)
        power = re * re + im * im
        spec[i, 0] = re
        spec[i, 1] = im
        pows[i] = power.astype(jnp.bfloat16)
        levels.append(jnp.sum(power.reshape(bins // 8, 8, 2 * SRC), axis=0))
    blocks, _, rows, _ = white.shape
    kb = bins // blocks
    for i in range(len(items)):
        level = jnp.sum(levels[i], axis=0, keepdims=True) * (0.1 * WIDTH / bins) + 1e-6 * WIDTH
        smoothed = jnp.dot(band[...], pows[i], preferred_element_type=jnp.float32)
        scale = lax.rsqrt(smoothed + level)
        for part in range(2):
            value = spec[i, part] * scale
            left = value[:, 0:SRC].reshape(blocks, kb, SRC)
            right = value[:, SRC:].reshape(blocks, kb, SRC)
            both = jnp.concatenate([left, right], axis=1).astype(jnp.bfloat16)
            white[:, part, 2 * kb * i : 2 * kb * (i + 1), :] = both


def receiver_products(white, select, pick):
    blocks, parts, rows, _ = white.shape
    kb = SEG // blocks
    deep = parts * rows
    lane = lax.broadcasted_iota(jnp.int32, (kb * RECV, deep), 1)
    sub = lax.broadcasted_iota(jnp.int32, (kb * RECV, deep), 0)
    same = (lane % kb == sub % kb).astype(jnp.float32)
    sign = jnp.where(lane < rows, 1.0, -1.0)
    for g in range(0, blocks, 2):
        sources = white[g : g + 2].reshape(2 * deep, SRC)
        both = lax.dot_general(
            select, sources, (((1,), (1,)), ((), ())), preferred_element_type=jnp.float32
        )
        for u in range(2):
            v = both[:, u * deep : (u + 1) * deep] * same
            turned = pltpu.roll(v, rows, 1) * sign
            pick[g + u, 0 : kb * RECV, :] = v.astype(jnp.bfloat16)
            pick[g + u, kb * RECV :, :] = turned.astype(jnp.bfloat16)
    sums = [
        jnp.dot(pick[g], white[g].reshape(deep, SRC), preferred_element_type=jnp.float32)
        for g in range(blocks)
    ]
    return [
        jnp.concatenate([s[at * kb : (at + 1) * kb] for s in sums], axis=0)
        for at in range(2 * RECV)
    ]


def pair_items(first, second, half):
    return [
        (first[z, 0:half], second[z, 0:half], first[z + 1, 0:half], second[z + 1, 0:half])
        for z in range(0, first.shape[0], 2)
    ]


def window_kernel(
    own, near, fwd, band, partial, perm, chosen, white, pick, spec, pows
):
    half = fwd.shape[1] // 2
    zb = own.shape[0]
    ch = lax.axis_index("ch")
    base = (ch * lax.axis_size("grp") + lax.axis_index("grp")) * RECV

    dest = own[0, half : half + 8, :]
    for z in range(1, zb):
        dest = jnp.maximum(dest, own[z, half : half + 8, :])
    for z in range(zb):
        dest = jnp.maximum(dest, near[z, half : half + 8, :])
    dest = dest.astype(jnp.float32)[0:1, :]
    rows = lax.broadcasted_iota(jnp.int32, (SRC, SRC), 0)
    perm[...] = (rows.astype(jnp.float32) == dest).astype(jnp.bfloat16)
    wanted = lax.broadcasted_iota(jnp.int32, chosen.shape, 0) * RECV // chosen.shape[0] + base
    chosen[...] = (wanted.astype(jnp.float32) == dest).astype(jnp.bfloat16)

    whiten_group(pair_items(own, near, half), fwd, band, spec, pows, white)
    for at, value in enumerate(receiver_products(white, chosen[...], pick)):
        partial[at] = value


def middle_kernel(sib, other, diag, fwd, band, chosen, before, partial, white, pick, spec, pows):
    zb, half = other.shape[0:2]
    items = pair_items(sib.at[0:zb], sib.at[zb : 2 * zb], half) + pair_items(other, diag, half)
    whiten_group(items, fwd, band, spec, pows, white)
    each = RECV * SEG // white.shape[0]
    step = chosen.shape[0] // RECV
    select = jnp.concatenate(
        [chosen[q * step : q * step + each // RECV, :] for q in range(RECV)], axis=0
    )
    for at, value in enumerate(receiver_products(white, select, pick)):
        partial[at] = before[at] + value


def cross_kernel(
    keep, sib, before, fwd, perm, chosen, band, inverse, out,
    white, pick, cross, lags, blank, spec, pows, sems,
):
    bins = band.shape[0]
    zb, half = sib.shape[0] // 2, sib.shape[1]

    blank[...] = jnp.zeros(blank.shape, blank.dtype)
    copies = [
        pltpu.make_async_copy(blank, out.at[q, pl.ds(1, MAXP - 1)], sems.at[q]) for q in range(RECV)
    ]
    for copy in copies:
        copy.start()

    whiten_group(
        pair_items(sib.at[0:zb], sib.at[zb : 2 * zb], half), fwd, band, spec, pows, white
    )
    for at, value in enumerate(receiver_products(white, chosen[...], pick)):
        total = (before[at] + value) * (WIDTH / (4 * zb))
        part, q = at // RECV, at % RECV
        lanes = slice((q % 2) * SRC, (q % 2 + 1) * SRC)
        cross[q // 2, part * bins : (part + 1) * bins, lanes] = total.astype(jnp.bfloat16)

    for q in range(RECV):
        held = cross[q // 2, :, (q % 2) * SRC : (q % 2 + 1) * SRC]
        turned = lax.dot_general(
            perm[...], held, (((1,), (1,)), ((), ())), preferred_element_type=jnp.float32
        ).astype(jnp.bfloat16)
        lag_values = jnp.dot(turned, inverse[...], preferred_element_type=jnp.float32)
        lags[q] = (lag_values * keep[0:1, :]).astype(jnp.bfloat16)
        copy = pltpu.make_async_copy(lags.at[q], out.at[q, 0], sems.at[RECV + q])
        copy.start()
        copies.append(copy)
    for copy in copies:
        copy.wait()


def one_block(raw, order, pair_blocks):
    groups = lax.axis_size("grp")
    total = lax.axis_size("ch") * groups
    half, channels = raw.shape[1:]
    vmem = pl.BlockSpec(memory_space=pltpu.VMEM)
    smem = pl.BlockSpec(memory_space=pltpu.SMEM)
    params = pltpu.CompilerParams(vmem_limit_bytes=24 * 1024 * 1024)
    dtype = raw.dtype

    block, keep = pl.pallas_call(
        label_kernel,
        out_shape=[pltpu.VMEM((1, half + 8, channels), dtype), pltpu.VMEM((8, 2 * SRC), jnp.float32)],
        in_specs=[smem, smem, vmem],
        out_specs=[vmem, vmem],
    )(order, pair_blocks, raw)

    def swap(value, ch_bits, grp_bits):
        flip = ch_bits * groups + grp_bits
        return lax.ppermute(value, ("ch", "grp"), [(d, d ^ flip) for d in range(total)])

    parts = [block, swap(block, 2, 0), swap(block, 6, 0), swap(block, 4, 0)]

    forward, inverse, band = transform_tables(SEG, LAGS, SMOOTH)
    forward, band, inverse = [
        jnp.asarray(np.ascontiguousarray(t), jnp.bfloat16) for t in (forward.T, band, inverse)
    ]
    anywhere = pl.BlockSpec(memory_space=pl.ANY)
    fwd, band, inverse = pl.pallas_call(
        tables_kernel,
        out_shape=[pltpu.VMEM(t.shape, t.dtype) for t in (forward, band, inverse)],
        in_specs=[anywhere] * 3,
        out_specs=[vmem] * 3,
        scratch_shapes=[pltpu.SemaphoreType.DMA((4,))],
    )(forward, band, inverse)
    parts, fwd, band, inverse = lax.optimization_barrier((parts, fwd, band, inverse))
    own = jnp.concatenate(parts, axis=0)
    bare = jnp.concatenate([p[:, 0:half] for p in parts], axis=0)
    near = swap(own, 1, 0)
    diag = swap(bare, 1, 2)
    other = swap(bare, 0, 2)
    first_sib = swap(jnp.concatenate([bare, near[:, 0:half]], axis=0), 0, 1)

    zb = own.shape[0]

    def scratch(segments):
        kb = DEEP // (2 * segments)
        return [
            pltpu.VMEM((SEG // kb, 2, DEEP // 2, SRC), jnp.bfloat16),
            pltpu.VMEM((SEG // kb, 2 * RECV * kb, DEEP), jnp.bfloat16),
        ], [
            pltpu.VMEM((segments // 2, 2, SEG, 2 * SRC), jnp.float32),
            pltpu.VMEM((segments // 2, SEG, 2 * SRC), jnp.bfloat16),
        ]

    partial = pltpu.VMEM((2 * RECV, SEG, SRC), jnp.float32)
    spectra, work = scratch(zb)
    before, perm, chosen = pl.pallas_call(
        window_kernel,
        out_shape=[
            partial,
            pltpu.VMEM((SRC, SRC), jnp.bfloat16),
            pltpu.VMEM((RECV * DEEP // (2 * zb), SRC), jnp.bfloat16),
        ],
        in_specs=[vmem] * 4,
        out_specs=[vmem] * 3,
        scratch_shapes=[*spectra, *work],
        compiler_params=params,
    )(own, near, fwd, band)
    other, diag, chosen = lax.optimization_barrier((other, diag, chosen))
    second_sib = swap(jnp.concatenate([other, diag], axis=0), 0, 1)
    many_spectra, many_work = scratch(2 * zb)
    before = pl.pallas_call(
        middle_kernel,
        out_shape=partial,
        in_specs=[vmem] * 7,
        out_specs=vmem,
        scratch_shapes=[*many_spectra, *many_work],
        compiler_params=params,
    )(first_sib, other, diag, fwd, band, chosen, before)
    return pl.pallas_call(
        cross_kernel,
        out_shape=jax.ShapeDtypeStruct((RECV, MAXP, SRC, LAGS), jnp.bfloat16),
        in_specs=[vmem] * 8,
        out_specs=pl.BlockSpec(memory_space=pl.ANY),
        scratch_shapes=[
            *spectra,
            pltpu.VMEM((RECV // 2, 2 * SEG, 2 * SRC), jnp.bfloat16),
            pltpu.VMEM((RECV, SRC, LAGS), jnp.bfloat16),
            pltpu.VMEM((MAXP - 1, SRC, LAGS), jnp.bfloat16),
            *work,
            pltpu.SemaphoreType.DMA((2 * RECV,)),
        ],
        compiler_params=params,
    )(keep, second_sib, before, fwd, perm, chosen, band, inverse)


def local(raw, order, pair_blocks):
    held = order.shape[1]
    gathered = (
        raw.shape[2] == SRC
        and lax.axis_size("ch") == 8
        and lax.axis_size("grp") == 4
        and raw.shape[0] == 1
        and 2 * raw.shape[1] == SEG
        and held == 4 * RECV
    )
    if gathered:
        return one_block(raw, order, pair_blocks)
    return many_blocks(raw, order, pair_blocks)


def solution(mesh):
    placed = (P("grp", "ch", None), P("ch", None), P("ch", None))
    return jax.shard_map(
        local,
        mesh=mesh,
        in_specs=placed,
        out_specs=P(("ch", "grp"), None, None, None),
        check_vma=False,
    )
```

```python
import functools
import math

import jax
import jax.numpy as jnp
import numpy as np
from jax import lax
from jax.experimental import pallas as pl
from jax.experimental.pallas import tpu as pltpu
from jax.sharding import PartitionSpec as P

SRC = 128
SEG = 256
LAGS = 256
SMOOTH = 8
MAXP = 3
REACH = 15


lag_scale = 1.0 / 16.0


def from_behind(value, axis, steps):
    count = lax.axis_size(axis)
    initial, last = (max(0, -steps), min(count, count - steps))
    return lax.ppermute(value, axis, [(source, source + steps) for source in range(initial, last)])


def transform_tables(half_len, lag_count, smooth_half):
    samples = np.arange(half_len)
    column = np.arange(2 * half_len)
    freq = column % half_len + 1
    angle_fwd = (samples[:, None] * freq[None, :] % (2 * half_len)) * (math.pi / half_len)
    forward = np.where(column[None, :] < half_len, np.cos(angle_fwd), -np.sin(angle_fwd))
    lag_steps = np.arange(lag_count) - lag_count // 2
    angle_inv = (freq[:, None] * lag_steps[None, :] % (2 * half_len)) * (math.pi / half_len)
    inverse = np.where(column[:, None] < half_len, np.cos(angle_inv), -np.sin(angle_inv)) * lag_scale
    bins = np.arange(half_len)
    band = np.abs(bins[:, None] - bins[None, :]) <= smooth_half
    return (forward.astype(np.float32), inverse.astype(np.float32), band.astype(np.float32))


def whiten(segments, forward, band):
    half_len = segments.shape[-1]
    flat_rows = segments.reshape(-1, half_len)
    spectrum = jnp.dot(flat_rows, forward, preferred_element_type=jnp.float32)
    real_part = spectrum[:, :half_len]
    imag_part = spectrum[:, half_len:]
    power_bins = real_part * real_part + imag_part * imag_part
    smoothed = jnp.dot(power_bins, band, precision=lax.Precision.HIGHEST) / (2 * SMOOTH + 1)
    water_level = jnp.mean(power_bins, axis=1, keepdims=True)
    divisor = jnp.sqrt(smoothed + 0.1 * water_level + 1e-06)
    whitened = spectrum / jnp.concatenate([divisor, divisor], axis=1)
    return whitened.astype(jnp.bfloat16).reshape(segments.shape[:-1] + (2 * half_len,))


def correlate(receivers, sources, inverse):
    half_len = receivers.shape[-1] // 2
    seg_count = receivers.shape[1]
    recv_re = receivers[..., :half_len]
    recv_im = receivers[..., half_len:]
    left_first = jnp.concatenate([recv_re, recv_im], axis=1)
    left_second = jnp.concatenate([recv_im, -recv_re], axis=1)
    right_both = jnp.concatenate([sources[..., :half_len], sources[..., half_len:]], axis=1)
    cross_re = jnp.einsum(
        "rnk,snk->rsk", left_first, right_both, preferred_element_type=jnp.float32
    )
    cross_im = jnp.einsum(
        "rnk,snk->rsk", left_second, right_both, preferred_element_type=jnp.float32
    )
    cross_spec = (jnp.concatenate([cross_re, cross_im], axis=2) * (1.0 / seg_count)).astype(
        jnp.bfloat16
    )
    recv_count = receivers.shape[0]
    src_count = sources.shape[0]
    lag_values = jnp.dot(
        cross_spec.reshape(-1, 2 * half_len), inverse, preferred_element_type=jnp.float32
    )
    return lag_values.reshape(recv_count, src_count, inverse.shape[1])


def many_blocks(raw, order, pair_blocks):
    recorded = lax.all_to_all(raw, "ch", split_axis=2, concat_axis=1, tiled=True)
    local_channels = recorded.shape[2]
    onehot = (order[0][:, None] == jnp.arange(local_channels, dtype=jnp.int32)[None, :]).astype(
        jnp.bfloat16
    )
    series = jnp.einsum(
        "ck,tc->kt", onehot, recorded[0], preferred_element_type=jnp.float32
    ).astype(jnp.bfloat16)
    segments = series.reshape(1, local_channels, -1, SEG)
    forward, inverse, band = transform_tables(SEG, LAGS, SMOOTH)
    forward = jnp.asarray(forward, jnp.bfloat16)
    inverse = jnp.asarray(inverse, jnp.bfloat16)
    own_white = whiten(segments, forward, band)
    before_list = []
    for distance in range(REACH, 0, -1):
        before_list.append(from_behind(own_white, "ch", distance))
    after_list = []
    for distance in range(1, REACH + 1):
        after_list.append(from_behind(own_white, "ch", -distance))
    window = jnp.concatenate(before_list + [own_white] + after_list, axis=1)
    window_base = (lax.axis_index("ch") - REACH) * local_channels
    groups = lax.axis_size("grp")
    receivers = own_white[0]
    slot_results = []
    for slot_index in range(MAXP):
        block_id = pair_blocks[0, slot_index]
        source_start = jnp.maximum(block_id, 0) * SRC - window_base
        sources = lax.dynamic_slice_in_dim(window[0], source_start, SRC, 0)
        is_live = (block_id >= 0).astype(jnp.float32)
        lag_values = correlate(receivers, sources, inverse) * is_live
        slot_results.append(lag_values)
    stacked = lax.psum_scatter(
        jnp.stack(slot_results, axis=1).astype(jnp.bfloat16), "grp", scatter_dimension=0, tiled=True
    ).astype(jnp.float32)
    return (stacked / groups).astype(jnp.bfloat16)


RECV = 4
WIDTH = 2 * SMOOTH + 1
DEEP = 128
LABEL = 16


def label_kernel(order, pairs, raw, out, keep):
    held = order.shape[1]
    half, channels = raw.shape[1:]
    me = lax.axis_index("ch")
    lanes = lax.broadcasted_iota(jnp.int32, (LABEL, channels), 1)
    row = jnp.zeros((LABEL, channels), jnp.int32)
    for c in range(held):
        row = jnp.where(lanes % held == c, order[0, c], row)
    row = jnp.where(lanes // held == me, row + held * me, 0)
    keep[...] = jnp.broadcast_to(jnp.where(pairs[0, 0] >= 0, 1.0, 0.0), keep.shape)
    out[0, 0:half, :] = raw[0]
    out[0, half : half + LABEL, :] = row.astype(jnp.float32).astype(out.dtype)


def tables_kernel(forward, band_from, inverse_from, fwd, band, inverse, sems):
    half = forward.shape[1] // 2
    mine = lax.axis_index("ch") % 2
    near = forward.at[:, pl.ds(pl.multiple_of(mine * half, half), half)]
    far = forward.at[:, pl.ds(pl.multiple_of((1 - mine) * half, half), half)]
    copies = [
        pltpu.make_async_copy(near, fwd.at[:, 0:half], sems.at[0]),
        pltpu.make_async_copy(far, fwd.at[:, half : 2 * half], sems.at[1]),
        pltpu.make_async_copy(band_from, band, sems.at[2]),
        pltpu.make_async_copy(inverse_from, inverse, sems.at[3]),
    ]
    for copy in copies:
        copy.start()
    for copy in copies:
        copy.wait()


def whiten_group(items, fwd, band, spec, pows, white):
    bins = band.shape[0]
    levels = []
    for i, (first, second, first_next, second_next) in enumerate(items):
        samples = jnp.concatenate(
            [
                jnp.concatenate([first, first_next], axis=1),
                jnp.concatenate([second, second_next], axis=1),
            ],
            axis=0,
        )
        re = jnp.dot(fwd[0:bins, :], samples, preferred_element_type=jnp.float32)
        im = jnp.dot(fwd[bins:, :], samples, preferred_element_type=jnp.float32)
        power = re * re + im * im
        spec[i, 0] = re
        spec[i, 1] = im
        pows[i] = power.astype(jnp.bfloat16)
        levels.append(jnp.sum(power.reshape(bins // 8, 8, 2 * SRC), axis=0))
    blocks, _, rows, _ = white.shape
    kb = bins // blocks
    for i in range(len(items)):
        level = jnp.sum(levels[i], axis=0, keepdims=True) * (0.1 * WIDTH / bins) + 1e-6 * WIDTH
        smoothed = jnp.dot(band[...], pows[i], preferred_element_type=jnp.float32)
        scale = lax.rsqrt(smoothed + level)
        for part in range(2):
            value = spec[i, part] * scale
            left = value[:, 0:SRC].reshape(blocks, kb, SRC)
            right = value[:, SRC:].reshape(blocks, kb, SRC)
            both = jnp.concatenate([left, right], axis=1).astype(jnp.bfloat16)
            white[:, part, 2 * kb * i : 2 * kb * (i + 1), :] = both


def receiver_products(white, select, pick):
    blocks, parts, rows, _ = white.shape
    kb = SEG // blocks
    deep = parts * rows
    lane = lax.broadcasted_iota(jnp.int32, (kb * RECV, deep), 1)
    sub = lax.broadcasted_iota(jnp.int32, (kb * RECV, deep), 0)
    same = (lane % kb == sub % kb).astype(jnp.float32)
    sign = jnp.where(lane < rows, 1.0, -1.0)
    for g in range(0, blocks, 2):
        sources = white[g : g + 2].reshape(2 * deep, SRC)
        both = lax.dot_general(
            select, sources, (((1,), (1,)), ((), ())), preferred_element_type=jnp.float32
        )
        for u in range(2):
            v = both[:, u * deep : (u + 1) * deep] * same
            turned = pltpu.roll(v, rows, 1) * sign
            pick[g + u, 0 : kb * RECV, :] = v.astype(jnp.bfloat16)
            pick[g + u, kb * RECV :, :] = turned.astype(jnp.bfloat16)
    sums = [
        jnp.dot(pick[g], white[g].reshape(deep, SRC), preferred_element_type=jnp.float32)
        for g in range(blocks)
    ]
    return [
        jnp.concatenate([s[at * kb : (at + 1) * kb] for s in sums], axis=0)
        for at in range(2 * RECV)
    ]


def pair_items(first, second, half):
    return [
        (first[z, 0:half], second[z, 0:half], first[z + 1, 0:half], second[z + 1, 0:half])
        for z in range(0, first.shape[0], 2)
    ]


def window_kernel(
    own, near, label, near_label, fwd, band, partial, perm, chosen, white, pick, spec, pows
):
    half = fwd.shape[1] // 2
    zb = own.shape[0]
    ch = lax.axis_index("ch")
    base = (ch * lax.axis_size("grp") + lax.axis_index("grp")) * RECV

    dest = jnp.maximum(label[...], near_label[...])
    dest = dest.astype(jnp.float32)[0:1, :]
    rows = lax.broadcasted_iota(jnp.int32, (SRC, SRC), 0)
    perm[...] = (rows.astype(jnp.float32) == dest).astype(jnp.bfloat16)
    wanted = lax.broadcasted_iota(jnp.int32, chosen.shape, 0) * RECV // chosen.shape[0] + base
    chosen[...] = (wanted.astype(jnp.float32) == dest).astype(jnp.float32)

    whiten_group(pair_items(own, near, half), fwd, band, spec, pows, white)
    for at, value in enumerate(receiver_products(white, chosen[...].astype(jnp.bfloat16), pick)):
        partial[at] = value


def middle_kernel(sib, other, diag, fwd, band, chosen, before, partial, white, pick, spec, pows):
    zb, half = other.shape[0:2]
    items = pair_items(sib.at[0:zb], sib.at[zb : 2 * zb], half) + pair_items(other, diag, half)
    whiten_group(items, fwd, band, spec, pows, white)
    each = RECV * SEG // white.shape[0]
    step = chosen.shape[0] // RECV
    select = jnp.concatenate(
        [chosen[q * step : q * step + each // RECV, :] for q in range(RECV)], axis=0
    )
    for at, value in enumerate(receiver_products(white, select.astype(jnp.bfloat16), pick)):
        partial[at] = before[at] + value


def cross_kernel(
    keep, sib, before, fwd, perm, chosen, band, inverse, out,
    white, pick, cross, lags, blank, spec, pows, sems,
):
    bins = band.shape[0]
    zb, half = sib.shape[0] // 2, sib.shape[1]

    blank[...] = jnp.zeros(blank.shape, blank.dtype)
    copies = [
        pltpu.make_async_copy(blank, out.at[q, pl.ds(1, MAXP - 1)], sems.at[q]) for q in range(RECV)
    ]
    for copy in copies:
        copy.start()

    whiten_group(
        pair_items(sib.at[0:zb], sib.at[zb : 2 * zb], half), fwd, band, spec, pows, white
    )
    for at, value in enumerate(receiver_products(white, chosen[...].astype(jnp.bfloat16), pick)):
        total = (before[at] + value) * (WIDTH / (4 * zb))
        part, q = at // RECV, at % RECV
        lanes = slice((q % 2) * SRC, (q % 2 + 1) * SRC)
        cross[q // 2, part * bins : (part + 1) * bins, lanes] = total.astype(jnp.bfloat16)

    for q in range(RECV):
        held = cross[q // 2, :, (q % 2) * SRC : (q % 2 + 1) * SRC]
        turned = lax.dot_general(
            perm[...], held, (((1,), (1,)), ((), ())), preferred_element_type=jnp.float32
        ).astype(jnp.bfloat16)
        lag_values = jnp.dot(turned, inverse[...], preferred_element_type=jnp.float32)
        lags[q] = (lag_values * keep[0:1, :]).astype(jnp.bfloat16)
        copy = pltpu.make_async_copy(lags.at[q], out.at[q, 0], sems.at[RECV + q])
        copy.start()
        copies.append(copy)
    for copy in copies:
        copy.wait()


def one_block(raw, order, pair_blocks):
    groups = lax.axis_size("grp")
    total = lax.axis_size("ch") * groups
    half, channels = raw.shape[1:]
    vmem = pl.BlockSpec(memory_space=pltpu.VMEM)
    smem = pl.BlockSpec(memory_space=pltpu.SMEM)
    params = pltpu.CompilerParams(vmem_limit_bytes=24 * 1024 * 1024)
    dtype = raw.dtype

    block, keep = pl.pallas_call(
        label_kernel,
        out_shape=[pltpu.VMEM((1, half + LABEL, channels), dtype), pltpu.VMEM((8, 2 * SRC), jnp.float32)],
        in_specs=[smem, smem, vmem],
        out_specs=[vmem, vmem],
    )(order, pair_blocks, raw)

    def swap(value, ch_bits, grp_bits):
        flip = ch_bits * groups + grp_bits
        return lax.ppermute(value, ("ch", "grp"), [(d, d ^ flip) for d in range(total)])

    parts = [block, swap(block, 2, 0), swap(block, 6, 0), swap(block, 4, 0)]

    forward, inverse, band = transform_tables(SEG, LAGS, SMOOTH)
    forward, band, inverse = [
        jnp.asarray(np.ascontiguousarray(t), jnp.bfloat16) for t in (forward.T, band, inverse)
    ]
    anywhere = pl.BlockSpec(memory_space=pl.ANY)
    fwd, band, inverse = pl.pallas_call(
        tables_kernel,
        out_shape=[pltpu.VMEM(t.shape, t.dtype) for t in (forward, band, inverse)],
        in_specs=[anywhere] * 3,
        out_specs=[vmem] * 3,
        scratch_shapes=[pltpu.SemaphoreType.DMA((4,))],
    )(forward, band, inverse)
    parts, fwd, band, inverse = lax.optimization_barrier((parts, fwd, band, inverse))
    own = jnp.concatenate([p[0, 0:half] for p in parts], axis=0)
    label = functools.reduce(jnp.maximum, [p[0, half:] for p in parts])
    near = swap(jnp.concatenate([own, label], axis=0), 1, 0)
    diag = swap(own, 1, 2).reshape(-1, half, channels)
    other = swap(own, 0, 2).reshape(-1, half, channels)
    near, near_label = near[: own.shape[0]].reshape(-1, half, channels), near[own.shape[0] :]
    own = own.reshape(-1, half, channels)
    first_sib = swap(jnp.concatenate([own, near], axis=0), 0, 1)

    zb = own.shape[0]

    def scratch(segments):
        kb = DEEP // (2 * segments)
        return [
            pltpu.VMEM((SEG // kb, 2, DEEP // 2, SRC), jnp.bfloat16),
            pltpu.VMEM((SEG // kb, 2 * RECV * kb, DEEP), jnp.bfloat16),
        ], [
            pltpu.VMEM((segments // 2, 2, SEG, 2 * SRC), jnp.float32),
            pltpu.VMEM((segments // 2, SEG, 2 * SRC), jnp.bfloat16),
        ]

    partial = pltpu.VMEM((2 * RECV, SEG, SRC), jnp.float32)
    spectra, work = scratch(zb)
    before, perm, chosen = pl.pallas_call(
        window_kernel,
        out_shape=[
            partial,
            pltpu.VMEM((SRC, SRC), jnp.bfloat16),
            pltpu.VMEM((RECV * DEEP // (2 * zb), SRC), jnp.float32),
        ],
        in_specs=[vmem] * 6,
        out_specs=[vmem] * 3,
        scratch_shapes=[*spectra, *work],
        compiler_params=params,
    )(own, near, label, near_label, fwd, band)
    other, diag, chosen = lax.optimization_barrier((other, diag, chosen))
    second_sib = swap(jnp.concatenate([other, diag], axis=0), 0, 1)
    many_spectra, many_work = scratch(2 * zb)
    before = pl.pallas_call(
        middle_kernel,
        out_shape=partial,
        in_specs=[vmem] * 7,
        out_specs=vmem,
        scratch_shapes=[*many_spectra, *many_work],
        compiler_params=params,
    )(first_sib, other, diag, fwd, band, chosen, before)
    return pl.pallas_call(
        cross_kernel,
        out_shape=jax.ShapeDtypeStruct((RECV, MAXP, SRC, LAGS), jnp.bfloat16),
        in_specs=[vmem] * 8,
        out_specs=pl.BlockSpec(memory_space=pl.ANY),
        scratch_shapes=[
            *spectra,
            pltpu.VMEM((RECV // 2, 2 * SEG, 2 * SRC), jnp.bfloat16),
            pltpu.VMEM((RECV, SRC, LAGS), jnp.bfloat16),
            pltpu.VMEM((MAXP - 1, SRC, LAGS), jnp.bfloat16),
            *work,
            pltpu.SemaphoreType.DMA((2 * RECV,)),
        ],
        compiler_params=params,
    )(keep, second_sib, before, fwd, perm, chosen, band, inverse)


def local(raw, order, pair_blocks):
    held = order.shape[1]
    gathered = (
        raw.shape[2] == SRC
        and lax.axis_size("ch") == 8
        and lax.axis_size("grp") == 4
        and raw.shape[0] == 1
        and 2 * raw.shape[1] == SEG
        and held == 4 * RECV
    )
    if gathered:
        return one_block(raw, order, pair_blocks)
    return many_blocks(raw, order, pair_blocks)


def solution(mesh):
    placed = (P("grp", "ch", None), P("ch", None), P("ch", None))
    return jax.shard_map(
        local,
        mesh=mesh,
        in_specs=placed,
        out_specs=P(("ch", "grp"), None, None, None),
        check_vma=False,
    )
```

```python
import functools
import math

import jax
import jax.numpy as jnp
import numpy as np
from jax import lax
from jax.experimental import pallas as pl
from jax.experimental.pallas import tpu as pltpu
from jax.sharding import PartitionSpec as P

SRC = 128
SEG = 256
LAGS = 256
SMOOTH = 8
MAXP = 3
REACH = 15


lag_scale = 1.0 / 16.0


def from_behind(value, axis, steps):
    count = lax.axis_size(axis)
    initial, last = (max(0, -steps), min(count, count - steps))
    return lax.ppermute(value, axis, [(source, source + steps) for source in range(initial, last)])


def transform_tables(half_len, lag_count, smooth_half):
    samples = np.arange(half_len)
    column = np.arange(2 * half_len)
    freq = column % half_len + 1
    angle_fwd = (samples[:, None] * freq[None, :] % (2 * half_len)) * (math.pi / half_len)
    forward = np.where(column[None, :] < half_len, np.cos(angle_fwd), -np.sin(angle_fwd))
    lag_steps = np.arange(lag_count) - lag_count // 2
    angle_inv = (freq[:, None] * lag_steps[None, :] % (2 * half_len)) * (math.pi / half_len)
    inverse = np.where(column[:, None] < half_len, np.cos(angle_inv), -np.sin(angle_inv)) * lag_scale
    bins = np.arange(half_len)
    band = np.abs(bins[:, None] - bins[None, :]) <= smooth_half
    return (forward.astype(np.float32), inverse.astype(np.float32), band.astype(np.float32))


def whiten(segments, forward, band):
    half_len = segments.shape[-1]
    flat_rows = segments.reshape(-1, half_len)
    spectrum = jnp.dot(flat_rows, forward, preferred_element_type=jnp.float32)
    real_part = spectrum[:, :half_len]
    imag_part = spectrum[:, half_len:]
    power_bins = real_part * real_part + imag_part * imag_part
    smoothed = jnp.dot(power_bins, band, precision=lax.Precision.HIGHEST) / (2 * SMOOTH + 1)
    water_level = jnp.mean(power_bins, axis=1, keepdims=True)
    divisor = jnp.sqrt(smoothed + 0.1 * water_level + 1e-06)
    whitened = spectrum / jnp.concatenate([divisor, divisor], axis=1)
    return whitened.astype(jnp.bfloat16).reshape(segments.shape[:-1] + (2 * half_len,))


def correlate(receivers, sources, inverse):
    half_len = receivers.shape[-1] // 2
    seg_count = receivers.shape[1]
    recv_re = receivers[..., :half_len]
    recv_im = receivers[..., half_len:]
    left_first = jnp.concatenate([recv_re, recv_im], axis=1)
    left_second = jnp.concatenate([recv_im, -recv_re], axis=1)
    right_both = jnp.concatenate([sources[..., :half_len], sources[..., half_len:]], axis=1)
    cross_re = jnp.einsum(
        "rnk,snk->rsk", left_first, right_both, preferred_element_type=jnp.float32
    )
    cross_im = jnp.einsum(
        "rnk,snk->rsk", left_second, right_both, preferred_element_type=jnp.float32
    )
    cross_spec = (jnp.concatenate([cross_re, cross_im], axis=2) * (1.0 / seg_count)).astype(
        jnp.bfloat16
    )
    recv_count = receivers.shape[0]
    src_count = sources.shape[0]
    lag_values = jnp.dot(
        cross_spec.reshape(-1, 2 * half_len), inverse, preferred_element_type=jnp.float32
    )
    return lag_values.reshape(recv_count, src_count, inverse.shape[1])


def many_blocks(raw, order, pair_blocks):
    recorded = lax.all_to_all(raw, "ch", split_axis=2, concat_axis=1, tiled=True)
    local_channels = recorded.shape[2]
    onehot = (order[0][:, None] == jnp.arange(local_channels, dtype=jnp.int32)[None, :]).astype(
        jnp.bfloat16
    )
    series = jnp.einsum(
        "ck,tc->kt", onehot, recorded[0], preferred_element_type=jnp.float32
    ).astype(jnp.bfloat16)
    segments = series.reshape(1, local_channels, -1, SEG)
    forward, inverse, band = transform_tables(SEG, LAGS, SMOOTH)
    forward = jnp.asarray(forward, jnp.bfloat16)
    inverse = jnp.asarray(inverse, jnp.bfloat16)
    own_white = whiten(segments, forward, band)
    before_list = []
    for distance in range(REACH, 0, -1):
        before_list.append(from_behind(own_white, "ch", distance))
    after_list = []
    for distance in range(1, REACH + 1):
        after_list.append(from_behind(own_white, "ch", -distance))
    window = jnp.concatenate(before_list + [own_white] + after_list, axis=1)
    window_base = (lax.axis_index("ch") - REACH) * local_channels
    groups = lax.axis_size("grp")
    receivers = own_white[0]
    slot_results = []
    for slot_index in range(MAXP):
        block_id = pair_blocks[0, slot_index]
        source_start = jnp.maximum(block_id, 0) * SRC - window_base
        sources = lax.dynamic_slice_in_dim(window[0], source_start, SRC, 0)
        is_live = (block_id >= 0).astype(jnp.float32)
        lag_values = correlate(receivers, sources, inverse) * is_live
        slot_results.append(lag_values)
    stacked = lax.psum_scatter(
        jnp.stack(slot_results, axis=1).astype(jnp.bfloat16), "grp", scatter_dimension=0, tiled=True
    ).astype(jnp.float32)
    return (stacked / groups).astype(jnp.bfloat16)


RECV = 4
WIDTH = 2 * SMOOTH + 1
DEEP = 128
LABEL = 16


def label_kernel(order, pairs, raw, out, keep):
    held = order.shape[1]
    half, channels = raw.shape[1:]
    me = lax.axis_index("ch")
    lanes = lax.broadcasted_iota(jnp.int32, (LABEL, channels), 1)
    row = jnp.zeros((LABEL, channels), jnp.int32)
    for c in range(held):
        row = jnp.where(lanes % held == c, order[0, c], row)
    row = jnp.where(lanes // held == me, row + held * me, 0)
    keep[...] = jnp.broadcast_to(jnp.where(pairs[0, 0] >= 0, 1.0, 0.0), keep.shape)
    out[0, 0:half, :] = raw[0]
    out[0, half : half + LABEL, :] = row.astype(jnp.float32).astype(out.dtype)


def tables_kernel(forward, band_from, inverse_from, fwd, band, inverse, sems):
    half = forward.shape[1] // 2
    mine = lax.axis_index("ch") % 2
    near = forward.at[:, pl.ds(pl.multiple_of(mine * half, half), half)]
    far = forward.at[:, pl.ds(pl.multiple_of((1 - mine) * half, half), half)]
    copies = [
        pltpu.make_async_copy(near, fwd.at[:, 0:half], sems.at[0]),
        pltpu.make_async_copy(far, fwd.at[:, half : 2 * half], sems.at[1]),
        pltpu.make_async_copy(band_from, band, sems.at[2]),
        pltpu.make_async_copy(inverse_from, inverse, sems.at[3]),
    ]
    for copy in copies:
        copy.start()
    for copy in copies:
        copy.wait()


def whiten_group(items, fwd, band, spec, pows, white):
    bins = band.shape[0]
    levels = []
    for i, (first, second, first_next, second_next) in enumerate(items):
        samples = jnp.concatenate(
            [
                jnp.concatenate([first, first_next], axis=1),
                jnp.concatenate([second, second_next], axis=1),
            ],
            axis=0,
        )
        re = jnp.dot(fwd[0:bins, :], samples, preferred_element_type=jnp.float32)
        im = jnp.dot(fwd[bins:, :], samples, preferred_element_type=jnp.float32)
        power = re * re + im * im
        spec[i, 0] = re
        spec[i, 1] = im
        pows[i] = power.astype(jnp.bfloat16)
        levels.append(jnp.sum(power.reshape(bins // 8, 8, 2 * SRC), axis=0))
    blocks, _, rows, _ = white.shape
    kb = bins // blocks
    for i in range(len(items)):
        level = jnp.sum(levels[i], axis=0, keepdims=True) * (0.1 * WIDTH / bins) + 1e-6 * WIDTH
        smoothed = jnp.dot(band[...], pows[i], preferred_element_type=jnp.float32)
        scale = lax.rsqrt(smoothed + level)
        for part in range(2):
            value = spec[i, part] * scale
            left = value[:, 0:SRC].reshape(blocks, kb, SRC)
            right = value[:, SRC:].reshape(blocks, kb, SRC)
            both = jnp.concatenate([left, right], axis=1).astype(jnp.bfloat16)
            white[:, part, 2 * kb * i : 2 * kb * (i + 1), :] = both


def receiver_products(white, select, pick):
    blocks, parts, rows, _ = white.shape
    kb = SEG // blocks
    deep = parts * rows
    lane = lax.broadcasted_iota(jnp.int32, (kb * RECV, deep), 1)
    sub = lax.broadcasted_iota(jnp.int32, (kb * RECV, deep), 0)
    same = (lane % kb == sub % kb).astype(jnp.float32)
    sign = jnp.where(lane < rows, 1.0, -1.0)
    for g in range(0, blocks, 2):
        sources = white[g : g + 2].reshape(2 * deep, SRC)
        both = lax.dot_general(
            select, sources, (((1,), (1,)), ((), ())), preferred_element_type=jnp.float32
        )
        for u in range(2):
            v = both[:, u * deep : (u + 1) * deep] * same
            turned = pltpu.roll(v, rows, 1) * sign
            pick[g + u, 0 : kb * RECV, :] = v.astype(jnp.bfloat16)
            pick[g + u, kb * RECV :, :] = turned.astype(jnp.bfloat16)
    sums = [
        jnp.dot(pick[g], white[g].reshape(deep, SRC), preferred_element_type=jnp.float32)
        for g in range(blocks)
    ]
    return [
        jnp.concatenate([s[at * kb : (at + 1) * kb] for s in sums], axis=0)
        for at in range(2 * RECV)
    ]


def pair_items(first, second, half):
    return [
        (first[z, 0:half], second[z, 0:half], first[z + 1, 0:half], second[z + 1, 0:half])
        for z in range(0, first.shape[0], 2)
    ]


def window_kernel(
    own, near, label, near_label, fwd, band, partial, perm, chosen, white, pick, spec, pows
):
    half = fwd.shape[1] // 2
    zb = own.shape[0]
    ch = lax.axis_index("ch")
    base = (ch * lax.axis_size("grp") + lax.axis_index("grp")) * RECV

    dest = jnp.maximum(label[...], near_label[...])
    dest = dest.astype(jnp.float32)[0:1, :]
    rows = lax.broadcasted_iota(jnp.int32, (SRC, SRC), 0)
    perm[...] = (rows.astype(jnp.float32) == dest).astype(jnp.bfloat16)
    wanted = lax.broadcasted_iota(jnp.int32, chosen.shape, 0) * RECV // chosen.shape[0] + base
    chosen[...] = (wanted.astype(jnp.float32) == dest).astype(jnp.float32)

    whiten_group(pair_items(own, near, half), fwd, band, spec, pows, white)
    for at, value in enumerate(receiver_products(white, chosen[...].astype(jnp.bfloat16), pick)):
        partial[at] = value


def middle_kernel(sib, other, diag, fwd, band, chosen, before, partial, white, pick, spec, pows):
    zb, half = other.shape[0:2]
    items = pair_items(sib.at[0:zb], sib.at[zb : 2 * zb], half) + pair_items(other, diag, half)
    whiten_group(items, fwd, band, spec, pows, white)
    each = RECV * SEG // white.shape[0]
    step = chosen.shape[0] // RECV
    select = jnp.concatenate(
        [chosen[q * step : q * step + each // RECV, :] for q in range(RECV)], axis=0
    )
    for at, value in enumerate(receiver_products(white, select.astype(jnp.bfloat16), pick)):
        partial[at] = before[at] + value


def cross_kernel(
    keep, sib, before, fwd, perm, chosen, band, inverse, out,
    white, pick, cross, lags, blank, spec, pows, sems,
):
    bins = band.shape[0]
    zb, half = sib.shape[0] // 2, sib.shape[1]

    blank[...] = jnp.zeros(blank.shape, blank.dtype)
    copies = [
        pltpu.make_async_copy(blank, out.at[q, pl.ds(1, MAXP - 1)], sems.at[q]) for q in range(RECV)
    ]
    for copy in copies:
        copy.start()

    whiten_group(
        pair_items(sib.at[0:zb], sib.at[zb : 2 * zb], half), fwd, band, spec, pows, white
    )
    for at, value in enumerate(receiver_products(white, chosen[...].astype(jnp.bfloat16), pick)):
        total = (before[at] + value) * (WIDTH / (4 * zb))
        part, q = at // RECV, at % RECV
        cross[q, part * bins : (part + 1) * bins, :] = total.astype(jnp.bfloat16)

    turned = lax.dot_general(
        perm[...],
        cross[...].reshape(RECV * 2 * bins, SRC),
        (((1,), (1,)), ((), ())),
        preferred_element_type=jnp.float32,
    ).astype(jnp.bfloat16)
    for q in range(RECV):
        held = turned[:, q * 2 * bins : (q + 1) * 2 * bins]
        lag_values = jnp.dot(held, inverse[...], preferred_element_type=jnp.float32)
        lags[q] = (lag_values * keep[0:1, :]).astype(jnp.bfloat16)
        copy = pltpu.make_async_copy(lags.at[q], out.at[q, 0], sems.at[RECV + q])
        copy.start()
        copies.append(copy)
    for copy in copies:
        copy.wait()


def one_block(raw, order, pair_blocks):
    groups = lax.axis_size("grp")
    total = lax.axis_size("ch") * groups
    half, channels = raw.shape[1:]
    vmem = pl.BlockSpec(memory_space=pltpu.VMEM)
    smem = pl.BlockSpec(memory_space=pltpu.SMEM)
    params = pltpu.CompilerParams(vmem_limit_bytes=24 * 1024 * 1024)
    dtype = raw.dtype

    block, keep = pl.pallas_call(
        label_kernel,
        out_shape=[pltpu.VMEM((1, half + LABEL, channels), dtype), pltpu.VMEM((8, 2 * SRC), jnp.float32)],
        in_specs=[smem, smem, vmem],
        out_specs=[vmem, vmem],
    )(order, pair_blocks, raw)

    def swap(value, ch_bits, grp_bits):
        flip = ch_bits * groups + grp_bits
        return lax.ppermute(value, ("ch", "grp"), [(d, d ^ flip) for d in range(total)])

    parts = [block, swap(block, 2, 0), swap(block, 6, 0), swap(block, 4, 0)]

    forward, inverse, band = transform_tables(SEG, LAGS, SMOOTH)
    forward, band, inverse = [
        jnp.asarray(np.ascontiguousarray(t), jnp.bfloat16) for t in (forward.T, band, inverse)
    ]
    anywhere = pl.BlockSpec(memory_space=pl.ANY)
    fwd, band, inverse = pl.pallas_call(
        tables_kernel,
        out_shape=[pltpu.VMEM(t.shape, t.dtype) for t in (forward, band, inverse)],
        in_specs=[anywhere] * 3,
        out_specs=[vmem] * 3,
        scratch_shapes=[pltpu.SemaphoreType.DMA((4,))],
    )(forward, band, inverse)
    parts, fwd, band, inverse = lax.optimization_barrier((parts, fwd, band, inverse))
    own = jnp.concatenate([p[0, 0:half] for p in parts], axis=0)
    label = functools.reduce(jnp.maximum, [p[0, half:] for p in parts])
    near = swap(jnp.concatenate([own, label], axis=0), 1, 0)
    diag = swap(own, 1, 2).reshape(-1, half, channels)
    other = swap(own, 0, 2).reshape(-1, half, channels)
    near, near_label = near[: own.shape[0]].reshape(-1, half, channels), near[own.shape[0] :]
    own = own.reshape(-1, half, channels)
    first_sib = swap(jnp.concatenate([own, near], axis=0), 0, 1)

    zb = own.shape[0]

    def scratch(segments):
        kb = DEEP // (2 * segments)
        return [
            pltpu.VMEM((SEG // kb, 2, DEEP // 2, SRC), jnp.bfloat16),
            pltpu.VMEM((SEG // kb, 2 * RECV * kb, DEEP), jnp.bfloat16),
        ], [
            pltpu.VMEM((segments // 2, 2, SEG, 2 * SRC), jnp.float32),
            pltpu.VMEM((segments // 2, SEG, 2 * SRC), jnp.bfloat16),
        ]

    partial = pltpu.VMEM((2 * RECV, SEG, SRC), jnp.float32)
    spectra, work = scratch(zb)
    before, perm, chosen = pl.pallas_call(
        window_kernel,
        out_shape=[
            partial,
            pltpu.VMEM((SRC, SRC), jnp.bfloat16),
            pltpu.VMEM((RECV * DEEP // (2 * zb), SRC), jnp.float32),
        ],
        in_specs=[vmem] * 6,
        out_specs=[vmem] * 3,
        scratch_shapes=[*spectra, *work],
        compiler_params=params,
    )(own, near, label, near_label, fwd, band)
    other, diag, chosen = lax.optimization_barrier((other, diag, chosen))
    second_sib = swap(jnp.concatenate([other, diag], axis=0), 0, 1)
    many_spectra, many_work = scratch(2 * zb)
    before = pl.pallas_call(
        middle_kernel,
        out_shape=partial,
        in_specs=[vmem] * 7,
        out_specs=vmem,
        scratch_shapes=[*many_spectra, *many_work],
        compiler_params=params,
    )(first_sib, other, diag, fwd, band, chosen, before)
    return pl.pallas_call(
        cross_kernel,
        out_shape=jax.ShapeDtypeStruct((RECV, MAXP, SRC, LAGS), jnp.bfloat16),
        in_specs=[vmem] * 8,
        out_specs=pl.BlockSpec(memory_space=pl.ANY),
        scratch_shapes=[
            *spectra,
            pltpu.VMEM((RECV, 2 * SEG, SRC), jnp.bfloat16),
            pltpu.VMEM((RECV, SRC, LAGS), jnp.bfloat16),
            pltpu.VMEM((MAXP - 1, SRC, LAGS), jnp.bfloat16),
            *work,
            pltpu.SemaphoreType.DMA((2 * RECV,)),
        ],
        compiler_params=params,
    )(keep, second_sib, before, fwd, perm, chosen, band, inverse)


def local(raw, order, pair_blocks):
    held = order.shape[1]
    gathered = (
        raw.shape[2] == SRC
        and lax.axis_size("ch") == 8
        and lax.axis_size("grp") == 4
        and raw.shape[0] == 1
        and 2 * raw.shape[1] == SEG
        and held == 4 * RECV
    )
    if gathered:
        return one_block(raw, order, pair_blocks)
    return many_blocks(raw, order, pair_blocks)


def solution(mesh):
    placed = (P("grp", "ch", None), P("ch", None), P("ch", None))
    return jax.shard_map(
        local,
        mesh=mesh,
        in_specs=placed,
        out_specs=P(("ch", "grp"), None, None, None),
        check_vma=False,
    )
```

```python
import functools
import math

import jax
import jax.numpy as jnp
import numpy as np
from jax import lax
from jax.experimental import pallas as pl
from jax.experimental.pallas import tpu as pltpu
from jax.sharding import PartitionSpec as P

SRC = 128
SEG = 256
LAGS = 256
SMOOTH = 8
MAXP = 3
REACH = 15


lag_scale = 1.0 / 16.0


def from_behind(value, axis, steps):
    count = lax.axis_size(axis)
    initial, last = (max(0, -steps), min(count, count - steps))
    return lax.ppermute(value, axis, [(source, source + steps) for source in range(initial, last)])


def transform_tables(half_len, lag_count, smooth_half):
    samples = np.arange(half_len)
    column = np.arange(2 * half_len)
    freq = column % half_len + 1
    angle_fwd = (samples[:, None] * freq[None, :] % (2 * half_len)) * (math.pi / half_len)
    forward = np.where(column[None, :] < half_len, np.cos(angle_fwd), -np.sin(angle_fwd))
    lag_steps = np.arange(lag_count) - lag_count // 2
    angle_inv = (freq[:, None] * lag_steps[None, :] % (2 * half_len)) * (math.pi / half_len)
    inverse = np.where(column[:, None] < half_len, np.cos(angle_inv), -np.sin(angle_inv)) * lag_scale
    bins = np.arange(half_len)
    band = np.abs(bins[:, None] - bins[None, :]) <= smooth_half
    return (forward.astype(np.float32), inverse.astype(np.float32), band.astype(np.float32))


def whiten(segments, forward, band):
    half_len = segments.shape[-1]
    flat_rows = segments.reshape(-1, half_len)
    spectrum = jnp.dot(flat_rows, forward, preferred_element_type=jnp.float32)
    real_part = spectrum[:, :half_len]
    imag_part = spectrum[:, half_len:]
    power_bins = real_part * real_part + imag_part * imag_part
    smoothed = jnp.dot(power_bins, band, precision=lax.Precision.HIGHEST) / (2 * SMOOTH + 1)
    water_level = jnp.mean(power_bins, axis=1, keepdims=True)
    divisor = jnp.sqrt(smoothed + 0.1 * water_level + 1e-06)
    whitened = spectrum / jnp.concatenate([divisor, divisor], axis=1)
    return whitened.astype(jnp.bfloat16).reshape(segments.shape[:-1] + (2 * half_len,))


def correlate(receivers, sources, inverse):
    half_len = receivers.shape[-1] // 2
    seg_count = receivers.shape[1]
    recv_re = receivers[..., :half_len]
    recv_im = receivers[..., half_len:]
    left_first = jnp.concatenate([recv_re, recv_im], axis=1)
    left_second = jnp.concatenate([recv_im, -recv_re], axis=1)
    right_both = jnp.concatenate([sources[..., :half_len], sources[..., half_len:]], axis=1)
    cross_re = jnp.einsum(
        "rnk,snk->rsk", left_first, right_both, preferred_element_type=jnp.float32
    )
    cross_im = jnp.einsum(
        "rnk,snk->rsk", left_second, right_both, preferred_element_type=jnp.float32
    )
    cross_spec = (jnp.concatenate([cross_re, cross_im], axis=2) * (1.0 / seg_count)).astype(
        jnp.bfloat16
    )
    recv_count = receivers.shape[0]
    src_count = sources.shape[0]
    lag_values = jnp.dot(
        cross_spec.reshape(-1, 2 * half_len), inverse, preferred_element_type=jnp.float32
    )
    return lag_values.reshape(recv_count, src_count, inverse.shape[1])


def many_blocks(raw, order, pair_blocks):
    recorded = lax.all_to_all(raw, "ch", split_axis=2, concat_axis=1, tiled=True)
    local_channels = recorded.shape[2]
    onehot = (order[0][:, None] == jnp.arange(local_channels, dtype=jnp.int32)[None, :]).astype(
        jnp.bfloat16
    )
    series = jnp.einsum(
        "ck,tc->kt", onehot, recorded[0], preferred_element_type=jnp.float32
    ).astype(jnp.bfloat16)
    segments = series.reshape(1, local_channels, -1, SEG)
    forward, inverse, band = transform_tables(SEG, LAGS, SMOOTH)
    forward = jnp.asarray(forward, jnp.bfloat16)
    inverse = jnp.asarray(inverse, jnp.bfloat16)
    own_white = whiten(segments, forward, band)
    before_list = []
    for distance in range(REACH, 0, -1):
        before_list.append(from_behind(own_white, "ch", distance))
    after_list = []
    for distance in range(1, REACH + 1):
        after_list.append(from_behind(own_white, "ch", -distance))
    window = jnp.concatenate(before_list + [own_white] + after_list, axis=1)
    window_base = (lax.axis_index("ch") - REACH) * local_channels
    groups = lax.axis_size("grp")
    receivers = own_white[0]
    slot_results = []
    for slot_index in range(MAXP):
        block_id = pair_blocks[0, slot_index]
        source_start = jnp.maximum(block_id, 0) * SRC - window_base
        sources = lax.dynamic_slice_in_dim(window[0], source_start, SRC, 0)
        is_live = (block_id >= 0).astype(jnp.float32)
        lag_values = correlate(receivers, sources, inverse) * is_live
        slot_results.append(lag_values)
    stacked = lax.psum_scatter(
        jnp.stack(slot_results, axis=1).astype(jnp.bfloat16), "grp", scatter_dimension=0, tiled=True
    ).astype(jnp.float32)
    return (stacked / groups).astype(jnp.bfloat16)


RECV = 4
WIDTH = 2 * SMOOTH + 1
DEEP = 256
LABEL = 16


def label_kernel(order, pairs, raw, out, keep):
    held = order.shape[1]
    half, channels = raw.shape[1:]
    me = lax.axis_index("ch")
    lanes = lax.broadcasted_iota(jnp.int32, (LABEL, channels), 1)
    row = jnp.zeros((LABEL, channels), jnp.int32)
    for c in range(held):
        row = jnp.where(lanes % held == c, order[0, c], row)
    row = jnp.where(lanes // held == me, row + held * me, 0)
    keep[...] = jnp.broadcast_to(jnp.where(pairs[0, 0] >= 0, 1.0, 0.0), keep.shape)
    out[0, 0:half, :] = raw[0]
    out[0, half : half + LABEL, :] = row.astype(jnp.float32).astype(out.dtype)


def tables_kernel(forward, band_from, inverse_from, fwd, band, inverse, sems):
    half = forward.shape[1] // 2
    mine = lax.axis_index("ch") % 2
    near = forward.at[:, pl.ds(pl.multiple_of(mine * half, half), half)]
    far = forward.at[:, pl.ds(pl.multiple_of((1 - mine) * half, half), half)]
    copies = [
        pltpu.make_async_copy(near, fwd.at[:, 0:half], sems.at[0]),
        pltpu.make_async_copy(far, fwd.at[:, half : 2 * half], sems.at[1]),
        pltpu.make_async_copy(band_from, band, sems.at[2]),
        pltpu.make_async_copy(inverse_from, inverse, sems.at[3]),
    ]
    for copy in copies:
        copy.start()
    for copy in copies:
        copy.wait()


def whiten_group(items, fwd, band, spec, pows, white):
    bins = band.shape[0]
    levels = []
    for i, (first, second, first_next, second_next) in enumerate(items):
        samples = jnp.concatenate(
            [
                jnp.concatenate([first, first_next], axis=1),
                jnp.concatenate([second, second_next], axis=1),
            ],
            axis=0,
        )
        re = jnp.dot(fwd[0:bins, :], samples, preferred_element_type=jnp.float32)
        im = jnp.dot(fwd[bins:, :], samples, preferred_element_type=jnp.float32)
        power = re * re + im * im
        spec[i, 0] = re
        spec[i, 1] = im
        pows[i] = power.astype(jnp.bfloat16)
        levels.append(jnp.sum(power.reshape(bins // 8, 8, 2 * SRC), axis=0))
    blocks, _, rows, _ = white.shape
    kb = bins // blocks
    for i in range(len(items)):
        level = jnp.sum(levels[i], axis=0, keepdims=True) * (0.1 * WIDTH / bins) + 1e-6 * WIDTH
        smoothed = jnp.dot(band[...], pows[i], preferred_element_type=jnp.float32)
        scale = lax.rsqrt(smoothed + level)
        for part in range(2):
            value = spec[i, part] * scale
            left = value[:, 0:SRC].reshape(blocks, kb, SRC)
            right = value[:, SRC:].reshape(blocks, kb, SRC)
            both = jnp.concatenate([left, right], axis=1).astype(jnp.bfloat16)
            white[:, part, 2 * kb * i : 2 * kb * (i + 1), :] = both


def receiver_products(white, select, pick):
    blocks, parts, rows, _ = white.shape
    kb = SEG // blocks
    deep = parts * rows
    lane = lax.broadcasted_iota(jnp.int32, (kb * RECV, deep), 1)
    sub = lax.broadcasted_iota(jnp.int32, (kb * RECV, deep), 0)
    same = (lane % kb == sub % kb).astype(jnp.float32)
    sign = jnp.where(lane < rows, 1.0, -1.0)
    for g in range(0, blocks, 2):
        sources = white[g : g + 2].reshape(2 * deep, SRC)
        both = lax.dot_general(
            select, sources, (((1,), (1,)), ((), ())), preferred_element_type=jnp.float32
        )
        for u in range(2):
            v = both[:, u * deep : (u + 1) * deep] * same
            turned = pltpu.roll(v, rows, 1) * sign
            pick[g + u, 0 : kb * RECV, :] = v.astype(jnp.bfloat16)
            pick[g + u, kb * RECV :, :] = turned.astype(jnp.bfloat16)
    sums = [
        jnp.dot(pick[g], white[g].reshape(deep, SRC), preferred_element_type=jnp.float32)
        for g in range(blocks)
    ]
    return [
        jnp.concatenate([s[at * kb : (at + 1) * kb] for s in sums], axis=0)
        for at in range(2 * RECV)
    ]


def pair_items(first, second, half):
    return [
        (first[z, 0:half], second[z, 0:half], first[z + 1, 0:half], second[z + 1, 0:half])
        for z in range(0, first.shape[0], 2)
    ]


def window_kernel(
    own, near, label, near_label, fwd, band, partial, perm, chosen, white, pick, spec, pows
):
    half = fwd.shape[1] // 2
    zb = own.shape[0]
    ch = lax.axis_index("ch")
    base = (ch * lax.axis_size("grp") + lax.axis_index("grp")) * RECV

    dest = jnp.maximum(label[...], near_label[...])
    dest = dest.astype(jnp.float32)[0:1, :]
    rows = lax.broadcasted_iota(jnp.int32, (SRC, SRC), 0)
    perm[...] = (rows.astype(jnp.float32) == dest).astype(jnp.bfloat16)
    wanted = lax.broadcasted_iota(jnp.int32, chosen.shape, 0) * RECV // chosen.shape[0] + base
    chosen[...] = (wanted.astype(jnp.float32) == dest).astype(jnp.float32)

    whiten_group(pair_items(own, near, half), fwd, band, spec, pows, white)
    for at, value in enumerate(receiver_products(white, chosen[...].astype(jnp.bfloat16), pick)):
        partial[at] = value


def middle_kernel(sib, other, diag, fwd, band, chosen, before, partial, white, pick, spec, pows):
    zb, half = other.shape[0:2]
    items = pair_items(sib.at[0:zb], sib.at[zb : 2 * zb], half) + pair_items(other, diag, half)
    whiten_group(items, fwd, band, spec, pows, white)
    each = RECV * SEG // white.shape[0]
    step = chosen.shape[0] // RECV
    select = jnp.concatenate(
        [chosen[q * step : q * step + each // RECV, :] for q in range(RECV)], axis=0
    )
    for at, value in enumerate(receiver_products(white, select.astype(jnp.bfloat16), pick)):
        partial[at] = before[at] + value


def cross_kernel(
    keep, sib, before, fwd, perm, chosen, band, inverse, out,
    white, pick, cross, lags, blank, spec, pows, sems,
):
    bins = band.shape[0]
    zb, half = sib.shape[0] // 2, sib.shape[1]

    blank[...] = jnp.zeros(blank.shape, blank.dtype)
    copies = [
        pltpu.make_async_copy(blank, out.at[q, pl.ds(1, MAXP - 1)], sems.at[q]) for q in range(RECV)
    ]
    for copy in copies:
        copy.start()

    whiten_group(
        pair_items(sib.at[0:zb], sib.at[zb : 2 * zb], half), fwd, band, spec, pows, white
    )
    for at, value in enumerate(receiver_products(white, chosen[...].astype(jnp.bfloat16), pick)):
        total = (before[at] + value) * (WIDTH / (4 * zb))
        part, q = at // RECV, at % RECV
        cross[q, part * bins : (part + 1) * bins, :] = total.astype(jnp.bfloat16)

    turned = lax.dot_general(
        perm[...],
        cross[...].reshape(RECV * 2 * bins, SRC),
        (((1,), (1,)), ((), ())),
        preferred_element_type=jnp.float32,
    ).astype(jnp.bfloat16)
    for q in range(RECV):
        held = turned[:, q * 2 * bins : (q + 1) * 2 * bins]
        lag_values = jnp.dot(held, inverse[...], preferred_element_type=jnp.float32)
        lags[q] = (lag_values * keep[0:1, :]).astype(jnp.bfloat16)
        copy = pltpu.make_async_copy(lags.at[q], out.at[q, 0], sems.at[RECV + q])
        copy.start()
        copies.append(copy)
    for copy in copies:
        copy.wait()


def one_block(raw, order, pair_blocks):
    groups = lax.axis_size("grp")
    total = lax.axis_size("ch") * groups
    half, channels = raw.shape[1:]
    vmem = pl.BlockSpec(memory_space=pltpu.VMEM)
    smem = pl.BlockSpec(memory_space=pltpu.SMEM)
    params = pltpu.CompilerParams(vmem_limit_bytes=24 * 1024 * 1024)
    dtype = raw.dtype

    block, keep = pl.pallas_call(
        label_kernel,
        out_shape=[pltpu.VMEM((1, half + LABEL, channels), dtype), pltpu.VMEM((8, 2 * SRC), jnp.float32)],
        in_specs=[smem, smem, vmem],
        out_specs=[vmem, vmem],
    )(order, pair_blocks, raw)

    def swap(value, ch_bits, grp_bits):
        flip = ch_bits * groups + grp_bits
        return lax.ppermute(value, ("ch", "grp"), [(d, d ^ flip) for d in range(total)])

    parts = [block, swap(block, 2, 0), swap(block, 6, 0), swap(block, 4, 0)]

    forward, inverse, band = transform_tables(SEG, LAGS, SMOOTH)
    forward, band, inverse = [
        jnp.asarray(np.ascontiguousarray(t), jnp.bfloat16) for t in (forward.T, band, inverse)
    ]
    anywhere = pl.BlockSpec(memory_space=pl.ANY)
    fwd, band, inverse = pl.pallas_call(
        tables_kernel,
        out_shape=[pltpu.VMEM(t.shape, t.dtype) for t in (forward, band, inverse)],
        in_specs=[anywhere] * 3,
        out_specs=[vmem] * 3,
        scratch_shapes=[pltpu.SemaphoreType.DMA((4,))],
    )(forward, band, inverse)
    own = jnp.concatenate([p[0, 0:half] for p in parts], axis=0)
    label = functools.reduce(jnp.maximum, [p[0, half:] for p in parts])
    near = swap(jnp.concatenate([own, label], axis=0), 1, 0)
    diag = swap(own, 1, 2).reshape(-1, half, channels)
    other = swap(own, 0, 2).reshape(-1, half, channels)
    near, near_label = near[: own.shape[0]].reshape(-1, half, channels), near[own.shape[0] :]
    own = own.reshape(-1, half, channels)
    near, fwd, band, inverse = lax.optimization_barrier((near, fwd, band, inverse))
    first_sib = swap(jnp.concatenate([own, near], axis=0), 0, 1)

    zb = own.shape[0]

    def scratch(segments):
        kb = DEEP // (2 * segments)
        return [
            pltpu.VMEM((SEG // kb, 2, DEEP // 2, SRC), jnp.bfloat16),
            pltpu.VMEM((SEG // kb, 2 * RECV * kb, DEEP), jnp.bfloat16),
        ], [
            pltpu.VMEM((segments // 2, 2, SEG, 2 * SRC), jnp.float32),
            pltpu.VMEM((segments // 2, SEG, 2 * SRC), jnp.bfloat16),
        ]

    partial = pltpu.VMEM((2 * RECV, SEG, SRC), jnp.float32)
    spectra, work = scratch(zb)
    before, perm, chosen = pl.pallas_call(
        window_kernel,
        out_shape=[
            partial,
            pltpu.VMEM((SRC, SRC), jnp.bfloat16),
            pltpu.VMEM((RECV * DEEP // (2 * zb), SRC), jnp.float32),
        ],
        in_specs=[vmem] * 6,
        out_specs=[vmem] * 3,
        scratch_shapes=[*spectra, *work],
        compiler_params=params,
    )(own, near, label, near_label, fwd, band)
    other, diag, chosen = lax.optimization_barrier((other, diag, chosen))
    second_sib = swap(jnp.concatenate([other, diag], axis=0), 0, 1)
    many_spectra, many_work = scratch(2 * zb)
    before = pl.pallas_call(
        middle_kernel,
        out_shape=partial,
        in_specs=[vmem] * 7,
        out_specs=vmem,
        scratch_shapes=[*many_spectra, *many_work],
        compiler_params=params,
    )(first_sib, other, diag, fwd, band, chosen, before)
    return pl.pallas_call(
        cross_kernel,
        out_shape=jax.ShapeDtypeStruct((RECV, MAXP, SRC, LAGS), jnp.bfloat16),
        in_specs=[vmem] * 8,
        out_specs=pl.BlockSpec(memory_space=pl.ANY),
        scratch_shapes=[
            *spectra,
            pltpu.VMEM((RECV, 2 * SEG, SRC), jnp.bfloat16),
            pltpu.VMEM((RECV, SRC, LAGS), jnp.bfloat16),
            pltpu.VMEM((MAXP - 1, SRC, LAGS), jnp.bfloat16),
            *work,
            pltpu.SemaphoreType.DMA((2 * RECV,)),
        ],
        compiler_params=params,
    )(keep, second_sib, before, fwd, perm, chosen, band, inverse)


def local(raw, order, pair_blocks):
    held = order.shape[1]
    gathered = (
        raw.shape[2] == SRC
        and lax.axis_size("ch") == 8
        and lax.axis_size("grp") == 4
        and raw.shape[0] == 1
        and 2 * raw.shape[1] == SEG
        and held == 4 * RECV
    )
    if gathered:
        return one_block(raw, order, pair_blocks)
    return many_blocks(raw, order, pair_blocks)


def solution(mesh):
    placed = (P("grp", "ch", None), P("ch", None), P("ch", None))
    return jax.shard_map(
        local,
        mesh=mesh,
        in_specs=placed,
        out_specs=P(("ch", "grp"), None, None, None),
        check_vma=False,
    )
```

```python
import functools
import math

import jax
import jax.numpy as jnp
import numpy as np
from jax import lax
from jax.experimental import pallas as pl
from jax.experimental.pallas import tpu as pltpu
from jax.sharding import PartitionSpec as P

SRC = 128
SEG = 256
LAGS = 256
SMOOTH = 8
MAXP = 3
REACH = 15


lag_scale = 1.0 / 16.0


def from_behind(value, axis, steps):
    count = lax.axis_size(axis)
    initial, last = (max(0, -steps), min(count, count - steps))
    return lax.ppermute(value, axis, [(source, source + steps) for source in range(initial, last)])


def transform_tables(half_len, lag_count, smooth_half):
    samples = np.arange(half_len)
    column = np.arange(2 * half_len)
    freq = column % half_len + 1
    angle_fwd = (samples[:, None] * freq[None, :] % (2 * half_len)) * (math.pi / half_len)
    forward = np.where(column[None, :] < half_len, np.cos(angle_fwd), -np.sin(angle_fwd))
    lag_steps = np.arange(lag_count) - lag_count // 2
    angle_inv = (freq[:, None] * lag_steps[None, :] % (2 * half_len)) * (math.pi / half_len)
    inverse = np.where(column[:, None] < half_len, np.cos(angle_inv), -np.sin(angle_inv)) * lag_scale
    bins = np.arange(half_len)
    band = np.abs(bins[:, None] - bins[None, :]) <= smooth_half
    return (forward.astype(np.float32), inverse.astype(np.float32), band.astype(np.float32))


def whiten(segments, forward, band):
    half_len = segments.shape[-1]
    flat_rows = segments.reshape(-1, half_len)
    spectrum = jnp.dot(flat_rows, forward, preferred_element_type=jnp.float32)
    real_part = spectrum[:, :half_len]
    imag_part = spectrum[:, half_len:]
    power_bins = real_part * real_part + imag_part * imag_part
    smoothed = jnp.dot(power_bins, band, precision=lax.Precision.HIGHEST) / (2 * SMOOTH + 1)
    water_level = jnp.mean(power_bins, axis=1, keepdims=True)
    divisor = jnp.sqrt(smoothed + 0.1 * water_level + 1e-06)
    whitened = spectrum / jnp.concatenate([divisor, divisor], axis=1)
    return whitened.astype(jnp.bfloat16).reshape(segments.shape[:-1] + (2 * half_len,))


def correlate(receivers, sources, inverse):
    half_len = receivers.shape[-1] // 2
    seg_count = receivers.shape[1]
    recv_re = receivers[..., :half_len]
    recv_im = receivers[..., half_len:]
    left_first = jnp.concatenate([recv_re, recv_im], axis=1)
    left_second = jnp.concatenate([recv_im, -recv_re], axis=1)
    right_both = jnp.concatenate([sources[..., :half_len], sources[..., half_len:]], axis=1)
    cross_re = jnp.einsum(
        "rnk,snk->rsk", left_first, right_both, preferred_element_type=jnp.float32
    )
    cross_im = jnp.einsum(
        "rnk,snk->rsk", left_second, right_both, preferred_element_type=jnp.float32
    )
    cross_spec = (jnp.concatenate([cross_re, cross_im], axis=2) * (1.0 / seg_count)).astype(
        jnp.bfloat16
    )
    recv_count = receivers.shape[0]
    src_count = sources.shape[0]
    lag_values = jnp.dot(
        cross_spec.reshape(-1, 2 * half_len), inverse, preferred_element_type=jnp.float32
    )
    return lag_values.reshape(recv_count, src_count, inverse.shape[1])


def many_blocks(raw, order, pair_blocks):
    recorded = lax.all_to_all(raw, "ch", split_axis=2, concat_axis=1, tiled=True)
    local_channels = recorded.shape[2]
    onehot = (order[0][:, None] == jnp.arange(local_channels, dtype=jnp.int32)[None, :]).astype(
        jnp.bfloat16
    )
    series = jnp.einsum(
        "ck,tc->kt", onehot, recorded[0], preferred_element_type=jnp.float32
    ).astype(jnp.bfloat16)
    segments = series.reshape(1, local_channels, -1, SEG)
    forward, inverse, band = transform_tables(SEG, LAGS, SMOOTH)
    forward = jnp.asarray(forward, jnp.bfloat16)
    inverse = jnp.asarray(inverse, jnp.bfloat16)
    own_white = whiten(segments, forward, band)
    before_list = []
    for distance in range(REACH, 0, -1):
        before_list.append(from_behind(own_white, "ch", distance))
    after_list = []
    for distance in range(1, REACH + 1):
        after_list.append(from_behind(own_white, "ch", -distance))
    window = jnp.concatenate(before_list + [own_white] + after_list, axis=1)
    window_base = (lax.axis_index("ch") - REACH) * local_channels
    groups = lax.axis_size("grp")
    receivers = own_white[0]
    slot_results = []
    for slot_index in range(MAXP):
        block_id = pair_blocks[0, slot_index]
        source_start = jnp.maximum(block_id, 0) * SRC - window_base
        sources = lax.dynamic_slice_in_dim(window[0], source_start, SRC, 0)
        is_live = (block_id >= 0).astype(jnp.float32)
        lag_values = correlate(receivers, sources, inverse) * is_live
        slot_results.append(lag_values)
    stacked = lax.psum_scatter(
        jnp.stack(slot_results, axis=1).astype(jnp.bfloat16), "grp", scatter_dimension=0, tiled=True
    ).astype(jnp.float32)
    return (stacked / groups).astype(jnp.bfloat16)


RECV = 4
WIDTH = 2 * SMOOTH + 1
DEEP = 256
LABEL = 16


def label_kernel(order, pairs, raw, out, keep):
    held = order.shape[1]
    half, channels = raw.shape[1:]
    me = lax.axis_index("ch")
    lanes = lax.broadcasted_iota(jnp.int32, (LABEL, channels), 1)
    row = jnp.zeros((LABEL, channels), jnp.int32)
    for c in range(held):
        row = jnp.where(lanes % held == c, order[0, c], row)
    row = jnp.where(lanes // held == me, row + held * me, 0)
    keep[...] = jnp.broadcast_to(jnp.where(pairs[0, 0] >= 0, 1.0, 0.0), keep.shape)
    out[0, 0:half, :] = raw[0]
    out[0, half : half + LABEL, :] = row.astype(jnp.float32).astype(out.dtype)


def tables_kernel(forward, band_from, inverse_from, fwd, band, inverse, sems):
    half = forward.shape[1] // 2
    mine = lax.axis_index("ch") % 2
    near = forward.at[:, pl.ds(pl.multiple_of(mine * half, half), half)]
    far = forward.at[:, pl.ds(pl.multiple_of((1 - mine) * half, half), half)]
    copies = [
        pltpu.make_async_copy(near, fwd.at[:, 0:half], sems.at[0]),
        pltpu.make_async_copy(far, fwd.at[:, half : 2 * half], sems.at[1]),
        pltpu.make_async_copy(band_from, band, sems.at[2]),
        pltpu.make_async_copy(inverse_from, inverse, sems.at[3]),
    ]
    for copy in copies:
        copy.start()
    for copy in copies:
        copy.wait()


def whiten_group(items, fwd, band, spec, pows, white):
    bins = band.shape[0]
    levels = []
    for i, (first, second, first_next, second_next) in enumerate(items):
        samples = jnp.concatenate(
            [
                jnp.concatenate([first, first_next], axis=1),
                jnp.concatenate([second, second_next], axis=1),
            ],
            axis=0,
        )
        re = jnp.dot(fwd[0:bins, :], samples, preferred_element_type=jnp.float32)
        im = jnp.dot(fwd[bins:, :], samples, preferred_element_type=jnp.float32)
        power = re * re + im * im
        spec[i, 0] = re
        spec[i, 1] = im
        pows[i] = power.astype(jnp.bfloat16)
        levels.append(jnp.sum(power.reshape(bins // 8, 8, 2 * SRC), axis=0))
    blocks, _, rows, _ = white.shape
    kb = bins // blocks
    for i in range(len(items)):
        level = jnp.sum(levels[i], axis=0, keepdims=True) * (0.1 * WIDTH / bins) + 1e-6 * WIDTH
        smoothed = jnp.dot(band[...], pows[i], preferred_element_type=jnp.float32)
        scale = lax.rsqrt(smoothed + level)
        for part in range(2):
            value = spec[i, part] * scale
            left = value[:, 0:SRC].reshape(blocks, kb, SRC)
            right = value[:, SRC:].reshape(blocks, kb, SRC)
            both = jnp.concatenate([left, right], axis=1).astype(jnp.bfloat16)
            white[:, part, 2 * kb * i : 2 * kb * (i + 1), :] = both


def receiver_products(white, select, pick):
    blocks, parts, rows, _ = white.shape
    kb = SEG // blocks
    deep = parts * rows
    lane = lax.broadcasted_iota(jnp.int32, (kb * RECV, deep), 1)
    sub = lax.broadcasted_iota(jnp.int32, (kb * RECV, deep), 0)
    same = (lane % kb == sub % kb).astype(jnp.float32)
    sign = jnp.where(lane < rows, 1.0, -1.0)
    for g in range(0, blocks, 2):
        sources = white[g : g + 2].reshape(2 * deep, SRC)
        both = lax.dot_general(
            select, sources, (((1,), (1,)), ((), ())), preferred_element_type=jnp.float32
        )
        for u in range(2):
            v = both[:, u * deep : (u + 1) * deep] * same
            turned = pltpu.roll(v, rows, 1) * sign
            pick[g + u, 0 : kb * RECV, :] = v.astype(jnp.bfloat16)
            pick[g + u, kb * RECV :, :] = turned.astype(jnp.bfloat16)
    sums = [
        jnp.dot(pick[g], white[g].reshape(deep, SRC), preferred_element_type=jnp.float32)
        for g in range(blocks)
    ]
    return [
        jnp.concatenate([s[at * kb : (at + 1) * kb] for s in sums], axis=0)
        for at in range(2 * RECV)
    ]


def pair_items(first, second, half):
    return [
        (first[z, 0:half], second[z, 0:half], first[z + 1, 0:half], second[z + 1, 0:half])
        for z in range(0, first.shape[0], 2)
    ]


def window_kernel(
    own, near, label, near_label, fwd, band, partial, perm, chosen, white, pick, spec, pows
):
    half = fwd.shape[1] // 2
    zb = own.shape[0]
    ch = lax.axis_index("ch")
    base = (ch * lax.axis_size("grp") + lax.axis_index("grp")) * RECV

    dest = jnp.maximum(label[...], near_label[...])
    dest = dest.astype(jnp.float32)[0:1, :]
    rows = lax.broadcasted_iota(jnp.int32, (SRC, SRC), 0)
    perm[...] = (rows.astype(jnp.float32) == dest).astype(jnp.bfloat16)
    wanted = lax.broadcasted_iota(jnp.int32, chosen.shape, 0) * RECV // chosen.shape[0] + base
    chosen[...] = (wanted.astype(jnp.float32) == dest).astype(jnp.float32)

    whiten_group(pair_items(own, near, half), fwd, band, spec, pows, white)
    for at, value in enumerate(receiver_products(white, chosen[...].astype(jnp.bfloat16), pick)):
        partial[at] = value


def middle_kernel(sib, other, diag, fwd, band, chosen, before, partial, white, pick, spec, pows):
    zb, half = other.shape[0:2]
    items = pair_items(sib.at[0:zb], sib.at[zb : 2 * zb], half) + pair_items(other, diag, half)
    whiten_group(items, fwd, band, spec, pows, white)
    each = RECV * SEG // white.shape[0]
    step = chosen.shape[0] // RECV
    select = jnp.concatenate(
        [chosen[q * step : q * step + each // RECV, :] for q in range(RECV)], axis=0
    )
    for at, value in enumerate(receiver_products(white, select.astype(jnp.bfloat16), pick)):
        partial[at] = before[at] + value


def cross_kernel(
    keep, sib, before, fwd, perm, chosen, band, inverse, out,
    white, pick, cross, lags, blank, spec, pows, sems,
):
    bins = band.shape[0]
    zb, half = sib.shape[0] // 2, sib.shape[1]

    blank[...] = jnp.zeros(blank.shape, blank.dtype)
    copies = [
        pltpu.make_async_copy(blank, out.at[q, pl.ds(1, MAXP - 1)], sems.at[q]) for q in range(RECV)
    ]
    for copy in copies:
        copy.start()

    whiten_group(
        pair_items(sib.at[0:zb], sib.at[zb : 2 * zb], half), fwd, band, spec, pows, white
    )
    for at, value in enumerate(receiver_products(white, chosen[...].astype(jnp.bfloat16), pick)):
        total = (before[at] + value) * (WIDTH / (4 * zb))
        part, q = at // RECV, at % RECV
        cross[q, part * bins : (part + 1) * bins, :] = total.astype(jnp.bfloat16)

    turned = lax.dot_general(
        perm[...],
        cross[...].reshape(RECV * 2 * bins, SRC),
        (((1,), (1,)), ((), ())),
        preferred_element_type=jnp.float32,
    ).astype(jnp.bfloat16)
    for q in range(RECV):
        held = turned[:, q * 2 * bins : (q + 1) * 2 * bins]
        lag_values = jnp.dot(held, inverse[...], preferred_element_type=jnp.float32)
        lags[q] = (lag_values * keep[0:1, :]).astype(jnp.bfloat16)
        copy = pltpu.make_async_copy(lags.at[q], out.at[q, 0], sems.at[RECV + q])
        copy.start()
        copies.append(copy)
    for copy in copies:
        copy.wait()


def one_block(raw, order, pair_blocks):
    groups = lax.axis_size("grp")
    total = lax.axis_size("ch") * groups
    half, channels = raw.shape[1:]
    vmem = pl.BlockSpec(memory_space=pltpu.VMEM)
    smem = pl.BlockSpec(memory_space=pltpu.SMEM)
    params = pltpu.CompilerParams(vmem_limit_bytes=24 * 1024 * 1024)
    dtype = raw.dtype

    block, keep = pl.pallas_call(
        label_kernel,
        out_shape=[pltpu.VMEM((1, half + LABEL, channels), dtype), pltpu.VMEM((8, 2 * SRC), jnp.float32)],
        in_specs=[smem, smem, vmem],
        out_specs=[vmem, vmem],
    )(order, pair_blocks, raw)

    def swap(value, ch_bits, grp_bits):
        flip = ch_bits * groups + grp_bits
        return lax.ppermute(value, ("ch", "grp"), [(d, d ^ flip) for d in range(total)])

    parts = [block, swap(block, 2, 0), swap(block, 6, 0), swap(block, 4, 0)]

    forward, inverse, band = transform_tables(SEG, LAGS, SMOOTH)
    forward, band, inverse = [
        jnp.asarray(np.ascontiguousarray(t), jnp.bfloat16) for t in (forward.T, band, inverse)
    ]
    anywhere = pl.BlockSpec(memory_space=pl.ANY)
    fwd, band, inverse = pl.pallas_call(
        tables_kernel,
        out_shape=[pltpu.VMEM(t.shape, t.dtype) for t in (forward, band, inverse)],
        in_specs=[anywhere] * 3,
        out_specs=[vmem] * 3,
        scratch_shapes=[pltpu.SemaphoreType.DMA((4,))],
    )(forward, band, inverse)
    near_1 = swap(block[0, 0:half], 1, 0)
    own = jnp.concatenate([p[0, 0:half] for p in parts], axis=0)
    label = functools.reduce(jnp.maximum, [p[0, half:] for p in parts])
    near = jnp.concatenate([near_1, swap(jnp.concatenate([own[half:], label], axis=0), 1, 0)], axis=0)
    diag = swap(own, 1, 2).reshape(-1, half, channels)
    other = swap(own, 0, 2).reshape(-1, half, channels)
    near, near_label = near[: own.shape[0]].reshape(-1, half, channels), near[own.shape[0] :]
    own = own.reshape(-1, half, channels)
    near, fwd, band, inverse = lax.optimization_barrier((near, fwd, band, inverse))
    first_sib = swap(jnp.concatenate([own, near], axis=0), 0, 1)

    zb = own.shape[0]

    def scratch(segments):
        kb = DEEP // (2 * segments)
        return [
            pltpu.VMEM((SEG // kb, 2, DEEP // 2, SRC), jnp.bfloat16),
            pltpu.VMEM((SEG // kb, 2 * RECV * kb, DEEP), jnp.bfloat16),
        ], [
            pltpu.VMEM((segments // 2, 2, SEG, 2 * SRC), jnp.float32),
            pltpu.VMEM((segments // 2, SEG, 2 * SRC), jnp.bfloat16),
        ]

    partial = pltpu.VMEM((2 * RECV, SEG, SRC), jnp.float32)
    spectra, work = scratch(zb)
    before, perm, chosen = pl.pallas_call(
        window_kernel,
        out_shape=[
            partial,
            pltpu.VMEM((SRC, SRC), jnp.bfloat16),
            pltpu.VMEM((RECV * DEEP // (2 * zb), SRC), jnp.float32),
        ],
        in_specs=[vmem] * 6,
        out_specs=[vmem] * 3,
        scratch_shapes=[*spectra, *work],
        compiler_params=params,
    )(own, near, label, near_label, fwd, band)
    other, diag, chosen = lax.optimization_barrier((other, diag, chosen))
    second_sib = swap(jnp.concatenate([other, diag], axis=0), 0, 1)
    many_spectra, many_work = scratch(2 * zb)
    before = pl.pallas_call(
        middle_kernel,
        out_shape=partial,
        in_specs=[vmem] * 7,
        out_specs=vmem,
        scratch_shapes=[*many_spectra, *many_work],
        compiler_params=params,
    )(first_sib, other, diag, fwd, band, chosen, before)
    return pl.pallas_call(
        cross_kernel,
        out_shape=jax.ShapeDtypeStruct((RECV, MAXP, SRC, LAGS), jnp.bfloat16),
        in_specs=[vmem] * 8,
        out_specs=pl.BlockSpec(memory_space=pl.ANY),
        scratch_shapes=[
            *spectra,
            pltpu.VMEM((RECV, 2 * SEG, SRC), jnp.bfloat16),
            pltpu.VMEM((RECV, SRC, LAGS), jnp.bfloat16),
            pltpu.VMEM((MAXP - 1, SRC, LAGS), jnp.bfloat16),
            *work,
            pltpu.SemaphoreType.DMA((2 * RECV,)),
        ],
        compiler_params=params,
    )(keep, second_sib, before, fwd, perm, chosen, band, inverse)


def local(raw, order, pair_blocks):
    held = order.shape[1]
    gathered = (
        raw.shape[2] == SRC
        and lax.axis_size("ch") == 8
        and lax.axis_size("grp") == 4
        and raw.shape[0] == 1
        and 2 * raw.shape[1] == SEG
        and held == 4 * RECV
    )
    if gathered:
        return one_block(raw, order, pair_blocks)
    return many_blocks(raw, order, pair_blocks)


def solution(mesh):
    placed = (P("grp", "ch", None), P("ch", None), P("ch", None))
    return jax.shard_map(
        local,
        mesh=mesh,
        in_specs=placed,
        out_specs=P(("ch", "grp"), None, None, None),
        check_vma=False,
    )
```

```python
import functools
import math

import jax
import jax.numpy as jnp
import numpy as np
from jax import lax
from jax.experimental import pallas as pl
from jax.experimental.pallas import tpu as pltpu
from jax.sharding import PartitionSpec as P

SRC = 128
SEG = 256
LAGS = 256
SMOOTH = 8
MAXP = 3
REACH = 15


lag_scale = 1.0 / 16.0


def from_behind(value, axis, steps):
    count = lax.axis_size(axis)
    initial, last = (max(0, -steps), min(count, count - steps))
    return lax.ppermute(value, axis, [(source, source + steps) for source in range(initial, last)])


def transform_tables(half_len, lag_count, smooth_half):
    samples = np.arange(half_len)
    column = np.arange(2 * half_len)
    freq = column % half_len + 1
    angle_fwd = (samples[:, None] * freq[None, :] % (2 * half_len)) * (math.pi / half_len)
    forward = np.where(column[None, :] < half_len, np.cos(angle_fwd), -np.sin(angle_fwd))
    lag_steps = np.arange(lag_count) - lag_count // 2
    angle_inv = (freq[:, None] * lag_steps[None, :] % (2 * half_len)) * (math.pi / half_len)
    inverse = np.where(column[:, None] < half_len, np.cos(angle_inv), -np.sin(angle_inv)) * lag_scale
    bins = np.arange(half_len)
    band = np.abs(bins[:, None] - bins[None, :]) <= smooth_half
    return (forward.astype(np.float32), inverse.astype(np.float32), band.astype(np.float32))


def whiten(segments, forward, band):
    half_len = segments.shape[-1]
    flat_rows = segments.reshape(-1, half_len)
    spectrum = jnp.dot(flat_rows, forward, preferred_element_type=jnp.float32)
    real_part = spectrum[:, :half_len]
    imag_part = spectrum[:, half_len:]
    power_bins = real_part * real_part + imag_part * imag_part
    smoothed = jnp.dot(power_bins, band, precision=lax.Precision.HIGHEST) / (2 * SMOOTH + 1)
    water_level = jnp.mean(power_bins, axis=1, keepdims=True)
    divisor = jnp.sqrt(smoothed + 0.1 * water_level + 1e-06)
    whitened = spectrum / jnp.concatenate([divisor, divisor], axis=1)
    return whitened.astype(jnp.bfloat16).reshape(segments.shape[:-1] + (2 * half_len,))


def correlate(receivers, sources, inverse):
    half_len = receivers.shape[-1] // 2
    seg_count = receivers.shape[1]
    recv_re = receivers[..., :half_len]
    recv_im = receivers[..., half_len:]
    left_first = jnp.concatenate([recv_re, recv_im], axis=1)
    left_second = jnp.concatenate([recv_im, -recv_re], axis=1)
    right_both = jnp.concatenate([sources[..., :half_len], sources[..., half_len:]], axis=1)
    cross_re = jnp.einsum(
        "rnk,snk->rsk", left_first, right_both, preferred_element_type=jnp.float32
    )
    cross_im = jnp.einsum(
        "rnk,snk->rsk", left_second, right_both, preferred_element_type=jnp.float32
    )
    cross_spec = (jnp.concatenate([cross_re, cross_im], axis=2) * (1.0 / seg_count)).astype(
        jnp.bfloat16
    )
    recv_count = receivers.shape[0]
    src_count = sources.shape[0]
    lag_values = jnp.dot(
        cross_spec.reshape(-1, 2 * half_len), inverse, preferred_element_type=jnp.float32
    )
    return lag_values.reshape(recv_count, src_count, inverse.shape[1])


def many_blocks(raw, order, pair_blocks):
    recorded = lax.all_to_all(raw, "ch", split_axis=2, concat_axis=1, tiled=True)
    local_channels = recorded.shape[2]
    onehot = (order[0][:, None] == jnp.arange(local_channels, dtype=jnp.int32)[None, :]).astype(
        jnp.bfloat16
    )
    series = jnp.einsum(
        "ck,tc->kt", onehot, recorded[0], preferred_element_type=jnp.float32
    ).astype(jnp.bfloat16)
    segments = series.reshape(1, local_channels, -1, SEG)
    forward, inverse, band = transform_tables(SEG, LAGS, SMOOTH)
    forward = jnp.asarray(forward, jnp.bfloat16)
    inverse = jnp.asarray(inverse, jnp.bfloat16)
    own_white = whiten(segments, forward, band)
    before_list = []
    for distance in range(REACH, 0, -1):
        before_list.append(from_behind(own_white, "ch", distance))
    after_list = []
    for distance in range(1, REACH + 1):
        after_list.append(from_behind(own_white, "ch", -distance))
    window = jnp.concatenate(before_list + [own_white] + after_list, axis=1)
    window_base = (lax.axis_index("ch") - REACH) * local_channels
    groups = lax.axis_size("grp")
    receivers = own_white[0]
    slot_results = []
    for slot_index in range(MAXP):
        block_id = pair_blocks[0, slot_index]
        source_start = jnp.maximum(block_id, 0) * SRC - window_base
        sources = lax.dynamic_slice_in_dim(window[0], source_start, SRC, 0)
        is_live = (block_id >= 0).astype(jnp.float32)
        lag_values = correlate(receivers, sources, inverse) * is_live
        slot_results.append(lag_values)
    stacked = lax.psum_scatter(
        jnp.stack(slot_results, axis=1).astype(jnp.bfloat16), "grp", scatter_dimension=0, tiled=True
    ).astype(jnp.float32)
    return (stacked / groups).astype(jnp.bfloat16)


RECV = 4
WIDTH = 2 * SMOOTH + 1
DEEP = 256
LABEL = 16


def label_kernel(order, pairs, raw, out, keep):
    held = order.shape[1]
    half, channels = raw.shape[1:]
    me = lax.axis_index("ch")
    lanes = lax.broadcasted_iota(jnp.int32, (LABEL, channels), 1)
    row = jnp.zeros((LABEL, channels), jnp.int32)
    for c in range(held):
        row = jnp.where(lanes % held == c, order[0, c], row)
    row = jnp.where(lanes // held == me, row + held * me, 0)
    keep[...] = jnp.broadcast_to(jnp.where(pairs[0, 0] >= 0, 1.0, 0.0), keep.shape)
    out[0, 0:half, :] = raw[0]
    out[0, half : half + LABEL, :] = row.astype(jnp.float32).astype(out.dtype)


def tables_kernel(forward, band_from, inverse_from, fwd, band, inverse, sems):
    half = forward.shape[1] // 2
    mine = lax.axis_index("ch") % 2
    near = forward.at[:, pl.ds(pl.multiple_of(mine * half, half), half)]
    far = forward.at[:, pl.ds(pl.multiple_of((1 - mine) * half, half), half)]
    copies = [
        pltpu.make_async_copy(near, fwd.at[:, 0:half], sems.at[0]),
        pltpu.make_async_copy(far, fwd.at[:, half : 2 * half], sems.at[1]),
        pltpu.make_async_copy(band_from, band, sems.at[2]),
        pltpu.make_async_copy(inverse_from, inverse, sems.at[3]),
    ]
    for copy in copies:
        copy.start()
    for copy in copies:
        copy.wait()


def whiten_group(items, fwd, band, spec, pows, white):
    bins = band.shape[0]
    levels = []
    for i, (first, second, first_next, second_next) in enumerate(items):
        samples = jnp.concatenate(
            [
                jnp.concatenate([first, first_next], axis=1),
                jnp.concatenate([second, second_next], axis=1),
            ],
            axis=0,
        )
        re = jnp.dot(fwd[0:bins, :], samples, preferred_element_type=jnp.float32)
        im = jnp.dot(fwd[bins:, :], samples, preferred_element_type=jnp.float32)
        power = re * re + im * im
        spec[i, 0] = re
        spec[i, 1] = im
        pows[i] = power.astype(jnp.bfloat16)
        levels.append(jnp.sum(power.reshape(bins // 8, 8, 2 * SRC), axis=0))
    blocks, _, rows, _ = white.shape
    kb = bins // blocks
    for i in range(len(items)):
        level = jnp.sum(levels[i], axis=0, keepdims=True) * (0.1 * WIDTH / bins) + 1e-6 * WIDTH
        smoothed = jnp.dot(band[...], pows[i], preferred_element_type=jnp.float32)
        scale = lax.rsqrt(smoothed + level)
        for part in range(2):
            value = spec[i, part] * scale
            left = value[:, 0:SRC].reshape(blocks, kb, SRC)
            right = value[:, SRC:].reshape(blocks, kb, SRC)
            both = jnp.concatenate([left, right], axis=1).astype(jnp.bfloat16)
            white[:, part, 2 * kb * i : 2 * kb * (i + 1), :] = both


def receiver_products(white, select):
    blocks, parts, rows, _ = white.shape
    kb = SEG // blocks
    deep = parts * rows
    lane = lax.broadcasted_iota(jnp.int32, (kb * RECV, deep), 1)
    sub = lax.broadcasted_iota(jnp.int32, (kb * RECV, deep), 0)
    same = (lane % kb == sub % kb).astype(jnp.float32)
    sign = jnp.where(lane < rows, 1.0, -1.0)
    picks = []
    for g in range(0, blocks, 2):
        sources = white[g : g + 2].reshape(2 * deep, SRC)
        both = lax.dot_general(
            select, sources, (((1,), (1,)), ((), ())), preferred_element_type=jnp.float32
        )
        for u in range(2):
            v = both[:, u * deep : (u + 1) * deep] * same
            turned = pltpu.roll(v, rows, 1) * sign
            picks.append(
                jnp.concatenate([v.astype(jnp.bfloat16), turned.astype(jnp.bfloat16)], axis=0)
            )
    sums = [
        jnp.dot(picks[g], white[g].reshape(deep, SRC), preferred_element_type=jnp.float32)
        for g in range(blocks)
    ]
    return [
        jnp.concatenate([s[at * kb : (at + 1) * kb] for s in sums], axis=0)
        for at in range(2 * RECV)
    ]


def pair_items(first, second, half):
    return [
        (first[z, 0:half], second[z, 0:half], first[z + 1, 0:half], second[z + 1, 0:half])
        for z in range(0, first.shape[0], 2)
    ]


def window_kernel(
    own, near, label, near_label, fwd, band, partial, perm, chosen, white, spec, pows
):
    half = fwd.shape[1] // 2
    zb = own.shape[0]
    ch = lax.axis_index("ch")
    base = (ch * lax.axis_size("grp") + lax.axis_index("grp")) * RECV

    dest = jnp.maximum(label[...], near_label[...])
    dest = dest.astype(jnp.float32)[0:1, :]
    rows = lax.broadcasted_iota(jnp.int32, (SRC, SRC), 0)
    perm[...] = (rows.astype(jnp.float32) == dest).astype(jnp.bfloat16)
    wanted = lax.broadcasted_iota(jnp.int32, chosen.shape, 0) * RECV // chosen.shape[0] + base
    chosen[...] = (wanted.astype(jnp.float32) == dest).astype(jnp.float32)

    whiten_group(pair_items(own, near, half), fwd, band, spec, pows, white)
    for at, value in enumerate(receiver_products(white, chosen[...].astype(jnp.bfloat16))):
        partial[at] = value


def middle_kernel(sib, other, diag, fwd, band, chosen, before, partial, white, spec, pows):
    zb, half = other.shape[0:2]
    items = pair_items(sib.at[0:zb], sib.at[zb : 2 * zb], half) + pair_items(other, diag, half)
    whiten_group(items, fwd, band, spec, pows, white)
    each = RECV * SEG // white.shape[0]
    step = chosen.shape[0] // RECV
    select = jnp.concatenate(
        [chosen[q * step : q * step + each // RECV, :] for q in range(RECV)], axis=0
    )
    for at, value in enumerate(receiver_products(white, select.astype(jnp.bfloat16))):
        partial[at] = before[at] + value


def cross_kernel(
    keep, sib, before, fwd, perm, chosen, band, inverse, out,
    white, cross, lags, blank, spec, pows, sems,
):
    bins = band.shape[0]
    zb, half = sib.shape[0] // 2, sib.shape[1]

    blank[...] = jnp.zeros(blank.shape, blank.dtype)
    copies = [
        pltpu.make_async_copy(blank, out.at[q, pl.ds(1, MAXP - 1)], sems.at[q]) for q in range(RECV)
    ]
    for copy in copies:
        copy.start()

    whiten_group(
        pair_items(sib.at[0:zb], sib.at[zb : 2 * zb], half), fwd, band, spec, pows, white
    )
    for at, value in enumerate(receiver_products(white, chosen[...].astype(jnp.bfloat16))):
        total = (before[at] + value) * (WIDTH / (4 * zb))
        part, q = at // RECV, at % RECV
        cross[q, part * bins : (part + 1) * bins, :] = total.astype(jnp.bfloat16)

    turned = lax.dot_general(
        perm[...],
        cross[...].reshape(RECV * 2 * bins, SRC),
        (((1,), (1,)), ((), ())),
        preferred_element_type=jnp.float32,
    ).astype(jnp.bfloat16)
    for q in range(RECV):
        held = turned[:, q * 2 * bins : (q + 1) * 2 * bins]
        lag_values = jnp.dot(held, inverse[...], preferred_element_type=jnp.float32)
        lags[q] = (lag_values * keep[0:1, :]).astype(jnp.bfloat16)
        copy = pltpu.make_async_copy(lags.at[q], out.at[q, 0], sems.at[RECV + q])
        copy.start()
        copies.append(copy)
    for copy in copies:
        copy.wait()


def one_block(raw, order, pair_blocks):
    groups = lax.axis_size("grp")
    total = lax.axis_size("ch") * groups
    half, channels = raw.shape[1:]
    vmem = pl.BlockSpec(memory_space=pltpu.VMEM)
    smem = pl.BlockSpec(memory_space=pltpu.SMEM)
    params = pltpu.CompilerParams(vmem_limit_bytes=24 * 1024 * 1024)
    dtype = raw.dtype

    block, keep = pl.pallas_call(
        label_kernel,
        out_shape=[pltpu.VMEM((1, half + LABEL, channels), dtype), pltpu.VMEM((8, 2 * SRC), jnp.float32)],
        in_specs=[smem, smem, vmem],
        out_specs=[vmem, vmem],
    )(order, pair_blocks, raw)

    def swap(value, ch_bits, grp_bits):
        flip = ch_bits * groups + grp_bits
        return lax.ppermute(value, ("ch", "grp"), [(d, d ^ flip) for d in range(total)])

    parts = [block, swap(block, 2, 0), swap(block, 6, 0), swap(block, 4, 0)]

    forward, inverse, band = transform_tables(SEG, LAGS, SMOOTH)
    forward, band, inverse = [
        jnp.asarray(np.ascontiguousarray(t), jnp.bfloat16) for t in (forward.T, band, inverse)
    ]
    anywhere = pl.BlockSpec(memory_space=pl.ANY)
    fwd, band, inverse = pl.pallas_call(
        tables_kernel,
        out_shape=[pltpu.VMEM(t.shape, t.dtype) for t in (forward, band, inverse)],
        in_specs=[anywhere] * 3,
        out_specs=[vmem] * 3,
        scratch_shapes=[pltpu.SemaphoreType.DMA((4,))],
    )(forward, band, inverse)
    near_1 = swap(block[0, 0:half], 1, 0)
    own = jnp.concatenate([p[0, 0:half] for p in parts], axis=0)
    label = functools.reduce(jnp.maximum, [p[0, half:] for p in parts])
    near = jnp.concatenate([near_1, swap(jnp.concatenate([own[half:], label], axis=0), 1, 0)], axis=0)
    diag = swap(own, 1, 2).reshape(-1, half, channels)
    other = swap(own, 0, 2).reshape(-1, half, channels)
    near, near_label = near[: own.shape[0]].reshape(-1, half, channels), near[own.shape[0] :]
    own = own.reshape(-1, half, channels)
    near, fwd, band, inverse = lax.optimization_barrier((near, fwd, band, inverse))
    first_sib = swap(jnp.concatenate([own, near], axis=0), 0, 1)

    zb = own.shape[0]

    def scratch(segments):
        kb = DEEP // (2 * segments)
        return [
            pltpu.VMEM((SEG // kb, 2, DEEP // 2, SRC), jnp.bfloat16),
        ], [
            pltpu.VMEM((segments // 2, 2, SEG, 2 * SRC), jnp.float32),
            pltpu.VMEM((segments // 2, SEG, 2 * SRC), jnp.bfloat16),
        ]

    partial = pltpu.VMEM((2 * RECV, SEG, SRC), jnp.float32)
    spectra, work = scratch(zb)
    before, perm, chosen = pl.pallas_call(
        window_kernel,
        out_shape=[
            partial,
            pltpu.VMEM((SRC, SRC), jnp.bfloat16),
            pltpu.VMEM((RECV * DEEP // (2 * zb), SRC), jnp.float32),
        ],
        in_specs=[vmem] * 6,
        out_specs=[vmem] * 3,
        scratch_shapes=[*spectra, *work],
        compiler_params=params,
    )(own, near, label, near_label, fwd, band)
    other, diag, chosen = lax.optimization_barrier((other, diag, chosen))
    second_sib = swap(jnp.concatenate([other, diag], axis=0), 0, 1)
    many_spectra, many_work = scratch(2 * zb)
    before = pl.pallas_call(
        middle_kernel,
        out_shape=partial,
        in_specs=[vmem] * 7,
        out_specs=vmem,
        scratch_shapes=[*many_spectra, *many_work],
        compiler_params=params,
    )(first_sib, other, diag, fwd, band, chosen, before)
    return pl.pallas_call(
        cross_kernel,
        out_shape=jax.ShapeDtypeStruct((RECV, MAXP, SRC, LAGS), jnp.bfloat16),
        in_specs=[vmem] * 8,
        out_specs=pl.BlockSpec(memory_space=pl.ANY),
        scratch_shapes=[
            *spectra,
            pltpu.VMEM((RECV, 2 * SEG, SRC), jnp.bfloat16),
            pltpu.VMEM((RECV, SRC, LAGS), jnp.bfloat16),
            pltpu.VMEM((MAXP - 1, SRC, LAGS), jnp.bfloat16),
            *work,
            pltpu.SemaphoreType.DMA((2 * RECV,)),
        ],
        compiler_params=params,
    )(keep, second_sib, before, fwd, perm, chosen, band, inverse)


def local(raw, order, pair_blocks):
    held = order.shape[1]
    gathered = (
        raw.shape[2] == SRC
        and lax.axis_size("ch") == 8
        and lax.axis_size("grp") == 4
        and raw.shape[0] == 1
        and 2 * raw.shape[1] == SEG
        and held == 4 * RECV
    )
    if gathered:
        return one_block(raw, order, pair_blocks)
    return many_blocks(raw, order, pair_blocks)


def solution(mesh):
    placed = (P("grp", "ch", None), P("ch", None), P("ch", None))
    return jax.shard_map(
        local,
        mesh=mesh,
        in_specs=placed,
        out_specs=P(("ch", "grp"), None, None, None),
        check_vma=False,
    )
```

```python
import functools
import math

import jax
import jax.numpy as jnp
import numpy as np
from jax import lax
from jax.experimental import pallas as pl
from jax.experimental.pallas import tpu as pltpu
from jax.sharding import PartitionSpec as P

SRC = 128
SEG = 256
LAGS = 256
SMOOTH = 8
MAXP = 3
REACH = 15


lag_scale = 1.0 / 16.0


def from_behind(value, axis, steps):
    count = lax.axis_size(axis)
    initial, last = (max(0, -steps), min(count, count - steps))
    return lax.ppermute(value, axis, [(source, source + steps) for source in range(initial, last)])


def transform_tables(half_len, lag_count, smooth_half):
    samples = np.arange(half_len)
    column = np.arange(2 * half_len)
    freq = column % half_len + 1
    angle_fwd = (samples[:, None] * freq[None, :] % (2 * half_len)) * (math.pi / half_len)
    forward = np.where(column[None, :] < half_len, np.cos(angle_fwd), -np.sin(angle_fwd))
    lag_steps = np.arange(lag_count) - lag_count // 2
    angle_inv = (freq[:, None] * lag_steps[None, :] % (2 * half_len)) * (math.pi / half_len)
    inverse = np.where(column[:, None] < half_len, np.cos(angle_inv), -np.sin(angle_inv)) * lag_scale
    bins = np.arange(half_len)
    band = np.abs(bins[:, None] - bins[None, :]) <= smooth_half
    return (forward.astype(np.float32), inverse.astype(np.float32), band.astype(np.float32))


def whiten(segments, forward, band):
    half_len = segments.shape[-1]
    flat_rows = segments.reshape(-1, half_len)
    spectrum = jnp.dot(flat_rows, forward, preferred_element_type=jnp.float32)
    real_part = spectrum[:, :half_len]
    imag_part = spectrum[:, half_len:]
    power_bins = real_part * real_part + imag_part * imag_part
    smoothed = jnp.dot(power_bins, band, precision=lax.Precision.HIGHEST) / (2 * SMOOTH + 1)
    water_level = jnp.mean(power_bins, axis=1, keepdims=True)
    divisor = jnp.sqrt(smoothed + 0.1 * water_level + 1e-06)
    whitened = spectrum / jnp.concatenate([divisor, divisor], axis=1)
    return whitened.astype(jnp.bfloat16).reshape(segments.shape[:-1] + (2 * half_len,))


def correlate(receivers, sources, inverse):
    half_len = receivers.shape[-1] // 2
    seg_count = receivers.shape[1]
    recv_re = receivers[..., :half_len]
    recv_im = receivers[..., half_len:]
    left_first = jnp.concatenate([recv_re, recv_im], axis=1)
    left_second = jnp.concatenate([recv_im, -recv_re], axis=1)
    right_both = jnp.concatenate([sources[..., :half_len], sources[..., half_len:]], axis=1)
    cross_re = jnp.einsum(
        "rnk,snk->rsk", left_first, right_both, preferred_element_type=jnp.float32
    )
    cross_im = jnp.einsum(
        "rnk,snk->rsk", left_second, right_both, preferred_element_type=jnp.float32
    )
    cross_spec = (jnp.concatenate([cross_re, cross_im], axis=2) * (1.0 / seg_count)).astype(
        jnp.bfloat16
    )
    recv_count = receivers.shape[0]
    src_count = sources.shape[0]
    lag_values = jnp.dot(
        cross_spec.reshape(-1, 2 * half_len), inverse, preferred_element_type=jnp.float32
    )
    return lag_values.reshape(recv_count, src_count, inverse.shape[1])


def many_blocks(raw, order, pair_blocks):
    recorded = lax.all_to_all(raw, "ch", split_axis=2, concat_axis=1, tiled=True)
    local_channels = recorded.shape[2]
    onehot = (order[0][:, None] == jnp.arange(local_channels, dtype=jnp.int32)[None, :]).astype(
        jnp.bfloat16
    )
    series = jnp.einsum(
        "ck,tc->kt", onehot, recorded[0], preferred_element_type=jnp.float32
    ).astype(jnp.bfloat16)
    segments = series.reshape(1, local_channels, -1, SEG)
    forward, inverse, band = transform_tables(SEG, LAGS, SMOOTH)
    forward = jnp.asarray(forward, jnp.bfloat16)
    inverse = jnp.asarray(inverse, jnp.bfloat16)
    own_white = whiten(segments, forward, band)
    before_list = []
    for distance in range(REACH, 0, -1):
        before_list.append(from_behind(own_white, "ch", distance))
    after_list = []
    for distance in range(1, REACH + 1):
        after_list.append(from_behind(own_white, "ch", -distance))
    window = jnp.concatenate(before_list + [own_white] + after_list, axis=1)
    window_base = (lax.axis_index("ch") - REACH) * local_channels
    groups = lax.axis_size("grp")
    receivers = own_white[0]
    slot_results = []
    for slot_index in range(MAXP):
        block_id = pair_blocks[0, slot_index]
        source_start = jnp.maximum(block_id, 0) * SRC - window_base
        sources = lax.dynamic_slice_in_dim(window[0], source_start, SRC, 0)
        is_live = (block_id >= 0).astype(jnp.float32)
        lag_values = correlate(receivers, sources, inverse) * is_live
        slot_results.append(lag_values)
    stacked = lax.psum_scatter(
        jnp.stack(slot_results, axis=1).astype(jnp.bfloat16), "grp", scatter_dimension=0, tiled=True
    ).astype(jnp.float32)
    return (stacked / groups).astype(jnp.bfloat16)


RECV = 4
WIDTH = 2 * SMOOTH + 1
DEEP = 256
LABEL = 16


def label_kernel(order, pairs, raw, out, keep):
    held = order.shape[1]
    half, channels = raw.shape[1:]
    me = lax.axis_index("ch")
    lanes = lax.broadcasted_iota(jnp.int32, (LABEL, channels), 1)
    row = jnp.zeros((LABEL, channels), jnp.int32)
    for c in range(held):
        row = jnp.where(lanes % held == c, order[0, c], row)
    row = jnp.where(lanes // held == me, row + held * me, 0)
    keep[...] = jnp.broadcast_to(jnp.where(pairs[0, 0] >= 0, 1.0, 0.0), keep.shape)
    out[0, 0:half, :] = raw[0]
    out[0, half : half + LABEL, :] = row.astype(jnp.float32).astype(out.dtype)


def tables_kernel(forward, band_from, inverse_from, fwd, band, inverse, sems):
    half = forward.shape[1] // 2
    mine = lax.axis_index("ch") % 2
    near = forward.at[:, pl.ds(pl.multiple_of(mine * half, half), half)]
    far = forward.at[:, pl.ds(pl.multiple_of((1 - mine) * half, half), half)]
    copies = [
        pltpu.make_async_copy(near, fwd.at[:, 0:half], sems.at[0]),
        pltpu.make_async_copy(far, fwd.at[:, half : 2 * half], sems.at[1]),
        pltpu.make_async_copy(band_from, band, sems.at[2]),
        pltpu.make_async_copy(inverse_from, inverse, sems.at[3]),
    ]
    for copy in copies:
        copy.start()
    for copy in copies:
        copy.wait()


def whiten_group(items, fwd, band, spec, pows, white):
    bins = band.shape[0]
    levels = []
    for i, (first, second, first_next, second_next) in enumerate(items):
        samples = jnp.concatenate(
            [
                jnp.concatenate([first, first_next], axis=1),
                jnp.concatenate([second, second_next], axis=1),
            ],
            axis=0,
        )
        re = jnp.dot(fwd[0:bins, :], samples, preferred_element_type=jnp.float32)
        im = jnp.dot(fwd[bins:, :], samples, preferred_element_type=jnp.float32)
        power = re * re + im * im
        spec[i, 0] = re
        spec[i, 1] = im
        pows[i] = power.astype(jnp.bfloat16)
        levels.append(jnp.sum(power.reshape(bins // 8, 8, 2 * SRC), axis=0))
    blocks, _, rows, _ = white.shape
    kb = bins // blocks
    for i in range(len(items)):
        level = jnp.sum(levels[i], axis=0, keepdims=True) * (0.1 * WIDTH / bins) + 1e-6 * WIDTH
        smoothed = jnp.dot(band[...], pows[i], preferred_element_type=jnp.float32)
        scale = lax.rsqrt(smoothed + level)
        for part in range(2):
            value = spec[i, part] * scale
            left = value[:, 0:SRC].reshape(blocks, kb, SRC)
            right = value[:, SRC:].reshape(blocks, kb, SRC)
            both = jnp.concatenate([left, right], axis=1).astype(jnp.bfloat16)
            white[:, part, 2 * kb * i : 2 * kb * (i + 1), :] = both


def receiver_products(white, select):
    blocks, parts, rows, _ = white.shape
    kb = SEG // blocks
    deep = parts * rows
    lane = lax.broadcasted_iota(jnp.int32, (kb * RECV, deep), 1)
    sub = lax.broadcasted_iota(jnp.int32, (kb * RECV, deep), 0)
    same = (lane % kb == sub % kb).astype(jnp.float32)
    sign = jnp.where(lane < rows, 1.0, -1.0)
    picks = []
    for g in range(0, blocks, 2):
        sources = white[g : g + 2].reshape(2 * deep, SRC)
        both = lax.dot_general(
            select, sources, (((1,), (1,)), ((), ())), preferred_element_type=jnp.float32
        )
        for u in range(2):
            v = both[:, u * deep : (u + 1) * deep] * same
            turned = pltpu.roll(v, rows, 1) * sign
            picks.append(
                jnp.concatenate([v.astype(jnp.bfloat16), turned.astype(jnp.bfloat16)], axis=0)
            )
    sums = [
        jnp.dot(picks[g], white[g].reshape(deep, SRC), preferred_element_type=jnp.float32)
        for g in range(blocks)
    ]
    return [
        jnp.concatenate([s[at * kb : (at + 1) * kb] for s in sums], axis=0)
        for at in range(2 * RECV)
    ]


def pair_items(first, second, half):
    return [
        (first[z, 0:half], second[z, 0:half], first[z + 1, 0:half], second[z + 1, 0:half])
        for z in range(0, first.shape[0], 2)
    ]


def window_kernel(
    own, near, label, near_label, fwd, band, partial, perm, chosen, white, spec, pows
):
    half = fwd.shape[1] // 2
    zb = own.shape[0]
    ch = lax.axis_index("ch")
    base = (ch * lax.axis_size("grp") + lax.axis_index("grp")) * RECV

    dest = jnp.maximum(label[...], near_label[...])
    dest = dest.astype(jnp.float32)[0:1, :]
    rows = lax.broadcasted_iota(jnp.int32, (SRC, SRC), 0)
    perm[...] = (rows.astype(jnp.float32) == dest).astype(jnp.bfloat16)
    wanted = lax.broadcasted_iota(jnp.int32, chosen.shape, 0) * RECV // chosen.shape[0] + base
    chosen[...] = (wanted.astype(jnp.float32) == dest).astype(jnp.float32)

    whiten_group(pair_items(own, near, half), fwd, band, spec, pows, white)
    for at, value in enumerate(receiver_products(white, chosen[...].astype(jnp.bfloat16))):
        partial[at] = value


def middle_kernel(sib, other, diag, fwd, band, chosen, before, partial, white, spec, pows):
    zb, half = other.shape[0:2]
    items = pair_items(sib.at[0:zb], sib.at[zb : 2 * zb], half) + pair_items(other, diag, half)
    whiten_group(items, fwd, band, spec, pows, white)
    each = RECV * SEG // white.shape[0]
    step = chosen.shape[0] // RECV
    select = jnp.concatenate(
        [chosen[q * step : q * step + each // RECV, :] for q in range(RECV)], axis=0
    )
    for at, value in enumerate(receiver_products(white, select.astype(jnp.bfloat16))):
        partial[at] = before[at] + value


def cross_kernel(
    keep, sib, before, fwd, perm, chosen, band, inverse, out,
    white, lags, blank, spec, pows, sems,
):
    bins = band.shape[0]
    zb, half = sib.shape[0] // 2, sib.shape[1]

    blank[...] = jnp.zeros(blank.shape, blank.dtype)
    copies = [
        pltpu.make_async_copy(blank, out.at[q, pl.ds(1, MAXP - 1)], sems.at[q]) for q in range(RECV)
    ]
    for copy in copies:
        copy.start()

    whiten_group(
        pair_items(sib.at[0:zb], sib.at[zb : 2 * zb], half), fwd, band, spec, pows, white
    )
    pieces = []
    for at, value in enumerate(receiver_products(white, chosen[...].astype(jnp.bfloat16))):
        total = (before[at] + value) * (WIDTH / (4 * zb))
        pieces.append(total.astype(jnp.bfloat16))
    ordered = [pieces[part * RECV + q] for q in range(RECV) for part in range(2)]

    turned = lax.dot_general(
        perm[...],
        jnp.concatenate(ordered, axis=0),
        (((1,), (1,)), ((), ())),
        preferred_element_type=jnp.float32,
    ).astype(jnp.bfloat16)
    for q in range(RECV):
        held = turned[:, q * 2 * bins : (q + 1) * 2 * bins]
        lag_values = jnp.dot(held, inverse[...], preferred_element_type=jnp.float32)
        lags[q] = (lag_values * keep[0:1, :]).astype(jnp.bfloat16)
        copy = pltpu.make_async_copy(lags.at[q], out.at[q, 0], sems.at[RECV + q])
        copy.start()
        copies.append(copy)
    for copy in copies:
        copy.wait()


def one_block(raw, order, pair_blocks):
    groups = lax.axis_size("grp")
    total = lax.axis_size("ch") * groups
    half, channels = raw.shape[1:]
    vmem = pl.BlockSpec(memory_space=pltpu.VMEM)
    smem = pl.BlockSpec(memory_space=pltpu.SMEM)
    params = pltpu.CompilerParams(vmem_limit_bytes=24 * 1024 * 1024)
    dtype = raw.dtype

    block, keep = pl.pallas_call(
        label_kernel,
        out_shape=[pltpu.VMEM((1, half + LABEL, channels), dtype), pltpu.VMEM((8, 2 * SRC), jnp.float32)],
        in_specs=[smem, smem, vmem],
        out_specs=[vmem, vmem],
    )(order, pair_blocks, raw)

    def swap(value, ch_bits, grp_bits):
        flip = ch_bits * groups + grp_bits
        return lax.ppermute(value, ("ch", "grp"), [(d, d ^ flip) for d in range(total)])

    parts = [block, swap(block, 2, 0), swap(block, 6, 0), swap(block, 4, 0)]

    forward, inverse, band = transform_tables(SEG, LAGS, SMOOTH)
    forward, band, inverse = [
        jnp.asarray(np.ascontiguousarray(t), jnp.bfloat16) for t in (forward.T, band, inverse)
    ]
    anywhere = pl.BlockSpec(memory_space=pl.ANY)
    fwd, band, inverse = pl.pallas_call(
        tables_kernel,
        out_shape=[pltpu.VMEM(t.shape, t.dtype) for t in (forward, band, inverse)],
        in_specs=[anywhere] * 3,
        out_specs=[vmem] * 3,
        scratch_shapes=[pltpu.SemaphoreType.DMA((4,))],
    )(forward, band, inverse)
    near_1 = swap(block[0, 0:half], 1, 0)
    own = jnp.concatenate([p[0, 0:half] for p in parts], axis=0)
    label = functools.reduce(jnp.maximum, [p[0, half:] for p in parts])
    near = jnp.concatenate([near_1, swap(jnp.concatenate([own[half:], label], axis=0), 1, 0)], axis=0)
    diag = swap(own, 1, 2).reshape(-1, half, channels)
    other = swap(own, 0, 2).reshape(-1, half, channels)
    near, near_label = near[: own.shape[0]].reshape(-1, half, channels), near[own.shape[0] :]
    own = own.reshape(-1, half, channels)
    near, fwd, band, inverse = lax.optimization_barrier((near, fwd, band, inverse))
    first_sib = swap(jnp.concatenate([own, near], axis=0), 0, 1)

    zb = own.shape[0]

    def scratch(segments):
        kb = DEEP // (2 * segments)
        return [
            pltpu.VMEM((SEG // kb, 2, DEEP // 2, SRC), jnp.bfloat16),
        ], [
            pltpu.VMEM((segments // 2, 2, SEG, 2 * SRC), jnp.float32),
            pltpu.VMEM((segments // 2, SEG, 2 * SRC), jnp.bfloat16),
        ]

    partial = pltpu.VMEM((2 * RECV, SEG, SRC), jnp.float32)
    spectra, work = scratch(zb)
    before, perm, chosen = pl.pallas_call(
        window_kernel,
        out_shape=[
            partial,
            pltpu.VMEM((SRC, SRC), jnp.bfloat16),
            pltpu.VMEM((RECV * DEEP // (2 * zb), SRC), jnp.float32),
        ],
        in_specs=[vmem] * 6,
        out_specs=[vmem] * 3,
        scratch_shapes=[*spectra, *work],
        compiler_params=params,
    )(own, near, label, near_label, fwd, band)
    other, diag, chosen = lax.optimization_barrier((other, diag, chosen))
    second_sib = swap(jnp.concatenate([other, diag], axis=0), 0, 1)
    many_spectra, many_work = scratch(2 * zb)
    before = pl.pallas_call(
        middle_kernel,
        out_shape=partial,
        in_specs=[vmem] * 7,
        out_specs=vmem,
        scratch_shapes=[*many_spectra, *many_work],
        compiler_params=params,
    )(first_sib, other, diag, fwd, band, chosen, before)
    return pl.pallas_call(
        cross_kernel,
        out_shape=jax.ShapeDtypeStruct((RECV, MAXP, SRC, LAGS), jnp.bfloat16),
        in_specs=[vmem] * 8,
        out_specs=pl.BlockSpec(memory_space=pl.ANY),
        scratch_shapes=[
            *spectra,
            pltpu.VMEM((RECV, SRC, LAGS), jnp.bfloat16),
            pltpu.VMEM((MAXP - 1, SRC, LAGS), jnp.bfloat16),
            *work,
            pltpu.SemaphoreType.DMA((2 * RECV,)),
        ],
        compiler_params=params,
    )(keep, second_sib, before, fwd, perm, chosen, band, inverse)


def local(raw, order, pair_blocks):
    held = order.shape[1]
    gathered = (
        raw.shape[2] == SRC
        and lax.axis_size("ch") == 8
        and lax.axis_size("grp") == 4
        and raw.shape[0] == 1
        and 2 * raw.shape[1] == SEG
        and held == 4 * RECV
    )
    if gathered:
        return one_block(raw, order, pair_blocks)
    return many_blocks(raw, order, pair_blocks)


def solution(mesh):
    placed = (P("grp", "ch", None), P("ch", None), P("ch", None))
    return jax.shard_map(
        local,
        mesh=mesh,
        in_specs=placed,
        out_specs=P(("ch", "grp"), None, None, None),
        check_vma=False,
    )
```

```python
import functools
import math

import jax
import jax.numpy as jnp
import numpy as np
from jax import lax
from jax.experimental import pallas as pl
from jax.experimental.pallas import tpu as pltpu
from jax.sharding import PartitionSpec as P

SRC = 128
SEG = 256
LAGS = 256
SMOOTH = 8
MAXP = 3
REACH = 15


lag_scale = 1.0 / 16.0


def from_behind(value, axis, steps):
    count = lax.axis_size(axis)
    initial, last = (max(0, -steps), min(count, count - steps))
    return lax.ppermute(value, axis, [(source, source + steps) for source in range(initial, last)])


def transform_tables(half_len, lag_count, smooth_half):
    samples = np.arange(half_len)
    column = np.arange(2 * half_len)
    freq = column % half_len + 1
    angle_fwd = (samples[:, None] * freq[None, :] % (2 * half_len)) * (math.pi / half_len)
    forward = np.where(column[None, :] < half_len, np.cos(angle_fwd), -np.sin(angle_fwd))
    lag_steps = np.arange(lag_count) - lag_count // 2
    angle_inv = (freq[:, None] * lag_steps[None, :] % (2 * half_len)) * (math.pi / half_len)
    inverse = np.where(column[:, None] < half_len, np.cos(angle_inv), -np.sin(angle_inv)) * lag_scale
    bins = np.arange(half_len)
    band = np.abs(bins[:, None] - bins[None, :]) <= smooth_half
    return (forward.astype(np.float32), inverse.astype(np.float32), band.astype(np.float32))


def whiten(segments, forward, band):
    half_len = segments.shape[-1]
    flat_rows = segments.reshape(-1, half_len)
    spectrum = jnp.dot(flat_rows, forward, preferred_element_type=jnp.float32)
    real_part = spectrum[:, :half_len]
    imag_part = spectrum[:, half_len:]
    power_bins = real_part * real_part + imag_part * imag_part
    smoothed = jnp.dot(power_bins, band, precision=lax.Precision.HIGHEST) / (2 * SMOOTH + 1)
    water_level = jnp.mean(power_bins, axis=1, keepdims=True)
    divisor = jnp.sqrt(smoothed + 0.1 * water_level + 1e-06)
    whitened = spectrum / jnp.concatenate([divisor, divisor], axis=1)
    return whitened.astype(jnp.bfloat16).reshape(segments.shape[:-1] + (2 * half_len,))


def correlate(receivers, sources, inverse):
    half_len = receivers.shape[-1] // 2
    seg_count = receivers.shape[1]
    recv_re = receivers[..., :half_len]
    recv_im = receivers[..., half_len:]
    left_first = jnp.concatenate([recv_re, recv_im], axis=1)
    left_second = jnp.concatenate([recv_im, -recv_re], axis=1)
    right_both = jnp.concatenate([sources[..., :half_len], sources[..., half_len:]], axis=1)
    cross_re = jnp.einsum(
        "rnk,snk->rsk", left_first, right_both, preferred_element_type=jnp.float32
    )
    cross_im = jnp.einsum(
        "rnk,snk->rsk", left_second, right_both, preferred_element_type=jnp.float32
    )
    cross_spec = (jnp.concatenate([cross_re, cross_im], axis=2) * (1.0 / seg_count)).astype(
        jnp.bfloat16
    )
    recv_count = receivers.shape[0]
    src_count = sources.shape[0]
    lag_values = jnp.dot(
        cross_spec.reshape(-1, 2 * half_len), inverse, preferred_element_type=jnp.float32
    )
    return lag_values.reshape(recv_count, src_count, inverse.shape[1])


def many_blocks(raw, order, pair_blocks):
    recorded = lax.all_to_all(raw, "ch", split_axis=2, concat_axis=1, tiled=True)
    local_channels = recorded.shape[2]
    onehot = (order[0][:, None] == jnp.arange(local_channels, dtype=jnp.int32)[None, :]).astype(
        jnp.bfloat16
    )
    series = jnp.einsum(
        "ck,tc->kt", onehot, recorded[0], preferred_element_type=jnp.float32
    ).astype(jnp.bfloat16)
    segments = series.reshape(1, local_channels, -1, SEG)
    forward, inverse, band = transform_tables(SEG, LAGS, SMOOTH)
    forward = jnp.asarray(forward, jnp.bfloat16)
    inverse = jnp.asarray(inverse, jnp.bfloat16)
    own_white = whiten(segments, forward, band)
    before_list = []
    for distance in range(REACH, 0, -1):
        before_list.append(from_behind(own_white, "ch", distance))
    after_list = []
    for distance in range(1, REACH + 1):
        after_list.append(from_behind(own_white, "ch", -distance))
    window = jnp.concatenate(before_list + [own_white] + after_list, axis=1)
    window_base = (lax.axis_index("ch") - REACH) * local_channels
    groups = lax.axis_size("grp")
    receivers = own_white[0]
    slot_results = []
    for slot_index in range(MAXP):
        block_id = pair_blocks[0, slot_index]
        source_start = jnp.maximum(block_id, 0) * SRC - window_base
        sources = lax.dynamic_slice_in_dim(window[0], source_start, SRC, 0)
        is_live = (block_id >= 0).astype(jnp.float32)
        lag_values = correlate(receivers, sources, inverse) * is_live
        slot_results.append(lag_values)
    stacked = lax.psum_scatter(
        jnp.stack(slot_results, axis=1).astype(jnp.bfloat16), "grp", scatter_dimension=0, tiled=True
    ).astype(jnp.float32)
    return (stacked / groups).astype(jnp.bfloat16)


RECV = 4
WIDTH = 2 * SMOOTH + 1
DEEP = 256
LABEL = 16


def label_kernel(order, pairs, raw, out, keep):
    held = order.shape[1]
    half, channels = raw.shape[1:]
    me = lax.axis_index("ch")
    lanes = lax.broadcasted_iota(jnp.int32, (LABEL, channels), 1)
    row = jnp.zeros((LABEL, channels), jnp.int32)
    for c in range(held):
        row = jnp.where(lanes % held == c, order[0, c], row)
    row = jnp.where(lanes // held == me, row + held * me, 0)
    keep[...] = jnp.broadcast_to(jnp.where(pairs[0, 0] >= 0, 1.0, 0.0), keep.shape)
    out[0, 0:half, :] = raw[0]
    out[0, half : half + LABEL, :] = row.astype(jnp.float32).astype(out.dtype)


def tables_kernel(forward, band_from, inverse_from, fwd, band, inverse, sems):
    half = forward.shape[1] // 2
    mine = lax.axis_index("ch") % 2
    near = forward.at[:, pl.ds(pl.multiple_of(mine * half, half), half)]
    far = forward.at[:, pl.ds(pl.multiple_of((1 - mine) * half, half), half)]
    copies = [
        pltpu.make_async_copy(near, fwd.at[:, 0:half], sems.at[0]),
        pltpu.make_async_copy(far, fwd.at[:, half : 2 * half], sems.at[1]),
        pltpu.make_async_copy(band_from, band, sems.at[2]),
        pltpu.make_async_copy(inverse_from, inverse, sems.at[3]),
    ]
    for copy in copies:
        copy.start()
    for copy in copies:
        copy.wait()


def whiten_group(items, fwd, band, spec, pows, white):
    bins = band.shape[0]
    levels = []
    for i, (first, second, first_next, second_next) in enumerate(items):
        samples = jnp.concatenate(
            [
                jnp.concatenate([first, first_next], axis=1),
                jnp.concatenate([second, second_next], axis=1),
            ],
            axis=0,
        )
        level = jnp.zeros((8, 2 * SRC), jnp.float32)
        step = bins // 2
        for c in range(0, bins, step):
            re = jnp.dot(fwd[c : c + step, :], samples, preferred_element_type=jnp.float32)
            im = jnp.dot(
                fwd[bins + c : bins + c + step, :], samples, preferred_element_type=jnp.float32
            )
            power = re * re + im * im
            spec[i, 0, c : c + step, :] = re
            spec[i, 1, c : c + step, :] = im
            pows[i, c : c + step, :] = power.astype(jnp.bfloat16)
            level += jnp.sum(power.reshape(step // 8, 8, 2 * SRC), axis=0)
        levels.append(level)
    blocks, _, rows, _ = white.shape
    kb = bins // blocks
    for i in range(len(items)):
        level = jnp.sum(levels[i], axis=0, keepdims=True) * (0.1 * WIDTH / bins) + 1e-6 * WIDTH
        smoothed = jnp.dot(band[...], pows[i], preferred_element_type=jnp.float32)
        scale = lax.rsqrt(smoothed + level)
        for part in range(2):
            value = spec[i, part] * scale
            left = value[:, 0:SRC].reshape(blocks, kb, SRC)
            right = value[:, SRC:].reshape(blocks, kb, SRC)
            both = jnp.concatenate([left, right], axis=1).astype(jnp.bfloat16)
            white[:, part, 2 * kb * i : 2 * kb * (i + 1), :] = both


def receiver_products(white, select):
    blocks, parts, rows, _ = white.shape
    kb = SEG // blocks
    deep = parts * rows
    lane = lax.broadcasted_iota(jnp.int32, (kb * RECV, deep), 1)
    sub = lax.broadcasted_iota(jnp.int32, (kb * RECV, deep), 0)
    same = (lane % kb == sub % kb).astype(jnp.float32)
    sign = jnp.where(lane < rows, 1.0, -1.0)
    picks = []
    for g in range(0, blocks, 2):
        sources = white[g : g + 2].reshape(2 * deep, SRC)
        both = lax.dot_general(
            select, sources, (((1,), (1,)), ((), ())), preferred_element_type=jnp.float32
        )
        for u in range(2):
            v = both[:, u * deep : (u + 1) * deep] * same
            turned = pltpu.roll(v, rows, 1) * sign
            picks.append(
                jnp.concatenate([v.astype(jnp.bfloat16), turned.astype(jnp.bfloat16)], axis=0)
            )
    sums = [
        jnp.dot(picks[g], white[g].reshape(deep, SRC), preferred_element_type=jnp.float32)
        for g in range(blocks)
    ]
    return [
        jnp.concatenate([s[at * kb : (at + 1) * kb] for s in sums], axis=0)
        for at in range(2 * RECV)
    ]


def pair_items(first, second, half):
    return [
        (first[z, 0:half], second[z, 0:half], first[z + 1, 0:half], second[z + 1, 0:half])
        for z in range(0, first.shape[0], 2)
    ]


def window_kernel(
    own, near, label, near_label, fwd, band, partial, perm, chosen, white, spec, pows
):
    half = fwd.shape[1] // 2
    zb = own.shape[0]
    ch = lax.axis_index("ch")
    base = (ch * lax.axis_size("grp") + lax.axis_index("grp")) * RECV

    dest = jnp.maximum(label[...], near_label[...])
    dest = dest.astype(jnp.float32)[0:1, :]
    rows = lax.broadcasted_iota(jnp.int32, (SRC, SRC), 0)
    perm[...] = (rows.astype(jnp.float32) == dest).astype(jnp.bfloat16)
    wanted = lax.broadcasted_iota(jnp.int32, chosen.shape, 0) * RECV // chosen.shape[0] + base
    chosen[...] = (wanted.astype(jnp.float32) == dest).astype(jnp.float32)

    whiten_group(pair_items(own, near, half), fwd, band, spec, pows, white)
    for at, value in enumerate(receiver_products(white, chosen[...].astype(jnp.bfloat16))):
        partial[at] = value


def middle_kernel(sib, other, diag, fwd, band, chosen, before, partial, white, spec, pows):
    zb, half = other.shape[0:2]
    items = pair_items(sib.at[0:zb], sib.at[zb : 2 * zb], half) + pair_items(other, diag, half)
    whiten_group(items, fwd, band, spec, pows, white)
    each = RECV * SEG // white.shape[0]
    step = chosen.shape[0] // RECV
    select = jnp.concatenate(
        [chosen[q * step : q * step + each // RECV, :] for q in range(RECV)], axis=0
    )
    for at, value in enumerate(receiver_products(white, select.astype(jnp.bfloat16))):
        partial[at] = before[at] + value


def cross_kernel(
    keep, sib, before, fwd, perm, chosen, band, inverse, out,
    white, lags, blank, spec, pows, sems,
):
    bins = band.shape[0]
    zb, half = sib.shape[0] // 2, sib.shape[1]

    blank[...] = jnp.zeros(blank.shape, blank.dtype)
    copies = [
        pltpu.make_async_copy(blank, out.at[q, pl.ds(1, MAXP - 1)], sems.at[q]) for q in range(RECV)
    ]
    for copy in copies:
        copy.start()

    whiten_group(
        pair_items(sib.at[0:zb], sib.at[zb : 2 * zb], half), fwd, band, spec, pows, white
    )
    pieces = []
    for at, value in enumerate(receiver_products(white, chosen[...].astype(jnp.bfloat16))):
        total = (before[at] + value) * (WIDTH / (4 * zb))
        pieces.append(total.astype(jnp.bfloat16))
    ordered = [pieces[part * RECV + q] for q in range(RECV) for part in range(2)]

    turned = lax.dot_general(
        perm[...],
        jnp.concatenate(ordered, axis=0),
        (((1,), (1,)), ((), ())),
        preferred_element_type=jnp.float32,
    ).astype(jnp.bfloat16)
    for q in range(RECV):
        held = turned[:, q * 2 * bins : (q + 1) * 2 * bins]
        lag_values = jnp.dot(held, inverse[...], preferred_element_type=jnp.float32)
        lags[q] = (lag_values * keep[0:1, :]).astype(jnp.bfloat16)
        copy = pltpu.make_async_copy(lags.at[q], out.at[q, 0], sems.at[RECV + q])
        copy.start()
        copies.append(copy)
    for copy in copies:
        copy.wait()


def one_block(raw, order, pair_blocks):
    groups = lax.axis_size("grp")
    total = lax.axis_size("ch") * groups
    half, channels = raw.shape[1:]
    vmem = pl.BlockSpec(memory_space=pltpu.VMEM)
    smem = pl.BlockSpec(memory_space=pltpu.SMEM)
    params = pltpu.CompilerParams(vmem_limit_bytes=24 * 1024 * 1024)
    dtype = raw.dtype

    block, keep = pl.pallas_call(
        label_kernel,
        out_shape=[pltpu.VMEM((1, half + LABEL, channels), dtype), pltpu.VMEM((8, 2 * SRC), jnp.float32)],
        in_specs=[smem, smem, vmem],
        out_specs=[vmem, vmem],
    )(order, pair_blocks, raw)

    def swap(value, ch_bits, grp_bits):
        flip = ch_bits * groups + grp_bits
        return lax.ppermute(value, ("ch", "grp"), [(d, d ^ flip) for d in range(total)])

    parts = [block, swap(block, 2, 0), swap(block, 6, 0), swap(block, 4, 0)]

    forward, inverse, band = transform_tables(SEG, LAGS, SMOOTH)
    forward, band, inverse = [
        jnp.asarray(np.ascontiguousarray(t), jnp.bfloat16) for t in (forward.T, band, inverse)
    ]
    anywhere = pl.BlockSpec(memory_space=pl.ANY)
    fwd, band, inverse = pl.pallas_call(
        tables_kernel,
        out_shape=[pltpu.VMEM(t.shape, t.dtype) for t in (forward, band, inverse)],
        in_specs=[anywhere] * 3,
        out_specs=[vmem] * 3,
        scratch_shapes=[pltpu.SemaphoreType.DMA((4,))],
    )(forward, band, inverse)
    near_1 = swap(block[0, 0:half], 1, 0)
    own = jnp.concatenate([p[0, 0:half] for p in parts], axis=0)
    label = functools.reduce(jnp.maximum, [p[0, half:] for p in parts])
    near = jnp.concatenate([near_1, swap(jnp.concatenate([own[half:], label], axis=0), 1, 0)], axis=0)
    diag = swap(own, 1, 2).reshape(-1, half, channels)
    other = swap(own, 0, 2).reshape(-1, half, channels)
    near, near_label = near[: own.shape[0]].reshape(-1, half, channels), near[own.shape[0] :]
    own = own.reshape(-1, half, channels)
    near, fwd, band, inverse = lax.optimization_barrier((near, fwd, band, inverse))
    first_sib = swap(jnp.concatenate([own, near], axis=0), 0, 1)

    zb = own.shape[0]

    def scratch(segments):
        kb = DEEP // (2 * segments)
        return [
            pltpu.VMEM((SEG // kb, 2, DEEP // 2, SRC), jnp.bfloat16),
        ], [
            pltpu.VMEM((segments // 2, 2, SEG, 2 * SRC), jnp.float32),
            pltpu.VMEM((segments // 2, SEG, 2 * SRC), jnp.bfloat16),
        ]

    partial = pltpu.VMEM((2 * RECV, SEG, SRC), jnp.float32)
    spectra, work = scratch(zb)
    before, perm, chosen = pl.pallas_call(
        window_kernel,
        out_shape=[
            partial,
            pltpu.VMEM((SRC, SRC), jnp.bfloat16),
            pltpu.VMEM((RECV * DEEP // (2 * zb), SRC), jnp.float32),
        ],
        in_specs=[vmem] * 6,
        out_specs=[vmem] * 3,
        scratch_shapes=[*spectra, *work],
        compiler_params=params,
    )(own, near, label, near_label, fwd, band)
    other, diag, chosen = lax.optimization_barrier((other, diag, chosen))
    second_sib = swap(jnp.concatenate([other, diag], axis=0), 0, 1)
    many_spectra, many_work = scratch(2 * zb)
    before = pl.pallas_call(
        middle_kernel,
        out_shape=partial,
        in_specs=[vmem] * 7,
        out_specs=vmem,
        scratch_shapes=[*many_spectra, *many_work],
        compiler_params=params,
    )(first_sib, other, diag, fwd, band, chosen, before)
    return pl.pallas_call(
        cross_kernel,
        out_shape=jax.ShapeDtypeStruct((RECV, MAXP, SRC, LAGS), jnp.bfloat16),
        in_specs=[vmem] * 8,
        out_specs=pl.BlockSpec(memory_space=pl.ANY),
        scratch_shapes=[
            *spectra,
            pltpu.VMEM((RECV, SRC, LAGS), jnp.bfloat16),
            pltpu.VMEM((MAXP - 1, SRC, LAGS), jnp.bfloat16),
            *work,
            pltpu.SemaphoreType.DMA((2 * RECV,)),
        ],
        compiler_params=params,
    )(keep, second_sib, before, fwd, perm, chosen, band, inverse)


def local(raw, order, pair_blocks):
    held = order.shape[1]
    gathered = (
        raw.shape[2] == SRC
        and lax.axis_size("ch") == 8
        and lax.axis_size("grp") == 4
        and raw.shape[0] == 1
        and 2 * raw.shape[1] == SEG
        and held == 4 * RECV
    )
    if gathered:
        return one_block(raw, order, pair_blocks)
    return many_blocks(raw, order, pair_blocks)


def solution(mesh):
    placed = (P("grp", "ch", None), P("ch", None), P("ch", None))
    return jax.shard_map(
        local,
        mesh=mesh,
        in_specs=placed,
        out_specs=P(("ch", "grp"), None, None, None),
        check_vma=False,
    )
```
